32 devices in a mesh: row: 4 (over z), col: 8 (over y, x, core).
Axes of the slice: x: 2, y: 2, z: 4, core: 2. Of those that a mesh axis runs over, the one named last changes fastest.
Arguments:
- block: float32 [2048, 1024], P('row', 'col'), may hold values from -6 to 6
- panels: float32 [2, 2048, 256], P(None, 'row', 'col'), may hold values from -0.125 to 0.125
- pivots: int32 [2, 256], replicated, may hold values from 0 to 2047, as said below
Outputs:
- updated: float32 [2048, 1024], P('row', 'col')
The draws below stay inside these ranges and needn't reach their ends.
Inputs may be any that keep to these rules, and one draw needn't show every extreme that they name: `pivots`: entry j of list k is either k*256+j itself or a global row at or beyond (k+1)*256; within one list the entries beyond are all different; entry 0 of list 0 is 0 and entry 255 of list 0 is 2047.
All inputs are finite; a program needn't handle non-finite values.
Results may differ from the reference program's by a relative error of at most 0.0001.
Values sent between devices are 32-bit elements; how exact they have to be, the bound alone decides.
A program may use at most 64 MiB of HBM per device.

```python
import jax
import jax.numpy as jnp
from jax import lax

PW = 256
ROWS = 2048
COLS = 1024


def draw_pivots(key, part):
    lists = []
    for panel in range(2):
        offset = panel * PW
        own = offset + jnp.arange(PW, dtype=jnp.int32)
        span = ROWS - 1 - (offset + PW)
        chosen = jax.random.permutation(jax.random.fold_in(key, 31 + panel), span)[:PW].astype(jnp.int32) + offset + PW
        keep = jax.random.randint(jax.random.fold_in(key, 57 + panel), (PW,), 0, 4) == 0
        entry = jnp.where(keep, own, chosen)
        if panel == 0:
            entry = entry.at[0].set(0).at[PW - 1].set(ROWS - 1)
        lists.append(entry.astype(jnp.int32))
    return jnp.stack(lists).astype(jnp.int32)


def shard_levels(own_key, dims, shards, smallest, largest):
    gain = 1.0
    for position, blocks in shards:
        steps = jax.random.uniform(jax.random.fold_in(jax.random.fold_in(own_key, 6), position), (blocks,), jnp.float32, smallest / len(shards), largest / len(shards))
        gain = gain * jnp.repeat(jnp.exp(steps), dims[position] // blocks).reshape((-1,) + (1,) * (len(dims) - 1 - position))
    return gain


def gaussian(stream_key, extent, spread, bound, cuts=(), held_as=jnp.bfloat16):
    array = spread * jax.random.normal(stream_key, extent, jnp.float32)
    if cuts:
        array = array * shard_levels(stream_key, extent, cuts, -0.22, 0.18)
    return jnp.clip(array, -bound, bound).astype(held_as)


def setup_inputs(seed: int = 0) -> dict:
    seeds = jax.random.split(jax.random.key(seed), 4)
    block = gaussian(seeds[0], (ROWS, COLS), 1.0, 6.0, ((0, 4), (1, 8)), jnp.float32)
    panels = gaussian(seeds[1], (2, ROWS, PW), (8 * PW) ** -0.5, 0.125, ((1, 4), (2, 8)), jnp.float32)
    pivots = draw_pivots(jax.random.fold_in(seeds[3], 71), 0)
    return dict(block=block, panels=panels, pivots=pivots)


def swap_order(piv_row, offset, count):

    def step(j, perm):
        first = offset + j
        second = piv_row[j]
        value_a = perm[first]
        value_b = perm[second]
        return perm.at[first].set(value_b).at[second].set(value_a)
    return lax.fori_loop(0, piv_row.shape[0], step, jnp.arange(count, dtype=jnp.int32))

def reference(block, panels, pivots):
    work = block
    for panel in range(2):
        offset = panel * PW
        perm = swap_order(pivots[panel], offset, ROWS)
        work = work[perm]
        lower = panels[panel]
        diag = jnp.tril(lower[offset:offset + PW], -1) + jnp.eye(PW, dtype=jnp.float32)
        upper = lax.linalg.triangular_solve(diag, work[offset:offset + PW], left_side=True, lower=True, unit_diagonal=True)
        below = work[offset + PW:] - jnp.dot(lower[offset + PW:].astype(jnp.float32), upper.astype(jnp.float32), precision=lax.Precision.HIGHEST, preferred_element_type=jnp.float32)
        work = jnp.concatenate([work[:offset], upper, below], 0)
    return work
```

```python
import functools

import jax
import jax.numpy as jnp
from jax import lax
from jax.experimental import pallas as pl
from jax.experimental.pallas import tpu as pltpu
from jax.sharding import PartitionSpec as P

PW = 256


def swap_order(piv_row, offset, count):
    own = offset + jnp.arange(piv_row.shape[0], dtype=jnp.int32)
    base = jnp.arange(count, dtype=jnp.int32)
    return base.at[own].set(piv_row).at[piv_row].set(own)


def pick_rows(data, perm, targets, start):
    local_src = perm[targets] - start
    owned = (local_src >= 0) & (local_src < data.shape[0])
    taken = jnp.take(data, jnp.clip(local_src, 0, data.shape[0] - 1), axis=0)
    return jnp.where(owned[:, None], taken, 0.0)


def place_rows(data, targets, values, start):
    local_dst = targets - start
    inside = (local_dst >= 0) & (local_dst < data.shape[0])
    where_to = jnp.where(inside, local_dst, data.shape[0])
    return data.at[where_to].set(values, mode="drop")


def solve_top(diag_rows, rows):
    strict = jnp.tril(diag_rows, -1)
    inverse = jnp.eye(PW, dtype=jnp.float32) - strict
    power = strict
    for level in range(1, PW.bit_length() - 1):
        power = jnp.dot(
            power, power, precision=lax.Precision.HIGHEST, preferred_element_type=jnp.float32
        )
        inverse = inverse + jnp.dot(
            inverse, power, precision=lax.Precision.HIGHEST, preferred_element_type=jnp.float32
        )
    return jnp.dot(
        inverse, rows, precision=lax.Precision.HIGHEST, preferred_element_type=jnp.float32
    )


def finish(work, lower, offset, start, upper):
    product = jnp.dot(
        lower, upper, precision=lax.Precision.HIGHEST, preferred_element_type=jnp.float32
    )
    global_rows = start + jnp.arange(work.shape[0], dtype=jnp.int32)
    work = jnp.where((global_rows >= offset + PW)[:, None], work - product, work)
    placed = work.at[offset : offset + PW].set(upper)
    in_top = (global_rows >= offset) & (global_rows < offset + PW)
    return jnp.where(in_top[:, None], placed, work)


def plain(block, panels, pivots):
    rows_here = block.shape[0]
    rows_all = rows_here * lax.axis_size("row")
    start = lax.axis_index("row") * rows_here
    identity_perm = jnp.arange(rows_all, dtype=jnp.int32)
    perms = [swap_order(pivots[panel], panel * PW, rows_all) for panel in range(2)]
    targets = [
        jnp.concatenate([jnp.arange(panel * PW, panel * PW + PW, dtype=jnp.int32), pivots[panel]])
        for panel in range(2)
    ]
    tops_index = [jnp.arange(panel * PW, panel * PW + PW, dtype=jnp.int32) for panel in range(2)]
    work = block
    lowers = lax.all_gather(panels, "col", axis=2, tiled=True)
    for panel in range(2):
        offset = panel * PW
        diag_rows = pick_rows(lowers[panel], identity_perm, tops_index[panel], start)
        picked = pick_rows(work, perms[panel], targets[panel], start)
        moved, diag_all = lax.psum((picked, diag_rows), "row")
        work = place_rows(work, targets[panel], moved, start)
        upper = solve_top(diag_all, moved[:PW])
        work = finish(work, lowers[panel], offset, start, upper)
    return work

MESH = pl.DeviceIdType.MESH
F32, BF16 = jnp.float32, jnp.bfloat16
CHUNKS = 4


def dot(a, b):
    return jnp.dot(a, b, preferred_element_type=F32)


def split(a):
    high = a.astype(BF16)
    return high, (a - high.astype(F32)).astype(BF16)


def dot_split(a, b):
    a_high, a_low = a
    b_high, b_low = b
    return dot(a_high, b_high) + (dot(a_high, b_low) + dot(a_low, b_high))


def dot_pick(a, one_hot):
    m = a.shape[0]
    high, rest = a.astype(BF16), None
    rest = a - high.astype(F32)
    mid = rest.astype(BF16)
    low = (rest - mid.astype(F32)).astype(BF16)
    out = dot(jnp.concatenate([high, mid, low], 0), one_hot)
    return out[:m] + (out[m : 2 * m] + out[2 * m :])


def iota(shape, dim):
    return lax.broadcasted_iota(jnp.int32, shape, dim)


def one_hot(condition):
    return jnp.where(condition, 1.0, 0.0)


def invert_upper(upper_part):
    n = upper_part.shape[0]
    row, col = iota((n, n), 0), iota((n, n), 1)
    strict = jnp.where(row < col, upper_part, 0.0)
    size = 32
    power = jnp.where(row // size == col // size, strict, 0.0)
    inverse = one_hot(row == col) - power
    span = 2
    while span < size:
        parts = split(power)
        power = dot_split(parts, parts)
        inverse = inverse + dot_split(split(inverse), split(power))
        span *= 2
    while size < n:
        pair = (row // (2 * size) == col // (2 * size)) & (row // size != col // size)
        parts = split(inverse)
        right = dot_split(split(jnp.where(pair, strict, 0.0)), parts)
        inverse = inverse - dot_split(parts, split(right))
        size *= 2
    return inverse


def kernel(
    n_row, n_col, piv_ref, block_ref, panels_ref, out_ref,
    g_diag, g_top, g_one, g_zero, v_in, v_out, s_in, s_out, vl_in, vl_out, sl_in, sl_out,
    d_sem, vl_sem, sl_sem, v_sem, s_sem, peer_send, peer_recv, sib_send, sib_recv,
):
    r, c = lax.axis_index("row"), lax.axis_index("col")
    rows, cols = block_ref.shape
    tops = 2 * PW
    kc = panels_ref.shape[2]
    n_peer = n_col // 2
    sibling = c + 1 - 2 * (c % 2)
    is_first, is_last = r == 0, r == n_row - 1
    start = r * rows

    barrier = pltpu.get_barrier_semaphore()

    @pl.when(r > 0)
    def _():
        pl.semaphore_signal(barrier, 1, device_id={"row": r - 1}, device_id_type=MESH)

    @pl.when(r < n_row - 1)
    def _():
        pl.semaphore_signal(barrier, 1, device_id={"row": r + 1}, device_id_type=MESH)

    for m in range(1, n_peer):
        pl.semaphore_signal(barrier, 1, device_id={"col": (c + 2 * m) % n_col}, device_id_type=MESH)
    pl.semaphore_signal(barrier, 1, device_id={"col": sibling}, device_id_type=MESH)

    zero_t, one_t = panels_ref[0].T, panels_ref[1].T
    block_t = block_ref[...].T
    g_one[c] = one_t

    @pl.when(is_first)
    def _():
        g_diag[c, 0] = zero_t[:, :PW]
        g_diag[c, 1] = one_t[:, PW:tops]

    @pl.when((r > 0) & (r < n_row - 1))
    def _():
        pl.semaphore_wait(barrier, n_peer + 2)

    @pl.when(is_first | is_last)
    def _():
        pl.semaphore_wait(barrier, n_peer + 1)

    def hop(src, dst, sem, k, to):
        return pltpu.make_async_remote_copy(
            src_ref=src, dst_ref=dst, send_sem=sem.at[0, k], recv_sem=sem.at[1, k],
            device_id={"row": to}, device_id_type=MESH,
        )

    gathered = (g_one, g_diag, g_top, g_zero)

    def peer_copy(kind, m, slot):
        buf = gathered[kind]
        return pltpu.make_async_remote_copy(
            src_ref=buf.at[slot], dst_ref=buf.at[slot],
            send_sem=peer_send.at[kind, m], recv_sem=peer_recv.at[kind, m],
            device_id={"col": (c + 2 * m) % n_col}, device_id_type=MESH,
        )

    def sib_copy(kind, m, slot):
        buf = gathered[kind]
        return pltpu.make_async_remote_copy(
            src_ref=buf.at[slot], dst_ref=buf.at[slot],
            send_sem=sib_send.at[kind, m], recv_sem=sib_recv.at[kind, m],
            device_id={"col": sibling}, device_id_type=MESH,
        )

    def spread(kind):
        for m in range(1, n_peer):
            peer_copy(kind, m, c).start()
        sib_copy(kind, 0, c).start()

    def share(kind):
        for m in range(1, n_peer):
            slot = (c + n_col - 2 * m) % n_col
            peer_copy(kind, m, slot).wait_recv()
            sib_copy(kind, m, slot).start()

    def settle(kind):
        for m in range(n_peer):
            sib_copy(kind, m, (sibling + n_col - 2 * m) % n_col).wait_recv()

    spread(0)

    diag_copy = hop(g_diag.at[c], g_diag.at[c], d_sem, 0, r + 1)

    @pl.when(r > 0)
    def _():
        diag_copy.wait_recv()

    @pl.when(r < n_row - 1)
    def _():
        diag_copy.start()

    spread(1)

    first = piv_ref[0:1, :].astype(F32)
    second = piv_ref[1:2, :].astype(F32)
    sub, lane = iota((PW, PW), 0).astype(F32), iota((PW, PW), 1).astype(F32)
    eye = sub == lane

    def upright(v):
        return jnp.sum(jnp.where(eye, v, 0.0), axis=1, keepdims=True)

    first_c, second_c = upright(first), upright(second)
    lane_row = lane[0:1, :]
    sub_col = sub[:, 0:1]

    def lookup(match, found, otherwise, axis):
        hit = jnp.sum(one_hot(match), axis=axis, keepdims=True)
        return jnp.sum(jnp.where(match, found, 0.0), axis=axis, keepdims=True) + jnp.where(hit > 0.5, 0.0, otherwise)

    q_second = lookup(first_c == second, sub, second, 0)
    q_second_c = lookup(second_c == first, lane, second_c, 1)
    home = lookup(first_c == lane + PW, sub, lane_row + PW, 0)
    home_c = lookup(first == sub + PW, lane, sub_col + PW, 1)
    out_first = jnp.where(first < tops, first, lookup(second_c == first, home_c, lane_row, 0))
    out_second = jnp.where(q_second < tops, q_second, home)
    q = jnp.concatenate([first, q_second], 1)
    q_c = jnp.concatenate([first_c, q_second_c], 0)
    outward = jnp.concatenate([out_first, out_second], 1)

    start_f = start.astype(F32)
    local = jnp.where(is_first, outward, q - start_f)
    local_one = jnp.where(is_first, lane_row + PW, second - start_f)
    mine = (q >= start_f) & (q < start_f + rows)
    before = q < start_f
    mine_one = (second >= start_f) & (second < start_f + rows)
    before_one = second < start_f

    pick_one = one_hot(iota((rows, PW), 0).astype(F32) == local_one).astype(BF16)
    own_top = dot_pick(zero_t, pick_one)

    right_l = hop(vl_out, vl_in, vl_sem, 0, r + 1)
    left_l = hop(sl_out, sl_in, sl_sem, 0, r - 1)

    def go_right_l():
        @pl.when(is_first)
        def _():
            vl_out[...] = own_top
            right_l.start()

        @pl.when(r > 0)
        def _():
            right_l.wait_recv()

        @pl.when((r > 0) & (r < n_row - 1))
        def _():
            vl_out[...] = jnp.where(mine_one, own_top, vl_in[...])
            right_l.start()

    def go_left_l():
        @pl.when(is_last)
        def _():
            sl_out[...] = jnp.where(mine_one, own_top, 0.0)
            left_l.start()

        @pl.when(r < n_row - 1)
        def _():
            left_l.wait_recv()

        @pl.when((r > 0) & (r < n_row - 1))
        def _():
            sl_out[...] = jnp.where(mine_one, own_top, sl_in[...])
            left_l.start()

    pick = one_hot(iota((rows, tops), 0).astype(F32) == local).astype(BF16)
    own = dot_pick(block_t, pick)
    part = cols // CHUNKS

    def go_right(k):
        at = pl.ds(k * part, part)
        piece = own[k * part : (k + 1) * part]
        copy = hop(v_out.at[at], v_in.at[at], v_sem, k, r + 1)

        @pl.when(is_first)
        def _():
            v_out[at, :] = piece
            copy.start()

        @pl.when(r > 0)
        def _():
            copy.wait_recv()

        @pl.when((r > 0) & (r < n_row - 1))
        def _():
            v_out[at, :] = jnp.where(mine, piece, v_in[at, :])
            copy.start()

    def go_left(k):
        at = pl.ds(k * part, part)
        piece = own[k * part : (k + 1) * part]
        copy = hop(s_out.at[at], s_in.at[at], s_sem, k, r - 1)

        @pl.when(is_last)
        def _():
            s_out[at, :] = jnp.where(mine, piece, 0.0)
            copy.start()

        @pl.when(r < n_row - 1)
        def _():
            copy.wait_recv()

        @pl.when((r > 0) & (r < n_row - 1))
        def _():
            s_out[at, :] = jnp.where(mine, piece, s_in[at, :])
            copy.start()

    def both(right, left):
        @pl.when(2 * r < n_row)
        def _():
            right()
            left()

        @pl.when(2 * r >= n_row)
        def _():
            left()
            right()

    both(go_right_l, go_left_l)

    @pl.when(is_first)
    def _():
        g_top[c] = jnp.where(mine_one, own_top, sl_in[...])
        g_zero[c] = zero_t

    @pl.when(is_last)
    def _():
        g_top[c] = jnp.where(before_one, vl_in[...], own_top)

    @pl.when((r > 0) & (r < n_row - 1))
    def _():
        g_top[c] = jnp.where(before_one, vl_in[...], jnp.where(mine_one, own_top, sl_in[...]))

    @pl.when(r > 0)
    def _():
        put = one_hot(iota((PW, rows), 1).astype(F32) == second_c - start_f)
        moved = jnp.sum(put, axis=0, keepdims=True) > 0.5
        g_zero[c] = jnp.where(moved, dot_pick(vl_in[...], put.astype(BF16)), zero_t)

    spread(2)
    spread(3)

    for k in range(CHUNKS):
        both(lambda: go_right(k), lambda: go_left(k))
        share(k)
    settle(1)
    inverses = [split(invert_upper(g_diag[:, p].reshape(PW, PW))) for p in range(2)]

    for kind in (0, 2, 3):
        settle(kind)

    @pl.when(is_first)
    def _():
        v_in[...] = jnp.where(mine, own, s_in[...])

    @pl.when(is_last)
    def _():
        s_in[...] = jnp.where(before, v_in[...], own)

    @pl.when((r > 0) & (r < n_row - 1))
    def _():
        s_in[...] = jnp.where(before, v_in[...], jnp.where(mine, own, s_in[...]))

    top = jnp.where(is_first, v_in[...], s_in[...])
    upper0 = split(dot_split(split(top[:, :PW]), inverses[0]))
    rest = top[:, PW:] - dot_split(upper0, split(g_top[...].reshape(PW, PW)))
    upper1_full = dot_split(split(rest), inverses[1])
    upper1 = split(upper1_full)

    @pl.when(is_first)
    def _():
        upper0_full = dot_split(split(top[:, :PW]), inverses[0])
        out_ref[...] = jnp.concatenate([upper0_full, upper1_full], 1).T

    @pl.when(r > 0)
    def _():
        put = one_hot(iota((tops, rows), 1).astype(F32) == q_c - start_f)
        moved = jnp.sum(put, axis=0, keepdims=True) > 0.5
        work = jnp.where(moved, dot_pick(v_in[...], put.astype(BF16)), block_t)
        work = work - dot_split(upper0, split(g_zero[...].reshape(PW, rows)))
        work = work - dot_split(upper1, split(g_one[...].reshape(PW, rows)))
        out_ref[...] = work.T

    for kind in range(4):
        for m in range(1, n_peer):
            peer_copy(kind, m, c).wait_send()
        for m in range(n_peer):
            sib_copy(kind, m, c).wait_send()

    @pl.when(r < n_row - 1)
    def _():
        diag_copy.wait_send()
        right_l.wait_send()
        for k in range(CHUNKS):
            at = pl.ds(k * part, part)
            hop(v_out.at[at], v_in.at[at], v_sem, k, r + 1).wait_send()

    @pl.when(r > 0)
    def _():
        left_l.wait_send()
        for k in range(CHUNKS):
            at = pl.ds(k * part, part)
            hop(s_out.at[at], s_in.at[at], s_sem, k, r - 1).wait_send()


def fused(block, panels, pivots):
    n_row, n_col = lax.axis_size("row"), lax.axis_size("col")
    rows, cols = block.shape
    kc = panels.shape[2]
    tops = 2 * PW
    vmem = pl.BlockSpec(memory_space=pltpu.VMEM)
    n_peer = n_col // 2
    dma = pltpu.SemaphoreType.DMA
    return pl.pallas_call(
        functools.partial(kernel, n_row, n_col),
        out_shape=jax.ShapeDtypeStruct((rows, cols), F32),
        in_specs=[vmem] * 3,
        out_specs=vmem,
        scratch_shapes=[
            pltpu.VMEM((n_col, 2, kc, PW), F32),
            pltpu.VMEM((n_col, kc, PW), F32),
            pltpu.VMEM((n_col, kc, rows), F32),
            pltpu.VMEM((n_col, kc, rows), F32),
        ]
        + [pltpu.VMEM((cols, tops), F32)] * 4
        + [pltpu.VMEM((kc, PW), F32)] * 4
        + [dma((2, 1))] * 3
        + [dma((2, CHUNKS))] * 2
        + [dma((4, n_peer))] * 4,
        compiler_params=pltpu.CompilerParams(
            collective_id=0, has_side_effects=True, vmem_limit_bytes=48 * 1024 * 1024
        ),
    )(pivots, block, panels)


def body(block, panels, pivots):
    fits = (
        block.shape[0] == 2 * PW
        and block.shape[1] % 128 == 0
        and panels.shape[2] % 8 == 0
        and lax.axis_size("col") % 2 == 0
        and lax.axis_size("row") > 1
    )
    return fused(block, panels, pivots) if fits else plain(block, panels, pivots)


def solution(mesh):
    return jax.shard_map(
        body,
        mesh=mesh,
        in_specs=(P("row", "col"), P(None, "row", "col"), P()),
        out_specs=P("row", "col"),
        check_vma=False,
    )
```

```python
import functools

import jax
import jax.numpy as jnp
from jax import lax
from jax.experimental import pallas as pl
from jax.experimental.pallas import tpu as pltpu
from jax.sharding import PartitionSpec as P

PW = 256


def swap_order(piv_row, offset, count):
    own = offset + jnp.arange(piv_row.shape[0], dtype=jnp.int32)
    base = jnp.arange(count, dtype=jnp.int32)
    return base.at[own].set(piv_row).at[piv_row].set(own)


def pick_rows(data, perm, targets, start):
    local_src = perm[targets] - start
    owned = (local_src >= 0) & (local_src < data.shape[0])
    taken = jnp.take(data, jnp.clip(local_src, 0, data.shape[0] - 1), axis=0)
    return jnp.where(owned[:, None], taken, 0.0)


def place_rows(data, targets, values, start):
    local_dst = targets - start
    inside = (local_dst >= 0) & (local_dst < data.shape[0])
    where_to = jnp.where(inside, local_dst, data.shape[0])
    return data.at[where_to].set(values, mode="drop")


def solve_top(diag_rows, rows):
    strict = jnp.tril(diag_rows, -1)
    inverse = jnp.eye(PW, dtype=jnp.float32) - strict
    power = strict
    for level in range(1, PW.bit_length() - 1):
        power = jnp.dot(
            power, power, precision=lax.Precision.HIGHEST, preferred_element_type=jnp.float32
        )
        inverse = inverse + jnp.dot(
            inverse, power, precision=lax.Precision.HIGHEST, preferred_element_type=jnp.float32
        )
    return jnp.dot(
        inverse, rows, precision=lax.Precision.HIGHEST, preferred_element_type=jnp.float32
    )


def finish(work, lower, offset, start, upper):
    product = jnp.dot(
        lower, upper, precision=lax.Precision.HIGHEST, preferred_element_type=jnp.float32
    )
    global_rows = start + jnp.arange(work.shape[0], dtype=jnp.int32)
    work = jnp.where((global_rows >= offset + PW)[:, None], work - product, work)
    placed = work.at[offset : offset + PW].set(upper)
    in_top = (global_rows >= offset) & (global_rows < offset + PW)
    return jnp.where(in_top[:, None], placed, work)


def plain(block, panels, pivots):
    rows_here = block.shape[0]
    rows_all = rows_here * lax.axis_size("row")
    start = lax.axis_index("row") * rows_here
    identity_perm = jnp.arange(rows_all, dtype=jnp.int32)
    perms = [swap_order(pivots[panel], panel * PW, rows_all) for panel in range(2)]
    targets = [
        jnp.concatenate([jnp.arange(panel * PW, panel * PW + PW, dtype=jnp.int32), pivots[panel]])
        for panel in range(2)
    ]
    tops_index = [jnp.arange(panel * PW, panel * PW + PW, dtype=jnp.int32) for panel in range(2)]
    work = block
    lowers = lax.all_gather(panels, "col", axis=2, tiled=True)
    for panel in range(2):
        offset = panel * PW
        diag_rows = pick_rows(lowers[panel], identity_perm, tops_index[panel], start)
        picked = pick_rows(work, perms[panel], targets[panel], start)
        moved, diag_all = lax.psum((picked, diag_rows), "row")
        work = place_rows(work, targets[panel], moved, start)
        upper = solve_top(diag_all, moved[:PW])
        work = finish(work, lowers[panel], offset, start, upper)
    return work

MESH = pl.DeviceIdType.MESH
F32, BF16 = jnp.float32, jnp.bfloat16
SMALL = 32
DIAG, ONE, ZERO, TOP = range(4)


def dot(a, b):
    return jnp.dot(a, b, preferred_element_type=F32)


def split(a):
    high = a.astype(BF16)
    return high, (a - high.astype(F32)).astype(BF16)


def dot_split(a, b):
    m = a[0].shape[0]
    both = dot(jnp.concatenate(a, 0), b[0])
    return both[:m] + (both[m:] + dot(a[0], b[1]))


def dot_pick(a, one_hot):
    m = a.shape[0]
    high = a.astype(BF16)
    rest = a - high.astype(F32)
    mid = rest.astype(BF16)
    low = (rest - mid.astype(F32)).astype(BF16)
    out = dot(jnp.concatenate([high, mid, low], 0), one_hot)
    return out[:m] + (out[m : 2 * m] + out[2 * m :])


def iota(shape, dim):
    return lax.broadcasted_iota(jnp.int32, shape, dim)


def one_hot(condition):
    return jnp.where(condition, 1.0, 0.0)


def kernel(
    n_row, n_col, piv_ref, block_ref, panels_ref, out_ref,
    g, g_top, own_ref, f_in, f_out, l_in, l_out, power_ref, small_ref, inverse_ref,
    d_sem, l_sem, f_sem, peer_send, peer_recv, sib_send, sib_recv,
):
    r, c = lax.axis_index("row"), lax.axis_index("col")
    rows, cols = block_ref.shape
    tops = 2 * PW
    kc = panels_ref.shape[1]
    n_peer = n_col // 2
    chunks = cols // kc
    last = n_row - 1
    sibling = c + 1 - 2 * (c % 2)
    is_first, is_last = r == 0, r == last
    is_middle = (r > 0) & (r < last)
    is_upper = 2 * r >= n_row
    start = r * rows

    barrier = pltpu.get_barrier_semaphore()

    @pl.when(r > 0)
    def _():
        pl.semaphore_signal(barrier, 1, device_id={"row": r - 1}, device_id_type=MESH)

    @pl.when(r < last)
    def _():
        pl.semaphore_signal(barrier, 1, device_id={"row": r + 1}, device_id_type=MESH)

    for m in range(1, n_peer):
        pl.semaphore_signal(barrier, 1, device_id={"col": (c + 2 * m) % n_col}, device_id_type=MESH)
    pl.semaphore_signal(barrier, 1, device_id={"col": sibling}, device_id_type=MESH)

    first = piv_ref[0:1, :].astype(F32)
    second = piv_ref[1:2, :].astype(F32)
    sub, lane = iota((PW, PW), 0).astype(F32), iota((PW, PW), 1).astype(F32)

    def upright(v):
        return jnp.sum(jnp.where(sub == lane, v, 0.0), axis=1, keepdims=True)

    first_c, second_c = upright(first), upright(second)
    lane_row = lane[0:1, :]
    sub_col = sub[:, 0:1]

    def lookup(match, found, otherwise, axis):
        hit = jnp.sum(one_hot(match), axis=axis, keepdims=True)
        return jnp.sum(jnp.where(match, found, 0.0), axis=axis, keepdims=True) + jnp.where(hit > 0.5, 0.0, otherwise)

    q_second = lookup(first_c == second, sub, second, 0)
    q_second_c = lookup(second_c == first, lane, second_c, 1)
    home = lookup(first_c == lane + PW, sub, lane_row + PW, 0)
    home_c = lookup(first == sub + PW, lane, sub_col + PW, 1)
    out_first = jnp.where(first < tops, first, lookup(second_c == first, home_c, lane_row, 0))
    out_second = jnp.where(q_second < tops, q_second, home)
    q = jnp.concatenate([first, q_second], 1)
    q_c = jnp.concatenate([first_c, q_second_c], 0)
    outward = jnp.concatenate([out_first, out_second], 1)

    start_f = start.astype(F32)
    local = jnp.where(is_first, outward, q - start_f)
    local_one = jnp.where(is_first, lane_row + PW, second - start_f)

    def from_here(v):
        return (v >= start_f) & (v < start_f + rows)

    own_top = dot_pick(panels_ref[0], one_hot(iota((rows, PW), 0).astype(F32) == local_one).astype(BF16))
    l_out[0] = own_top
    l_out[1] = own_top
    block_t = block_ref[...].T
    own = dot_pick(block_t, one_hot(iota((rows, tops), 0).astype(F32) == local).astype(BF16))
    own_ref[...] = own
    f_out[0] = own
    f_out[1] = own

    @pl.when(is_first)
    def _():
        g[DIAG, c] = jnp.concatenate([panels_ref[0, :, :PW], panels_ref[1, :, PW:tops]], 1)

    @pl.when(r > 0)
    def _():
        g[ONE, c] = panels_ref[1]

    @pl.when(is_middle)
    def _():
        pl.semaphore_wait(barrier, n_peer + 2)

    @pl.when(is_first | is_last)
    def _():
        pl.semaphore_wait(barrier, n_peer + 1)

    def l_copy(d):
        return pltpu.make_async_remote_copy(
            src_ref=l_out.at[d], dst_ref=l_in.at[d], send_sem=l_sem.at[0, d], recv_sem=l_sem.at[1, d],
            device_id={"row": r + 1 - 2 * d}, device_id_type=MESH,
        )

    def f_copy(k, d):
        at = pl.ds(pl.multiple_of(k * kc, 8), kc)
        return pltpu.make_async_remote_copy(
            src_ref=f_out.at[d, at], dst_ref=f_in.at[d, at],
            send_sem=f_sem.at[0, d, k], recv_sem=f_sem.at[1, d, k],
            device_id={"row": r + 1 - 2 * d}, device_id_type=MESH,
        )

    diag_copy = pltpu.make_async_remote_copy(
        src_ref=g.at[DIAG, c], dst_ref=g.at[DIAG, c], send_sem=d_sem.at[0], recv_sem=d_sem.at[1],
        device_id={"row": r + 1}, device_id_type=MESH,
    )

    def arrives(d):
        return jnp.where(d == 0, r > 0, r < last)

    def l_step(d):
        @pl.when(arrives(d))
        def _():
            l_copy(d).wait_recv()

        @pl.when(is_middle)
        def _():
            l_out[d] = jnp.where(from_here(second), l_out[d], l_in[d])
            l_copy(d).start()

    def f_step(k, d):
        @pl.when(arrives(d))
        def _():
            f_copy(k, d).wait_recv()

        @pl.when(is_middle)
        def _():
            at = pl.ds(pl.multiple_of(k * kc, 8), kc)
            f_out[d, at, :] = jnp.where(from_here(q), f_out[d, at, :], f_in[d, at, :])
            f_copy(k, d).start()

    def slot_ref(kind, slot):
        return g_top.at[slot] if kind == TOP else g.at[kind, slot]

    def peer_copy(kind, m, slot):
        return pltpu.make_async_remote_copy(
            src_ref=slot_ref(kind, slot), dst_ref=slot_ref(kind, slot),
            send_sem=peer_send.at[kind, m], recv_sem=peer_recv.at[kind, m],
            device_id={"col": (c + 2 * m) % n_col}, device_id_type=MESH,
        )

    def sib_copy(kind, m, slot):
        return pltpu.make_async_remote_copy(
            src_ref=slot_ref(kind, slot), dst_ref=slot_ref(kind, slot),
            send_sem=sib_send.at[kind, m], recv_sem=sib_recv.at[kind, m],
            device_id={"col": sibling}, device_id_type=MESH,
        )

    def spread(kind):
        for m in range(1, n_peer):
            peer_copy(kind, m, c).start()
        sib_copy(kind, 0, c).start()

    def share(kind):
        for m in range(1, n_peer):
            slot = (c + n_col - 2 * m) % n_col
            peer_copy(kind, m, slot).wait_recv()
            sib_copy(kind, m, slot).start()

    def settle(kind):
        for m in range(n_peer):
            sib_copy(kind, m, (sibling + n_col - 2 * m) % n_col).wait_recv()

    def drain(kind):
        for m in range(1, n_peer):
            peer_copy(kind, m, c).wait_send()
        for m in range(n_peer):
            sib_copy(kind, m, c).wait_send()

    @pl.when(is_first)
    def _():
        diag_copy.start()
        spread(DIAG)
        l_copy(0).start()
        for k in range(chunks):
            f_copy(k, 0).start()

    @pl.when(is_last)
    def _():
        l_copy(1).start()
        for k in range(chunks):
            f_copy(k, 1).start()

    @pl.when(is_upper)
    def _():
        l_step(1)

    @pl.when(r > 0)
    def _():
        diag_copy.wait_recv()

        @pl.when(r < last)
        def _():
            diag_copy.start()

        spread(DIAG)

    l_step(0)

    @pl.when(jnp.logical_not(is_upper))
    def _():
        l_step(1)

    top_rows = jnp.where(second < start_f, l_in[0], jnp.where(from_here(second), own_top, l_in[1]))
    g_top[c] = top_rows
    spread(TOP)

    @pl.when(r > 0)
    def _():
        put = one_hot(iota((PW, rows), 1).astype(F32) == second_c - start_f)
        moved = jnp.sum(put, axis=0, keepdims=True) > 0.5
        g[ZERO, c] = jnp.where(moved, dot_pick(l_in[0], put.astype(BF16)), panels_ref[0])
        spread(ZERO)
        spread(ONE)

    def strict(p):
        upper = g[DIAG, :, :, p * PW : (p + 1) * PW].reshape(PW, PW)
        return jnp.where(iota((PW, PW), 0) < iota((PW, PW), 1), upper, 0.0)

    def spaced(small):
        same = iota((PW, PW), 0) // SMALL == iota((PW, PW), 1) // SMALL
        return jnp.where(same, jnp.concatenate([small] * (PW // SMALL), 0), 0.0)

    def begin():
        share(DIAG)
        settle(DIAG)
        lanes = iota((SMALL, PW), 1)
        for p in range(2):
            whole = strict(p)
            small = jnp.zeros((SMALL, PW), F32)
            for b in range(PW // SMALL):
                small += jnp.where(lanes // SMALL == b, whole[b * SMALL : (b + 1) * SMALL], 0.0)
            small_ref[p] = one_hot(lanes % SMALL == iota((SMALL, PW), 0)) - small
            power_ref[p] = dot_split(split(small), split(spaced(small)))

    def double(_, carry):
        for p in range(2):
            power, small = power_ref[p], small_ref[p]
            new = dot_split(split(jnp.concatenate([power, small], 0)), split(spaced(power)))
            power_ref[p] = new[:SMALL]
            small_ref[p] = small + new[SMALL:]
        return carry

    def widen():
        for p in range(2):
            inverse_ref[p] = spaced(small_ref[p])

    def merge(level):
        shift = SMALL.bit_length() - 1 + level
        row, col = iota((PW, PW), 0), iota((PW, PW), 1)
        pair = ((row >> (shift + 1)) == (col >> (shift + 1))) & ((row >> shift) != (col >> shift))
        for p in range(2):
            inverse = inverse_ref[p]
            parts = split(inverse)
            right = dot_split(split(jnp.where(pair, strict(p), 0.0)), parts)
            inverse_ref[p] = inverse - dot_split(parts, split(right))

    doublings = SMALL.bit_length() - 2
    merges = (PW // SMALL).bit_length() - 1

    def turn(k, carry):
        @pl.when(k < chunks)
        def _():
            upper = jnp.where(is_upper, 1, 0)
            f_step(k, upper)
            f_step(k, 1 - upper)

        @pl.when(k == 0)
        def _():
            begin()

        @pl.when(k == 1)
        def _():
            share(TOP)

        @pl.when((k == 2) & (r > 0))
        def _():
            share(ZERO)

        @pl.when((k == 3) & (r > 0))
        def _():
            share(ONE)

        @pl.when(k < 2)
        def _():
            lax.fori_loop(0, doublings // 2, double, 0)

        @pl.when(k == 2)
        def _():
            widen()

        @pl.when(k >= 2)
        def _():
            merge(k - 2)

        return carry

    lax.fori_loop(0, 2 + merges, turn, 0)
    settle(TOP)

    top = jnp.where(q < start_f, f_in[0], jnp.where(from_here(q), own_ref[...], f_in[1]))
    upper0_full = dot_split(split(top[:, :PW]), split(inverse_ref[0]))
    upper0 = split(upper0_full)
    rest = top[:, PW:] - dot_split(upper0, split(g_top[...].reshape(PW, PW)))
    upper1_full = dot_split(split(rest), split(inverse_ref[1]))

    @pl.when(is_first)
    def _():
        out_ref[...] = jnp.concatenate([upper0_full, upper1_full], 1).T

    @pl.when(r > 0)
    def _():
        settle(ZERO)
        settle(ONE)
        put = one_hot(iota((tops, rows), 1).astype(F32) == q_c - start_f)
        moved = jnp.sum(put, axis=0, keepdims=True) > 0.5
        work = jnp.where(moved, dot_pick(f_in[0], put.astype(BF16)), block_ref[...].T)
        work = work - dot_split(upper0, split(g[ZERO].reshape(PW, rows)))
        work = work - dot_split(split(upper1_full), split(g[ONE].reshape(PW, rows)))
        out_ref[...] = work.T
        drain(ZERO)
        drain(ONE)

    drain(DIAG)
    drain(TOP)

    @pl.when(r < last)
    def _():
        diag_copy.wait_send()

    for d in range(2):
        @pl.when((r < last) if d == 0 else (r > 0))
        def _():
            l_copy(d).wait_send()
            for k in range(chunks):
                f_copy(k, d).wait_send()


def fused(block, panels, pivots):
    n_row, n_col = lax.axis_size("row"), lax.axis_size("col")
    rows, cols = block.shape
    kc = panels.shape[2]
    tops = 2 * PW
    vmem = pl.BlockSpec(memory_space=pltpu.VMEM)
    n_peer = n_col // 2
    dma = pltpu.SemaphoreType.DMA
    return pl.pallas_call(
        functools.partial(kernel, n_row, n_col),
        out_shape=jax.ShapeDtypeStruct((rows, cols), F32),
        in_specs=[vmem] * 3,
        out_specs=vmem,
        scratch_shapes=[
            pltpu.VMEM((3, n_col, kc, rows), F32),
            pltpu.VMEM((n_col, kc, PW), F32),
            pltpu.VMEM((cols, tops), F32),
            pltpu.VMEM((2, cols, tops), F32),
            pltpu.VMEM((2, cols, tops), F32),
            pltpu.VMEM((2, kc, PW), F32),
            pltpu.VMEM((2, kc, PW), F32),
            pltpu.VMEM((2, SMALL, PW), F32),
            pltpu.VMEM((2, SMALL, PW), F32),
            pltpu.VMEM((2, PW, PW), F32),
            dma((2,)),
            dma((2, 2)),
            dma((2, 2, cols // kc)),
        ]
        + [dma((4, n_peer))] * 4,
        compiler_params=pltpu.CompilerParams(
            collective_id=0, has_side_effects=True, vmem_limit_bytes=48 * 1024 * 1024
        ),
    )(pivots, block, jnp.swapaxes(panels, 1, 2))


def body(block, panels, pivots):
    kc = panels.shape[2]
    fits = (
        block.shape[0] == 2 * PW
        and block.shape[1] % 128 == 0
        and kc % 8 == 0
        and block.shape[1] // kc in range(1, 6)
        and block.shape[1] % kc == 0
        and lax.axis_size("col") % 2 == 0
        and lax.axis_size("row") > 1
    )
    return fused(block, panels, pivots) if fits else plain(block, panels, pivots)


def solution(mesh):
    return jax.shard_map(
        body,
        mesh=mesh,
        in_specs=(P("row", "col"), P(None, "row", "col"), P()),
        out_specs=P("row", "col"),
        check_vma=False,
    )
```

```python
import functools

import jax
import jax.numpy as jnp
from jax import lax
from jax.experimental import pallas as pl
from jax.experimental.pallas import tpu as pltpu
from jax.sharding import PartitionSpec as P

PW = 256


def swap_order(piv_row, offset, count):
    own = offset + jnp.arange(piv_row.shape[0], dtype=jnp.int32)
    base = jnp.arange(count, dtype=jnp.int32)
    return base.at[own].set(piv_row).at[piv_row].set(own)


def pick_rows(data, perm, targets, start):
    local_src = perm[targets] - start
    owned = (local_src >= 0) & (local_src < data.shape[0])
    taken = jnp.take(data, jnp.clip(local_src, 0, data.shape[0] - 1), axis=0)
    return jnp.where(owned[:, None], taken, 0.0)


def place_rows(data, targets, values, start):
    local_dst = targets - start
    inside = (local_dst >= 0) & (local_dst < data.shape[0])
    where_to = jnp.where(inside, local_dst, data.shape[0])
    return data.at[where_to].set(values, mode="drop")


def solve_top(diag_rows, rows):
    strict = jnp.tril(diag_rows, -1)
    inverse = jnp.eye(PW, dtype=jnp.float32) - strict
    power = strict
    for level in range(1, PW.bit_length() - 1):
        power = jnp.dot(
            power, power, precision=lax.Precision.HIGHEST, preferred_element_type=jnp.float32
        )
        inverse = inverse + jnp.dot(
            inverse, power, precision=lax.Precision.HIGHEST, preferred_element_type=jnp.float32
        )
    return jnp.dot(
        inverse, rows, precision=lax.Precision.HIGHEST, preferred_element_type=jnp.float32
    )


def finish(work, lower, offset, start, upper):
    product = jnp.dot(
        lower, upper, precision=lax.Precision.HIGHEST, preferred_element_type=jnp.float32
    )
    global_rows = start + jnp.arange(work.shape[0], dtype=jnp.int32)
    work = jnp.where((global_rows >= offset + PW)[:, None], work - product, work)
    placed = work.at[offset : offset + PW].set(upper)
    in_top = (global_rows >= offset) & (global_rows < offset + PW)
    return jnp.where(in_top[:, None], placed, work)


def plain(block, panels, pivots):
    rows_here = block.shape[0]
    rows_all = rows_here * lax.axis_size("row")
    start = lax.axis_index("row") * rows_here
    identity_perm = jnp.arange(rows_all, dtype=jnp.int32)
    perms = [swap_order(pivots[panel], panel * PW, rows_all) for panel in range(2)]
    targets = [
        jnp.concatenate([jnp.arange(panel * PW, panel * PW + PW, dtype=jnp.int32), pivots[panel]])
        for panel in range(2)
    ]
    tops_index = [jnp.arange(panel * PW, panel * PW + PW, dtype=jnp.int32) for panel in range(2)]
    work = block
    lowers = lax.all_gather(panels, "col", axis=2, tiled=True)
    for panel in range(2):
        offset = panel * PW
        diag_rows = pick_rows(lowers[panel], identity_perm, tops_index[panel], start)
        picked = pick_rows(work, perms[panel], targets[panel], start)
        moved, diag_all = lax.psum((picked, diag_rows), "row")
        work = place_rows(work, targets[panel], moved, start)
        upper = solve_top(diag_all, moved[:PW])
        work = finish(work, lowers[panel], offset, start, upper)
    return work

MESH = pl.DeviceIdType.MESH
F32, BF16 = jnp.float32, jnp.bfloat16
SMALL = 32
DIAG, ONE, ZERO, TOP = range(4)


def dot(a, b):
    return jnp.dot(a, b, preferred_element_type=F32)


def split(a):
    high = a.astype(BF16)
    return high, (a - high.astype(F32)).astype(BF16)


def dot_split(a, b):
    m = a[0].shape[0]
    both = dot(jnp.concatenate(a, 0), b[0])
    return both[:m] + (both[m:] + dot(a[0], b[1]))


def three(parts_ref, a):
    m = a.shape[0]
    high = a.astype(BF16)
    rest = a - high.astype(F32)
    mid = rest.astype(BF16)
    parts_ref[0:m] = high
    parts_ref[m : 2 * m] = mid
    parts_ref[2 * m : 3 * m] = (rest - mid.astype(F32)).astype(BF16)


def pick(parts_ref, one_hot):
    out = dot(parts_ref[...], one_hot.astype(BF16))
    m = out.shape[0] // 3
    return out[:m] + (out[m : 2 * m] + out[2 * m :])


def iota(shape, dim):
    return lax.broadcasted_iota(jnp.int32, shape, dim)


def one_hot(condition):
    return jnp.where(condition, 1.0, 0.0)


def kernel(
    n_row, n_col, piv_hbm, block_hbm, panels_hbm, out_ref,
    piv_ref, block_ref, panels_ref, block_t, load_sem,
    g, g_top, own_ref, f_in, f_out, l_in, l_out, power_ref, small_ref, inverse_ref,
    own_top_ref, parts, parts_one, put_parts_one, index,
    d_sem, l_sem, f_sem, peer_send, peer_recv, sib_send, sib_recv,
):
    r, c = lax.axis_index("row"), lax.axis_index("col")
    loads = [
        pltpu.make_async_copy(src, dst, load_sem.at[i])
        for i, (src, dst) in enumerate(
            ((piv_hbm, piv_ref), (panels_hbm, panels_ref), (block_hbm, block_ref))
        )
    ]
    for load in loads:
        load.start()
    rows, cols = block_ref.shape
    tops = 2 * PW
    kc = panels_ref.shape[1]
    n_peer = n_col // 2
    chunks = cols // kc
    last = n_row - 1
    sibling = c + 1 - 2 * (c % 2)
    is_first, is_last = r == 0, r == last
    is_middle = (r > 0) & (r < last)
    is_upper = 2 * r >= n_row
    start = r * rows

    barrier = pltpu.get_barrier_semaphore()

    @pl.when(r > 0)
    def _():
        pl.semaphore_signal(barrier, 1, device_id={"row": r - 1}, device_id_type=MESH)

    @pl.when(r < last)
    def _():
        pl.semaphore_signal(barrier, 1, device_id={"row": r + 1}, device_id_type=MESH)

    for m in range(1, n_peer):
        pl.semaphore_signal(barrier, 1, device_id={"col": (c + 2 * m) % n_col}, device_id_type=MESH)
    pl.semaphore_signal(barrier, 1, device_id={"col": sibling}, device_id_type=MESH)

    loads[0].wait()
    first = piv_ref[0:1, :].astype(F32)
    second = piv_ref[1:2, :].astype(F32)
    sub, lane = iota((PW, PW), 0).astype(F32), iota((PW, PW), 1).astype(F32)

    def upright(v):
        return jnp.sum(jnp.where(sub == lane, v, 0.0), axis=1, keepdims=True)

    first_c, second_c = upright(first), upright(second)
    lane_row = lane[0:1, :]
    sub_col = sub[:, 0:1]

    def lookup(match, found, otherwise, axis):
        hit = jnp.sum(one_hot(match), axis=axis, keepdims=True)
        return jnp.sum(jnp.where(match, found, 0.0), axis=axis, keepdims=True) + jnp.where(hit > 0.5, 0.0, otherwise)

    q_second = lookup(first_c == second, sub, second, 0)
    q_second_c = lookup(second_c == first, lane, second_c, 1)
    home = lookup(first_c == lane + PW, sub, lane_row + PW, 0)
    home_c = lookup(first == sub + PW, lane, sub_col + PW, 1)
    out_first = jnp.where(first < tops, first, lookup(second_c == first, home_c, lane_row, 0))
    out_second = jnp.where(q_second < tops, q_second, home)
    q = jnp.concatenate([first, q_second], 1)
    q_c = jnp.concatenate([first_c, q_second_c], 0)
    outward = jnp.concatenate([out_first, out_second], 1)

    start_f = start.astype(F32)
    local = jnp.where(is_first, outward, q - start_f)
    local_one = jnp.where(is_first, lane_row + PW, second - start_f)

    def from_here(v):
        return (v >= start_f) & (v < start_f + rows)

    loads[1].wait()
    loads[2].wait()
    index[0:1, 0:tops] = local
    index[0:1, tops : tops + PW] = local_one
    for n in range(rows // 128):
        block_t[:, n * 128 : (n + 1) * 128] = block_ref[n * 128 : (n + 1) * 128, :].T
    three(parts, block_t[...])
    three(parts_one, panels_ref[0])

    def take(n, carry):
        at = pl.ds(pl.multiple_of(n * 128, 128), 128)
        picked = pick(parts, one_hot(iota((rows, 128), 0).astype(F32) == index[0:1, at]))
        own_ref[:, at] = picked
        f_out[0, :, at] = picked
        f_out[1, :, at] = picked
        return carry

    def take_one(n, carry):
        at = pl.ds(pl.multiple_of(n * 128, 128), 128)
        here = pl.ds(pl.multiple_of(tops + n * 128, 128), 128)
        picked = pick(parts_one, one_hot(iota((rows, 128), 0).astype(F32) == index[0:1, here]))
        own_top_ref[:, at] = picked
        l_out[0, :, at] = picked
        l_out[1, :, at] = picked
        return carry

    lax.fori_loop(0, PW // 128, take_one, 0)
    lax.fori_loop(0, tops // 128, take, 0)

    @pl.when(is_first)
    def _():
        g[DIAG, c] = jnp.concatenate([panels_ref[0, :, :PW], panels_ref[1, :, PW:tops]], 1)

    @pl.when(r > 0)
    def _():
        g[ONE, c] = panels_ref[1]

    @pl.when(is_middle)
    def _():
        pl.semaphore_wait(barrier, n_peer + 2)

    @pl.when(is_first | is_last)
    def _():
        pl.semaphore_wait(barrier, n_peer + 1)

    def l_copy(d):
        return pltpu.make_async_remote_copy(
            src_ref=l_out.at[d], dst_ref=l_in.at[d], send_sem=l_sem.at[0, d], recv_sem=l_sem.at[1, d],
            device_id={"row": r + 1 - 2 * d}, device_id_type=MESH,
        )

    def f_copy(k, d):
        at = pl.ds(pl.multiple_of(k * kc, 8), kc)
        return pltpu.make_async_remote_copy(
            src_ref=f_out.at[d, at], dst_ref=f_in.at[d, at],
            send_sem=f_sem.at[0, d, k], recv_sem=f_sem.at[1, d, k],
            device_id={"row": r + 1 - 2 * d}, device_id_type=MESH,
        )

    diag_copy = pltpu.make_async_remote_copy(
        src_ref=g.at[DIAG, c], dst_ref=g.at[DIAG, c], send_sem=d_sem.at[0], recv_sem=d_sem.at[1],
        device_id={"row": r + 1}, device_id_type=MESH,
    )

    def arrives(d):
        return jnp.where(d == 0, r > 0, r < last)

    def l_step(d):
        @pl.when(arrives(d))
        def _():
            l_copy(d).wait_recv()

        @pl.when(is_middle)
        def _():
            l_out[d] = jnp.where(from_here(second), l_out[d], l_in[d])
            l_copy(d).start()

    def f_step(k, d):
        @pl.when(arrives(d))
        def _():
            f_copy(k, d).wait_recv()

        @pl.when(is_middle)
        def _():
            at = pl.ds(pl.multiple_of(k * kc, 8), kc)
            f_out[d, at, :] = jnp.where(from_here(q), f_out[d, at, :], f_in[d, at, :])
            f_copy(k, d).start()

    def slot_ref(kind, slot):
        return g_top.at[slot] if kind == TOP else g.at[kind, slot]

    def peer_copy(kind, m, slot):
        return pltpu.make_async_remote_copy(
            src_ref=slot_ref(kind, slot), dst_ref=slot_ref(kind, slot),
            send_sem=peer_send.at[kind, m], recv_sem=peer_recv.at[kind, m],
            device_id={"col": (c + 2 * m) % n_col}, device_id_type=MESH,
        )

    def sib_copy(kind, m, slot):
        return pltpu.make_async_remote_copy(
            src_ref=slot_ref(kind, slot), dst_ref=slot_ref(kind, slot),
            send_sem=sib_send.at[kind, m], recv_sem=sib_recv.at[kind, m],
            device_id={"col": sibling}, device_id_type=MESH,
        )

    def spread(kind):
        for m in range(1, n_peer):
            peer_copy(kind, m, c).start()
        sib_copy(kind, 0, c).start()

    def share(kind):
        for m in range(1, n_peer):
            slot = (c + n_col - 2 * m) % n_col
            peer_copy(kind, m, slot).wait_recv()
            sib_copy(kind, m, slot).start()

    def settle(kind):
        for m in range(n_peer):
            sib_copy(kind, m, (sibling + n_col - 2 * m) % n_col).wait_recv()

    def drain(kind):
        for m in range(1, n_peer):
            peer_copy(kind, m, c).wait_send()
        for m in range(n_peer):
            sib_copy(kind, m, c).wait_send()

    @pl.when(is_first)
    def _():
        diag_copy.start()
        spread(DIAG)
        l_copy(0).start()
        for k in range(chunks):
            f_copy(k, 0).start()

    @pl.when(is_last)
    def _():
        l_copy(1).start()
        for k in range(chunks):
            f_copy(k, 1).start()

    @pl.when(is_upper)
    def _():
        l_step(1)

    @pl.when(r > 0)
    def _():
        diag_copy.wait_recv()

        @pl.when(r < last)
        def _():
            diag_copy.start()

        spread(DIAG)

    l_step(0)

    @pl.when(jnp.logical_not(is_upper))
    def _():
        l_step(1)

    top_rows = jnp.where(second < start_f, l_in[0], jnp.where(from_here(second), own_top_ref[...], l_in[1]))
    g_top[c] = top_rows
    spread(TOP)

    @pl.when(r > 0)
    def _():
        three(put_parts_one, l_in[0])

        def put_one(n, carry):
            at = pl.ds(pl.multiple_of(n * 128, 128), 128)
            put = one_hot((iota((PW, 128), 1) + n * 128).astype(F32) == second_c - start_f)
            moved = jnp.sum(put, axis=0, keepdims=True) > 0.5
            g[ZERO, c, :, at] = jnp.where(moved, pick(put_parts_one, put), panels_ref[0, :, at])
            return carry

        lax.fori_loop(0, rows // 128, put_one, 0)
        spread(ZERO)
        spread(ONE)

    def strict(p):
        upper = g[DIAG, :, :, pl.ds(pl.multiple_of(p * PW, 128), PW)].reshape(PW, PW)
        return jnp.where(iota((PW, PW), 0) < iota((PW, PW), 1), upper, 0.0)

    def spaced(small):
        same = iota((PW, PW), 0) // SMALL == iota((PW, PW), 1) // SMALL
        return jnp.where(same, jnp.concatenate([small] * (PW // SMALL), 0), 0.0)

    def begin():
        share(DIAG)
        settle(DIAG)
        lanes = iota((SMALL, PW), 1)
        def one(p, carry):
            whole = strict(p)
            small = jnp.zeros((SMALL, PW), F32)
            for b in range(PW // SMALL):
                small += jnp.where(lanes // SMALL == b, whole[b * SMALL : (b + 1) * SMALL], 0.0)
            small_ref[p] = one_hot(lanes % SMALL == iota((SMALL, PW), 0)) - small
            power_ref[p] = dot_split(split(small), split(spaced(small)))
            return carry

        lax.fori_loop(0, 2, one, 0)

    def double(_, carry):
        def one(p, carry):
            power, small = power_ref[p], small_ref[p]
            new = dot_split(split(jnp.concatenate([power, small], 0)), split(spaced(power)))
            power_ref[p] = new[:SMALL]
            small_ref[p] = small + new[SMALL:]
            return carry

        return lax.fori_loop(0, 2, one, carry)

    def widen():
        for p in range(2):
            inverse_ref[p] = spaced(small_ref[p])

    def merge(level):
        shift = SMALL.bit_length() - 1 + level
        row, col = iota((PW, PW), 0), iota((PW, PW), 1)
        pair = ((row >> (shift + 1)) == (col >> (shift + 1))) & ((row >> shift) != (col >> shift))
        def one(p, carry):
            inverse = inverse_ref[p]
            parts = split(inverse)
            right = dot_split(split(jnp.where(pair, strict(p), 0.0)), parts)
            inverse_ref[p] = inverse - dot_split(parts, split(right))
            return carry

        lax.fori_loop(0, 2, one, 0)

    doublings = SMALL.bit_length() - 2
    merges = (PW // SMALL).bit_length() - 1

    def turn(k, carry):
        @pl.when(k < chunks)
        def _():
            upper = jnp.where(is_upper, 1, 0)
            f_step(k, upper)
            f_step(k, 1 - upper)

        @pl.when(k == 0)
        def _():
            begin()

        @pl.when(k == 1)
        def _():
            share(TOP)

        @pl.when((k == 2) & (r > 0))
        def _():
            share(ZERO)

        @pl.when((k == 3) & (r > 0))
        def _():
            share(ONE)

        @pl.when(k < 2)
        def _():
            lax.fori_loop(0, doublings // 2, double, 0)

        @pl.when(k == 2)
        def _():
            widen()

        @pl.when(k >= 2)
        def _():
            merge(k - 2)

        return carry

    lax.fori_loop(0, 2 + merges, turn, 0)
    settle(TOP)

    top = jnp.where(q < start_f, f_in[0], jnp.where(from_here(q), own_ref[...], f_in[1]))
    upper0_full = dot_split(split(top[:, :PW]), split(inverse_ref[0]))
    upper0 = split(upper0_full)
    rest = top[:, PW:] - dot_split(upper0, split(g_top[...].reshape(PW, PW)))
    upper1_full = dot_split(split(rest), split(inverse_ref[1]))

    @pl.when(is_first)
    def _():
        out_ref[...] = jnp.concatenate([upper0_full, upper1_full], 1).T

    @pl.when(r > 0)
    def _():
        settle(ZERO)
        settle(ONE)
        three(parts, f_in[0])
        both = jnp.concatenate([upper0_full, upper1_full], 1)
        left = split(both)

        def finish_rows(n, carry):
            at = pl.ds(pl.multiple_of(n * 128, 128), 128)
            put = one_hot((iota((tops, 128), 1) + n * 128).astype(F32) == q_c - start_f)
            moved = jnp.sum(put, axis=0, keepdims=True) > 0.5
            work = jnp.where(moved, pick(parts, put), block_t[:, at])
            lower = jnp.concatenate([g[ZERO, :, :, at].reshape(PW, 128), g[ONE, :, :, at].reshape(PW, 128)], 0)
            out_ref[at, :] = (work - dot_split(left, split(lower))).T
            return carry

        lax.fori_loop(0, rows // 128, finish_rows, 0)
        drain(ZERO)
        drain(ONE)

    drain(DIAG)
    drain(TOP)

    @pl.when(r < last)
    def _():
        diag_copy.wait_send()

    for d in range(2):
        @pl.when((r < last) if d == 0 else (r > 0))
        def _():
            l_copy(d).wait_send()
            for k in range(chunks):
                f_copy(k, d).wait_send()


def fused(block, panels, pivots):
    n_row, n_col = lax.axis_size("row"), lax.axis_size("col")
    rows, cols = block.shape
    kc = panels.shape[2]
    tops = 2 * PW
    vmem = pl.BlockSpec(memory_space=pltpu.VMEM)
    n_peer = n_col // 2
    dma = pltpu.SemaphoreType.DMA
    return pl.pallas_call(
        functools.partial(kernel, n_row, n_col),
        out_shape=jax.ShapeDtypeStruct((rows, cols), F32),
        in_specs=[pl.BlockSpec(memory_space=pl.ANY)] * 3,
        out_specs=vmem,
        scratch_shapes=[
            pltpu.VMEM(pivots.shape, jnp.int32),
            pltpu.VMEM((rows, cols), F32),
            pltpu.VMEM((2, kc, rows), F32),
            pltpu.VMEM((cols, rows), F32),
            dma((3,)),
            pltpu.VMEM((3, n_col, kc, rows), F32),
            pltpu.VMEM((n_col, kc, PW), F32),
            pltpu.VMEM((cols, tops), F32),
            pltpu.VMEM((2, cols, tops), F32),
            pltpu.VMEM((2, cols, tops), F32),
            pltpu.VMEM((2, kc, PW), F32),
            pltpu.VMEM((2, kc, PW), F32),
            pltpu.VMEM((2, SMALL, PW), F32),
            pltpu.VMEM((2, SMALL, PW), F32),
            pltpu.VMEM((2, PW, PW), F32),
            pltpu.VMEM((kc, PW), F32),
            pltpu.VMEM((3 * cols, tops), BF16),
            pltpu.VMEM((3 * kc, rows), BF16),
            pltpu.VMEM((3 * kc, PW), BF16),
            pltpu.VMEM((8, tops + PW), F32),
            dma((2,)),
            dma((2, 2)),
            dma((2, 2, cols // kc)),
        ]
        + [dma((4, n_peer))] * 4,
        compiler_params=pltpu.CompilerParams(
            collective_id=0, has_side_effects=True, vmem_limit_bytes=60 * 1024 * 1024
        ),
    )(pivots, block, jnp.swapaxes(panels, 1, 2))


def body(block, panels, pivots):
    kc = panels.shape[2]
    fits = (
        block.shape[0] == 2 * PW
        and block.shape[1] % 128 == 0
        and kc % 8 == 0
        and block.shape[1] // kc in range(1, 6)
        and block.shape[1] % kc == 0
        and lax.axis_size("col") % 2 == 0
        and lax.axis_size("row") > 1
    )
    return fused(block, panels, pivots) if fits else plain(block, panels, pivots)


def solution(mesh):
    return jax.shard_map(
        body,
        mesh=mesh,
        in_specs=(P("row", "col"), P(None, "row", "col"), P()),
        out_specs=P("row", "col"),
        check_vma=False,
    )
```

```python
import functools

import jax
import jax.numpy as jnp
from jax import lax
from jax.experimental import pallas as pl
from jax.experimental.pallas import tpu as pltpu
from jax.sharding import PartitionSpec as P

PW = 256


def swap_order(piv_row, offset, count):
    own = offset + jnp.arange(piv_row.shape[0], dtype=jnp.int32)
    base = jnp.arange(count, dtype=jnp.int32)
    return base.at[own].set(piv_row).at[piv_row].set(own)


def pick_rows(data, perm, targets, start):
    local_src = perm[targets] - start
    owned = (local_src >= 0) & (local_src < data.shape[0])
    taken = jnp.take(data, jnp.clip(local_src, 0, data.shape[0] - 1), axis=0)
    return jnp.where(owned[:, None], taken, 0.0)


def place_rows(data, targets, values, start):
    local_dst = targets - start
    inside = (local_dst >= 0) & (local_dst < data.shape[0])
    where_to = jnp.where(inside, local_dst, data.shape[0])
    return data.at[where_to].set(values, mode="drop")


def solve_top(diag_rows, rows):
    strict = jnp.tril(diag_rows, -1)
    inverse = jnp.eye(PW, dtype=jnp.float32) - strict
    power = strict
    for level in range(1, PW.bit_length() - 1):
        power = jnp.dot(
            power, power, precision=lax.Precision.HIGHEST, preferred_element_type=jnp.float32
        )
        inverse = inverse + jnp.dot(
            inverse, power, precision=lax.Precision.HIGHEST, preferred_element_type=jnp.float32
        )
    return jnp.dot(
        inverse, rows, precision=lax.Precision.HIGHEST, preferred_element_type=jnp.float32
    )


def finish(work, lower, offset, start, upper):
    product = jnp.dot(
        lower, upper, precision=lax.Precision.HIGHEST, preferred_element_type=jnp.float32
    )
    global_rows = start + jnp.arange(work.shape[0], dtype=jnp.int32)
    work = jnp.where((global_rows >= offset + PW)[:, None], work - product, work)
    placed = work.at[offset : offset + PW].set(upper)
    in_top = (global_rows >= offset) & (global_rows < offset + PW)
    return jnp.where(in_top[:, None], placed, work)


def plain(block, panels, pivots):
    rows_here = block.shape[0]
    rows_all = rows_here * lax.axis_size("row")
    start = lax.axis_index("row") * rows_here
    identity_perm = jnp.arange(rows_all, dtype=jnp.int32)
    perms = [swap_order(pivots[panel], panel * PW, rows_all) for panel in range(2)]
    targets = [
        jnp.concatenate([jnp.arange(panel * PW, panel * PW + PW, dtype=jnp.int32), pivots[panel]])
        for panel in range(2)
    ]
    tops_index = [jnp.arange(panel * PW, panel * PW + PW, dtype=jnp.int32) for panel in range(2)]
    work = block
    lowers = lax.all_gather(panels, "col", axis=2, tiled=True)
    for panel in range(2):
        offset = panel * PW
        diag_rows = pick_rows(lowers[panel], identity_perm, tops_index[panel], start)
        picked = pick_rows(work, perms[panel], targets[panel], start)
        moved, diag_all = lax.psum((picked, diag_rows), "row")
        work = place_rows(work, targets[panel], moved, start)
        upper = solve_top(diag_all, moved[:PW])
        work = finish(work, lowers[panel], offset, start, upper)
    return work

MESH = pl.DeviceIdType.MESH
F32, BF16 = jnp.float32, jnp.bfloat16
SMALL = 32
ONE, ZERO, TOP, DIAG = range(4)


def dot(a, b):
    return jnp.dot(a, b, preferred_element_type=F32)


def split(a):
    high = a.astype(BF16)
    return high, (a - high.astype(F32)).astype(BF16)


def dot_split(a, b):
    m = a[0].shape[0]
    both = dot(jnp.concatenate(a, 0), b[0])
    return both[:m] + (both[m:] + dot(a[0], b[1]))


def dot_pick(a, one_hot):
    m = a.shape[0]
    high = a.astype(BF16)
    rest = a - high.astype(F32)
    mid = rest.astype(BF16)
    low = (rest - mid.astype(F32)).astype(BF16)
    out = dot(jnp.concatenate([high, mid, low], 0), one_hot)
    return out[:m] + (out[m : 2 * m] + out[2 * m :])


def iota(shape, dim):
    return lax.broadcasted_iota(jnp.int32, shape, dim)


def one_hot(condition):
    return jnp.where(condition, 1.0, 0.0)


def kernel(
    n_row, n_col, piv_ref, block_ref, panels_ref, out_ref, d_from, g_diag,
    g, g_top, own_ref, f_in, f_out, l_in, l_out, inverse_ref,
    d_sem, i_sem, l_sem, f_sem, peer_send, peer_recv, sib_send, sib_recv,
):
    r, c = lax.axis_index("row"), lax.axis_index("col")
    rows, cols = block_ref.shape
    tops = 2 * PW
    kc = panels_ref.shape[1]
    n_peer = n_col // 2
    chunks = cols // kc
    last = n_row - 1
    p = c % 2
    sibling = c + 1 - 2 * p
    is_first, is_last = r == 0, r == last
    is_middle = (r > 0) & (r < last)
    is_upper = 2 * r >= n_row
    start = r * rows

    barrier = pltpu.get_barrier_semaphore()

    @pl.when(r > 0)
    def _():
        pl.semaphore_signal(barrier, 1, device_id={"row": r - 1}, device_id_type=MESH)

    @pl.when(r < last)
    def _():
        pl.semaphore_signal(barrier, 1, device_id={"row": r + 1}, device_id_type=MESH)

    for m in range(1, n_col):
        pl.semaphore_signal(barrier, 1, device_id={"col": (c + m) % n_col}, device_id_type=MESH)

    first = piv_ref[0:1, :].astype(F32)
    second = piv_ref[1:2, :].astype(F32)
    sub, lane = iota((PW, PW), 0).astype(F32), iota((PW, PW), 1).astype(F32)

    def upright(v):
        return jnp.sum(jnp.where(sub == lane, v, 0.0), axis=1, keepdims=True)

    first_c, second_c = upright(first), upright(second)
    lane_row = lane[0:1, :]
    sub_col = sub[:, 0:1]

    def lookup(match, found, otherwise, axis):
        hit = jnp.sum(one_hot(match), axis=axis, keepdims=True)
        return jnp.sum(jnp.where(match, found, 0.0), axis=axis, keepdims=True) + jnp.where(hit > 0.5, 0.0, otherwise)

    q_second = lookup(first_c == second, sub, second, 0)
    q_second_c = lookup(second_c == first, lane, second_c, 1)
    home = lookup(first_c == lane + PW, sub, lane_row + PW, 0)
    home_c = lookup(first == sub + PW, lane, sub_col + PW, 1)
    out_first = jnp.where(first < tops, first, lookup(second_c == first, home_c, lane_row, 0))
    out_second = jnp.where(q_second < tops, q_second, home)
    q = jnp.concatenate([first, q_second], 1)
    q_c = jnp.concatenate([first_c, q_second_c], 0)
    outward = jnp.concatenate([out_first, out_second], 1)

    start_f = start.astype(F32)
    local = jnp.where(is_first, outward, q - start_f)
    local_one = jnp.where(is_first, lane_row + PW, second - start_f)

    def from_here(v):
        return (v >= start_f) & (v < start_f + rows)

    own_top = dot_pick(panels_ref[0], one_hot(iota((rows, PW), 0).astype(F32) == local_one).astype(BF16))
    l_out[0] = own_top
    l_out[1] = own_top
    block_t = block_ref[...].T
    own = dot_pick(block_t, one_hot(iota((rows, tops), 0).astype(F32) == local).astype(BF16))
    own_ref[...] = own
    f_out[0] = own
    f_out[1] = own

    @pl.when(is_first)
    def _():
        d_from[0] = panels_ref[0, :, :PW]
        d_from[1] = panels_ref[1, :, PW:tops]

    @pl.when(r > 0)
    def _():
        g[ONE, c] = panels_ref[1]

    @pl.when(is_middle)
    def _():
        pl.semaphore_wait(barrier, n_col + 1)

    @pl.when(is_first | is_last)
    def _():
        pl.semaphore_wait(barrier, n_col)

    def l_copy(d):
        return pltpu.make_async_remote_copy(
            src_ref=l_out.at[d], dst_ref=l_in.at[d], send_sem=l_sem.at[0, d], recv_sem=l_sem.at[1, d],
            device_id={"row": r + 1 - 2 * d}, device_id_type=MESH,
        )

    def f_copy(k, d):
        at = pl.ds(k * kc, kc)
        return pltpu.make_async_remote_copy(
            src_ref=f_out.at[d, at], dst_ref=f_in.at[d, at],
            send_sem=f_sem.at[0, d, k], recv_sem=f_sem.at[1, d, k],
            device_id={"row": r + 1 - 2 * d}, device_id_type=MESH,
        )

    diag_copy = pltpu.make_async_remote_copy(
        src_ref=d_from, dst_ref=d_from, send_sem=d_sem.at[0], recv_sem=d_sem.at[1],
        device_id={"row": r + 1}, device_id_type=MESH,
    )

    def arrives(d):
        return jnp.where(d == 0, r > 0, r < last)

    def l_step(d):
        @pl.when(arrives(d))
        def _():
            l_copy(d).wait_recv()

        @pl.when(is_middle)
        def _():
            l_out[d] = jnp.where(from_here(second), l_out[d], l_in[d])
            l_copy(d).start()

    def f_step(k, d):
        at = pl.ds(k * kc, kc)
        f_copy(k, d).wait_recv()
        f_out[d, at, :] = jnp.where(from_here(q), f_out[d, at, :], f_in[d, at, :])
        f_copy(k, d).start()

    def f_both(k):
        if k < chunks:
            @pl.when(is_middle)
            def _():
                upper = jnp.where(is_upper, 1, 0)
                f_step(k, upper)
                f_step(k, 1 - upper)

    def slot_ref(kind, slot):
        return g_top.at[slot] if kind == TOP else g.at[kind, slot]

    def peer_copy(kind, m, slot):
        return pltpu.make_async_remote_copy(
            src_ref=slot_ref(kind, slot), dst_ref=slot_ref(kind, slot),
            send_sem=peer_send.at[kind, m], recv_sem=peer_recv.at[kind, m],
            device_id={"col": (c + 2 * m) % n_col}, device_id_type=MESH,
        )

    def sib_copy(kind, m, slot):
        return pltpu.make_async_remote_copy(
            src_ref=slot_ref(kind, slot), dst_ref=slot_ref(kind, slot),
            send_sem=sib_send.at[kind, m], recv_sem=sib_recv.at[kind, m],
            device_id={"col": sibling}, device_id_type=MESH,
        )

    def spread(kind):
        for m in range(1, n_peer):
            peer_copy(kind, m, c).start()
        sib_copy(kind, 0, c).start()

    def diag_peer(m):
        return pltpu.make_async_remote_copy(
            src_ref=d_from.at[p], dst_ref=g_diag.at[c],
            send_sem=peer_send.at[DIAG, m], recv_sem=peer_recv.at[DIAG, m],
            device_id={"col": (c + 2 * m) % n_col}, device_id_type=MESH,
        )

    def diag_cross(m):
        return pltpu.make_async_remote_copy(
            src_ref=d_from.at[1 - p], dst_ref=g_diag.at[c],
            send_sem=sib_send.at[DIAG, m], recv_sem=sib_recv.at[DIAG, m],
            device_id={"col": (sibling + 2 * m) % n_col}, device_id_type=MESH,
        )

    def spread_diag():
        for m in range(n_peer - 1, 0, -1):
            diag_peer(m).start()
            diag_cross(m).start()
        diag_cross(0).start()
        g_diag[c] = d_from[p]

    inverse_copy = pltpu.make_async_remote_copy(
        src_ref=inverse_ref.at[p], dst_ref=inverse_ref.at[p], send_sem=i_sem.at[0], recv_sem=i_sem.at[1],
        device_id={"col": sibling}, device_id_type=MESH,
    )

    def share(kind):
        for m in range(1, n_peer):
            slot = (c + n_col - 2 * m) % n_col
            peer_copy(kind, m, slot).wait_recv()
            sib_copy(kind, m, slot).start()

    def settle(kind):
        for m in range(n_peer):
            sib_copy(kind, m, (sibling + n_col - 2 * m) % n_col).wait_recv()

    def drain(kind):
        for m in range(1, n_peer):
            peer_copy(kind, m, c).wait_send()
        for m in range(n_peer):
            sib_copy(kind, m, c).wait_send()

    @pl.when(is_first)
    def _():
        diag_copy.start()
        spread_diag()
        l_copy(0).start()
        for k in range(chunks):
            f_copy(k, 0).start()

    @pl.when(is_last)
    def _():
        l_copy(1).start()
        for k in range(chunks):
            f_copy(k, 1).start()

    @pl.when(is_upper)
    def _():
        l_step(1)

    @pl.when(r > 0)
    def _():
        diag_copy.wait_recv()

        @pl.when(r < last)
        def _():
            diag_copy.start()

        spread_diag()

    l_step(0)

    @pl.when(jnp.logical_not(is_upper))
    def _():
        l_step(1)

    top_rows = jnp.where(second < start_f, l_in[0], jnp.where(from_here(second), own_top, l_in[1]))
    g_top[c] = top_rows
    spread(TOP)
    f_both(0)

    @pl.when(r > 0)
    def _():
        put = one_hot(iota((PW, rows), 1).astype(F32) == second_c - start_f)
        moved = jnp.sum(put, axis=0, keepdims=True) > 0.5
        g[ZERO, c] = jnp.where(moved, dot_pick(l_in[0], put.astype(BF16)), panels_ref[0])
        spread(ZERO)
        spread(ONE)

    f_both(1)

    for m in range(n_peer):
        diag_cross(m).wait_recv()
        if m:
            diag_peer(m).wait_recv()
    whole = jnp.where(iota((PW, PW), 0) < iota((PW, PW), 1), g_diag[...].reshape(PW, PW), 0.0)
    lanes = iota((SMALL, PW), 1)
    small = jnp.zeros((SMALL, PW), F32)
    for b in range(PW // SMALL):
        small += jnp.where(lanes // SMALL == b, whole[b * SMALL : (b + 1) * SMALL], 0.0)

    def spaced(small):
        same = iota((PW, PW), 0) // SMALL == iota((PW, PW), 1) // SMALL
        return split(jnp.where(same, jnp.concatenate([small] * (PW // SMALL), 0), 0.0))

    power = dot_split(split(small), spaced(small))
    small = one_hot(lanes % SMALL == iota((SMALL, PW), 0)) - small
    span = 2
    while span < SMALL:
        last_one = 2 * span >= SMALL
        new = dot_split(split(small if last_one else jnp.concatenate([small, power], 0)), spaced(power))
        small = small + new[:SMALL]
        power = new[SMALL:]
        span *= 2
        if span == 8:
            f_both(2)
    f_both(3)
    for k in range(4, chunks):
        f_both(k)
    share(TOP)

    same = iota((PW, PW), 0) // SMALL == iota((PW, PW), 1) // SMALL
    inverse = jnp.where(same, jnp.concatenate([small] * (PW // SMALL), 0), 0.0)
    size = SMALL
    while size < PW:
        pairs = PW // (2 * size)
        pair_lanes = iota((size, PW), 1) // (2 * size)

        def fold(a):
            return sum(a[2 * size * i : 2 * size * i + size] for i in range(pairs))

        def unfold(a):
            empty = jnp.zeros((size, PW), F32)
            return jnp.concatenate([x for i in range(pairs) for x in (jnp.where(pair_lanes == i, a, 0.0), empty)], 0)

        other = (iota((size, PW), 1) // size) % 2 == 1
        beside = sum(
            jnp.where(other & (pair_lanes == i), whole[2 * size * i : 2 * size * i + size], 0.0) for i in range(pairs)
        )
        right = dot_split(split(beside), split(inverse))
        inverse = inverse - unfold(dot_split(split(fold(inverse)), split(unfold(right))))
        size *= 2
    inverse_ref[p] = inverse
    inverse_copy.start()

    @pl.when(r > 0)
    def _():
        share(ZERO)
        share(ONE)

    @pl.when(is_first)
    def _():
        for k in range(chunks):
            f_copy(k, 1).wait_recv()

    @pl.when(is_last)
    def _():
        for k in range(chunks):
            f_copy(k, 0).wait_recv()

    settle(TOP)
    inverse_copy.wait_recv()

    top = jnp.where(q < start_f, f_in[0], jnp.where(from_here(q), own_ref[...], f_in[1]))
    upper0_full = dot_split(split(top[:, :PW]), split(inverse_ref[0]))
    upper0 = split(upper0_full)
    rest = top[:, PW:] - dot_split(upper0, split(g_top[...].reshape(PW, PW)))
    upper1_full = dot_split(split(rest), split(inverse_ref[1]))

    @pl.when(is_first)
    def _():
        out_ref[...] = jnp.concatenate([upper0_full, upper1_full], 1).T

    @pl.when(r > 0)
    def _():
        settle(ZERO)
        settle(ONE)
        put = one_hot(iota((tops, rows), 1).astype(F32) == q_c - start_f)
        moved = jnp.sum(put, axis=0, keepdims=True) > 0.5
        work = jnp.where(moved, dot_pick(f_in[0], put.astype(BF16)), block_ref[...].T)
        work = work - dot_split(upper0, split(g[ZERO].reshape(PW, rows)))
        work = work - dot_split(split(upper1_full), split(g[ONE].reshape(PW, rows)))
        out_ref[...] = work.T
        drain(ZERO)
        drain(ONE)

    for m in range(n_peer):
        diag_cross(m).wait_send()
        if m:
            diag_peer(m).wait_send()
    inverse_copy.wait_send()
    drain(TOP)

    @pl.when(r < last)
    def _():
        diag_copy.wait_send()

    for d in range(2):
        @pl.when((r < last) if d == 0 else (r > 0))
        def _():
            l_copy(d).wait_send()
            for k in range(chunks):
                f_copy(k, d).wait_send()


def fused(block, panels, pivots):
    n_row, n_col = lax.axis_size("row"), lax.axis_size("col")
    rows, cols = block.shape
    kc = panels.shape[2]
    tops = 2 * PW
    vmem = pl.BlockSpec(memory_space=pltpu.VMEM)
    n_peer = n_col // 2
    dma = pltpu.SemaphoreType.DMA
    return pl.pallas_call(
        functools.partial(kernel, n_row, n_col),
        out_shape=jax.ShapeDtypeStruct((rows, cols), F32),
        in_specs=[vmem] * 3,
        out_specs=vmem,
        scratch_shapes=[
            pltpu.VMEM((2, kc, PW), F32),
            pltpu.VMEM((n_col, kc, PW), F32),
            pltpu.VMEM((2, n_col, kc, rows), F32),
            pltpu.VMEM((n_col, kc, PW), F32),
            pltpu.VMEM((cols, tops), F32),
            pltpu.VMEM((2, cols, tops), F32),
            pltpu.VMEM((2, cols, tops), F32),
            pltpu.VMEM((2, kc, PW), F32),
            pltpu.VMEM((2, kc, PW), F32),
            pltpu.VMEM((2, PW, PW), F32),
            dma((2,)),
            dma((2,)),
            dma((2, 2)),
            dma((2, 2, cols // kc)),
        ]
        + [dma((4, n_peer))] * 4,
        compiler_params=pltpu.CompilerParams(
            collective_id=0, has_side_effects=True, vmem_limit_bytes=48 * 1024 * 1024
        ),
    )(pivots, block, jnp.swapaxes(panels, 1, 2))


def body(block, panels, pivots):
    kc = panels.shape[2]
    fits = (
        block.shape[0] == 2 * PW
        and block.shape[1] % 128 == 0
        and kc % 8 == 0
        and block.shape[1] % kc == 0
        and lax.axis_size("col") % 2 == 0
        and lax.axis_size("row") > 1
    )
    return fused(block, panels, pivots) if fits else plain(block, panels, pivots)


def solution(mesh):
    return jax.shard_map(
        body,
        mesh=mesh,
        in_specs=(P("row", "col"), P(None, "row", "col"), P()),
        out_specs=P("row", "col"),
        check_vma=False,
    )
```

```python
import functools

import jax
import jax.numpy as jnp
from jax import lax
from jax.experimental import pallas as pl
from jax.experimental.pallas import tpu as pltpu
from jax.sharding import PartitionSpec as P

PW = 256


def swap_order(piv_row, offset, count):
    own = offset + jnp.arange(piv_row.shape[0], dtype=jnp.int32)
    base = jnp.arange(count, dtype=jnp.int32)
    return base.at[own].set(piv_row).at[piv_row].set(own)


def pick_rows(data, perm, targets, start):
    local_src = perm[targets] - start
    owned = (local_src >= 0) & (local_src < data.shape[0])
    taken = jnp.take(data, jnp.clip(local_src, 0, data.shape[0] - 1), axis=0)
    return jnp.where(owned[:, None], taken, 0.0)


def place_rows(data, targets, values, start):
    local_dst = targets - start
    inside = (local_dst >= 0) & (local_dst < data.shape[0])
    where_to = jnp.where(inside, local_dst, data.shape[0])
    return data.at[where_to].set(values, mode="drop")


def solve_top(diag_rows, rows):
    strict = jnp.tril(diag_rows, -1)
    inverse = jnp.eye(PW, dtype=jnp.float32) - strict
    power = strict
    for level in range(1, PW.bit_length() - 1):
        power = jnp.dot(
            power, power, precision=lax.Precision.HIGHEST, preferred_element_type=jnp.float32
        )
        inverse = inverse + jnp.dot(
            inverse, power, precision=lax.Precision.HIGHEST, preferred_element_type=jnp.float32
        )
    return jnp.dot(
        inverse, rows, precision=lax.Precision.HIGHEST, preferred_element_type=jnp.float32
    )


def finish(work, lower, offset, start, upper):
    product = jnp.dot(
        lower, upper, precision=lax.Precision.HIGHEST, preferred_element_type=jnp.float32
    )
    global_rows = start + jnp.arange(work.shape[0], dtype=jnp.int32)
    work = jnp.where((global_rows >= offset + PW)[:, None], work - product, work)
    placed = work.at[offset : offset + PW].set(upper)
    in_top = (global_rows >= offset) & (global_rows < offset + PW)
    return jnp.where(in_top[:, None], placed, work)


def plain(block, panels, pivots):
    rows_here = block.shape[0]
    rows_all = rows_here * lax.axis_size("row")
    start = lax.axis_index("row") * rows_here
    identity_perm = jnp.arange(rows_all, dtype=jnp.int32)
    perms = [swap_order(pivots[panel], panel * PW, rows_all) for panel in range(2)]
    targets = [
        jnp.concatenate([jnp.arange(panel * PW, panel * PW + PW, dtype=jnp.int32), pivots[panel]])
        for panel in range(2)
    ]
    tops_index = [jnp.arange(panel * PW, panel * PW + PW, dtype=jnp.int32) for panel in range(2)]
    work = block
    lowers = lax.all_gather(panels, "col", axis=2, tiled=True)
    for panel in range(2):
        offset = panel * PW
        diag_rows = pick_rows(lowers[panel], identity_perm, tops_index[panel], start)
        picked = pick_rows(work, perms[panel], targets[panel], start)
        moved, diag_all = lax.psum((picked, diag_rows), "row")
        work = place_rows(work, targets[panel], moved, start)
        upper = solve_top(diag_all, moved[:PW])
        work = finish(work, lowers[panel], offset, start, upper)
    return work

MESH = pl.DeviceIdType.MESH
F32, BF16 = jnp.float32, jnp.bfloat16
SMALL = 32
PART = 16
ONE, ZERO, TOP, DIAG = range(4)


def dot(a, b):
    return jnp.dot(a, b, preferred_element_type=F32)


def split(a):
    high = a.astype(BF16)
    return high, (a - high.astype(F32)).astype(BF16)


def dot_split(a, b):
    m = a[0].shape[0]
    both = dot(jnp.concatenate(a, 0), b[0])
    return both[:m] + (both[m:] + dot(a[0], b[1]))


def dot_pick(a, one_hot):
    m = a.shape[0]
    out = dot(jnp.concatenate(split(a), 0), one_hot)
    return out[:m] + out[m:]


def iota(shape, dim):
    return lax.broadcasted_iota(jnp.int32, shape, dim)


def one_hot(condition):
    return jnp.where(condition, 1.0, 0.0)


def kernel(
    n_row, n_col, piv_ref, block_ref, panels_ref, out_ref, d_from, g_diag,
    g, g_top, own_ref, f_in, f_out, l_in, l_out, inverse_ref,
    block_t, put_ref, moved_ref, low_high, low_low,
    d_sem, i_sem, l_sem, f_sem, peer_send, peer_recv, sib_send, sib_recv,
):
    r, c = lax.axis_index("row"), lax.axis_index("col")
    rows, cols = block_ref.shape
    tops = 2 * PW
    kc = panels_ref.shape[1]
    n_peer = n_col // 2
    chunks = cols // PART
    last = n_row - 1
    p = c % 2
    sibling = c + 1 - 2 * p
    is_first, is_last = r == 0, r == last
    is_middle = (r > 0) & (r < last)
    is_upper = 2 * r >= n_row
    start = r * rows

    barrier = pltpu.get_barrier_semaphore()

    @pl.when(r > 0)
    def _():
        pl.semaphore_signal(barrier, 1, device_id={"row": r - 1}, device_id_type=MESH)

    @pl.when(r < last)
    def _():
        pl.semaphore_signal(barrier, 1, device_id={"row": r + 1}, device_id_type=MESH)

    for m in range(1, n_col):
        pl.semaphore_signal(barrier, 1, device_id={"col": (c + m) % n_col}, device_id_type=MESH)

    first = piv_ref[0:1, :].astype(F32)
    second = piv_ref[1:2, :].astype(F32)
    sub, lane = iota((PW, PW), 0).astype(F32), iota((PW, PW), 1).astype(F32)

    def upright(v):
        return jnp.sum(jnp.where(sub == lane, v, 0.0), axis=1, keepdims=True)

    first_c, second_c = upright(first), upright(second)
    lane_row = lane[0:1, :]
    sub_col = sub[:, 0:1]

    def lookup(match, found, otherwise, axis):
        hit = jnp.sum(one_hot(match), axis=axis, keepdims=True)
        return jnp.sum(jnp.where(match, found, 0.0), axis=axis, keepdims=True) + jnp.where(hit > 0.5, 0.0, otherwise)

    q_second = lookup(first_c == second, sub, second, 0)
    q_second_c = lookup(second_c == first, lane, second_c, 1)
    home = lookup(first_c == lane + PW, sub, lane_row + PW, 0)
    home_c = lookup(first == sub + PW, lane, sub_col + PW, 1)
    out_first = jnp.where(first < tops, first, lookup(second_c == first, home_c, lane_row, 0))
    out_second = jnp.where(q_second < tops, q_second, home)
    q = jnp.concatenate([first, q_second], 1)
    q_c = jnp.concatenate([first_c, q_second_c], 0)
    outward = jnp.concatenate([out_first, out_second], 1)

    start_f = start.astype(F32)
    local = jnp.where(is_first, outward, q - start_f)
    local_one = jnp.where(is_first, lane_row + PW, second - start_f)

    def from_here(v):
        return (v >= start_f) & (v < start_f + rows)

    @pl.when(is_first)
    def _():
        d_from[0] = panels_ref[0, :, :PW]
        d_from[1] = panels_ref[1, :, PW:tops]

    @pl.when(r > 0)
    def _():
        g[ONE, c] = panels_ref[1]

    @pl.when(is_middle)
    def _():
        pl.semaphore_wait(barrier, n_col + 1)

    @pl.when(is_first | is_last)
    def _():
        pl.semaphore_wait(barrier, n_col)

    def l_copy(d):
        return pltpu.make_async_remote_copy(
            src_ref=l_out.at[d], dst_ref=l_in.at[d], send_sem=l_sem.at[0, d], recv_sem=l_sem.at[1, d],
            device_id={"row": r + 1 - 2 * d}, device_id_type=MESH,
        )

    def f_copy(k, d):
        at = pl.ds(k * PART, PART)
        return pltpu.make_async_remote_copy(
            src_ref=f_out.at[d, at], dst_ref=f_in.at[d, at],
            send_sem=f_sem.at[0, d, k], recv_sem=f_sem.at[1, d, k],
            device_id={"row": r + 1 - 2 * d}, device_id_type=MESH,
        )

    diag_copy = pltpu.make_async_remote_copy(
        src_ref=d_from, dst_ref=d_from, send_sem=d_sem.at[0], recv_sem=d_sem.at[1],
        device_id={"row": r + 1}, device_id_type=MESH,
    )

    def arrives(d):
        return jnp.where(d == 0, r > 0, r < last)

    def l_step(d):
        @pl.when(arrives(d))
        def _():
            l_copy(d).wait_recv()

        @pl.when(is_middle)
        def _():
            l_out[d] = jnp.where(from_here(second), l_out[d], l_in[d])
            l_copy(d).start()

    def f_step(k, d):
        at = pl.ds(k * PART, PART)
        f_copy(k, d).wait_recv()
        f_out[d, at, :] = jnp.where(from_here(q), f_out[d, at, :], f_in[d, at, :])
        f_copy(k, d).start()

    def f_both(k):
        if k < chunks:
            @pl.when(is_middle)
            def _():
                upper = jnp.where(is_upper, 1, 0)
                f_step(k, upper)
                f_step(k, 1 - upper)

    def slot_ref(kind, slot):
        return g_top.at[slot] if kind == TOP else g.at[kind, slot]

    def peer_copy(kind, m, slot):
        return pltpu.make_async_remote_copy(
            src_ref=slot_ref(kind, slot), dst_ref=slot_ref(kind, slot),
            send_sem=peer_send.at[kind, m], recv_sem=peer_recv.at[kind, m],
            device_id={"col": (c + 2 * m) % n_col}, device_id_type=MESH,
        )

    def sib_copy(kind, m, slot):
        return pltpu.make_async_remote_copy(
            src_ref=slot_ref(kind, slot), dst_ref=slot_ref(kind, slot),
            send_sem=sib_send.at[kind, m], recv_sem=sib_recv.at[kind, m],
            device_id={"col": sibling}, device_id_type=MESH,
        )

    def spread(kind):
        for m in range(1, n_peer):
            peer_copy(kind, m, c).start()
        sib_copy(kind, 0, c).start()

    def diag_peer(m):
        return pltpu.make_async_remote_copy(
            src_ref=d_from.at[p], dst_ref=g_diag.at[c],
            send_sem=peer_send.at[DIAG, m], recv_sem=peer_recv.at[DIAG, m],
            device_id={"col": (c + 2 * m) % n_col}, device_id_type=MESH,
        )

    def diag_cross(m):
        return pltpu.make_async_remote_copy(
            src_ref=d_from.at[1 - p], dst_ref=g_diag.at[c],
            send_sem=sib_send.at[DIAG, m], recv_sem=sib_recv.at[DIAG, m],
            device_id={"col": (sibling + 2 * m) % n_col}, device_id_type=MESH,
        )

    def spread_diag():
        for m in range(n_peer - 1, 0, -1):
            diag_peer(m).start()
            diag_cross(m).start()
        diag_cross(0).start()
        g_diag[c] = d_from[p]

    inverse_copy = pltpu.make_async_remote_copy(
        src_ref=inverse_ref.at[p], dst_ref=inverse_ref.at[p], send_sem=i_sem.at[0], recv_sem=i_sem.at[1],
        device_id={"col": sibling}, device_id_type=MESH,
    )

    def share(kind):
        for m in range(1, n_peer):
            slot = (c + n_col - 2 * m) % n_col
            peer_copy(kind, m, slot).wait_recv()
            sib_copy(kind, m, slot).start()

    def settle(kind):
        for m in range(n_peer):
            sib_copy(kind, m, (sibling + n_col - 2 * m) % n_col).wait_recv()

    def drain(kind):
        for m in range(1, n_peer):
            peer_copy(kind, m, c).wait_send()
        for m in range(n_peer):
            sib_copy(kind, m, c).wait_send()

    @pl.when(is_first)
    def _():
        diag_copy.start()
        spread_diag()

    @pl.when(r > 0)
    def _():
        spread(ONE)

    own_top = dot_pick(panels_ref[0], one_hot(iota((rows, PW), 0).astype(F32) == local_one).astype(BF16))
    l_out[0] = own_top
    l_out[1] = own_top
    block_t[...] = block_ref[...].T
    own = dot_pick(block_t[...], one_hot(iota((rows, tops), 0).astype(F32) == local).astype(BF16))
    own_ref[...] = own
    f_out[0] = own
    f_out[1] = own

    @pl.when(is_first)
    def _():
        l_copy(0).start()
        for k in range(chunks):
            f_copy(k, 0).start()

    @pl.when(is_last)
    def _():
        l_copy(1).start()
        for k in range(chunks):
            f_copy(k, 1).start()

    @pl.when(is_upper)
    def _():
        l_step(1)

    @pl.when(r > 0)
    def _():
        diag_copy.wait_recv()

        @pl.when(r < last)
        def _():
            diag_copy.start()

        spread_diag()

    l_step(0)

    @pl.when(jnp.logical_not(is_upper))
    def _():
        l_step(1)

    top_rows = jnp.where(second < start_f, l_in[0], jnp.where(from_here(second), own_top, l_in[1]))
    g_top[c] = top_rows
    spread(TOP)
    f_both(0)

    @pl.when(r > 0)
    def _():
        put = one_hot(iota((PW, rows), 1).astype(F32) == second_c - start_f)
        moved = jnp.sum(put, axis=0, keepdims=True) > 0.5
        g[ZERO, c] = jnp.where(moved, dot_pick(l_in[0], put.astype(BF16)), panels_ref[0])
        spread(ZERO)

    f_both(1)
    f_both(2)

    for m in range(n_peer):
        diag_cross(m).wait_recv()
        if m:
            diag_peer(m).wait_recv()
    whole = jnp.where(iota((PW, PW), 0) < iota((PW, PW), 1), g_diag[...].reshape(PW, PW), 0.0)
    lanes = iota((SMALL, PW), 1)
    small = jnp.zeros((SMALL, PW), F32)
    for b in range(PW // SMALL):
        small += jnp.where(lanes // SMALL == b, whole[b * SMALL : (b + 1) * SMALL], 0.0)

    def spaced(small):
        same = iota((PW, PW), 0) // SMALL == iota((PW, PW), 1) // SMALL
        return split(jnp.where(same, jnp.concatenate([small] * (PW // SMALL), 0), 0.0))

    power = dot_split(split(small), spaced(small))
    f_both(3)
    small = one_hot(lanes % SMALL == iota((SMALL, PW), 0)) - small
    span = 2
    while span < SMALL:
        last_one = 2 * span >= SMALL
        new = dot_split(split(small if last_one else jnp.concatenate([small, power], 0)), spaced(power))
        small = small + new[:SMALL]
        power = new[SMALL:]
        span *= 2
        f_both(span.bit_length() + 1)
    share(TOP)

    same = iota((PW, PW), 0) // SMALL == iota((PW, PW), 1) // SMALL
    inverse = jnp.where(same, jnp.concatenate([small] * (PW // SMALL), 0), 0.0)
    size = SMALL
    while size < PW:
        pairs = PW // (2 * size)
        pair_lanes = iota((size, PW), 1) // (2 * size)

        def fold(a):
            return sum(a[2 * size * i : 2 * size * i + size] for i in range(pairs))

        def unfold(a):
            empty = jnp.zeros((size, PW), F32)
            return jnp.concatenate([x for i in range(pairs) for x in (jnp.where(pair_lanes == i, a, 0.0), empty)], 0)

        other = (iota((size, PW), 1) // size) % 2 == 1
        beside = sum(
            jnp.where(other & (pair_lanes == i), whole[2 * size * i : 2 * size * i + size], 0.0) for i in range(pairs)
        )
        right = dot_split(split(beside), split(inverse))
        inverse = inverse - unfold(dot_split(split(fold(inverse)), split(unfold(right))))
        size *= 2
    for k in range(8, chunks):
        f_both(k)
    inverse_ref[p] = inverse
    inverse_copy.start()

    @pl.when(r > 0)
    def _():
        share(ZERO)
        share(ONE)

    @pl.when(r > 0)
    def _():
        put = one_hot(iota((tops, rows), 1).astype(F32) == q_c - start_f)
        moved_ref[0:1, :] = jnp.sum(put, axis=0, keepdims=True)
        put_ref[...] = put.astype(BF16)
        for kind, at in ((ZERO, 0), (ONE, PW)):
            settle(kind)
            high, low = split(g[kind].reshape(PW, rows))
            low_high[at : at + PW] = high
            low_low[at : at + PW] = low

    settle(TOP)
    above = split(g_top[...].reshape(PW, PW))
    inverse_copy.wait_recv()
    inverses = [split(inverse_ref[0]), split(inverse_ref[1])]

    for half in range(2):
        mine = range(half * chunks // 2, (half + 1) * chunks // 2)
        at = slice(mine[0] * PART, (mine[-1] + 1) * PART)

        @pl.when(is_first)
        def _():
            for k in mine:
                f_copy(k, 1).wait_recv()

        @pl.when(is_last)
        def _():
            for k in mine:
                f_copy(k, 0).wait_recv()

        top = jnp.where(q < start_f, f_in[0, at], jnp.where(from_here(q), own_ref[at], f_in[1, at]))
        upper0 = dot_split(split(top[:, :PW]), inverses[0])
        upper1 = dot_split(split(top[:, PW:] - dot_split(split(upper0), above)), inverses[1])
        upper = jnp.concatenate([upper0, upper1], 1)

        @pl.when(is_first)
        def _():
            out_ref[:, at] = upper.T

        @pl.when(r > 0)
        def _():
            work = jnp.where(moved_ref[0:1, :] > 0.5, dot_pick(f_in[0, at], put_ref[...]), block_t[at])
            out_ref[:, at] = (work - dot_split(split(upper), (low_high[...], low_low[...]))).T

    @pl.when(r > 0)
    def _():
        drain(ZERO)
        drain(ONE)

    for m in range(n_peer):
        diag_cross(m).wait_send()
        if m:
            diag_peer(m).wait_send()
    inverse_copy.wait_send()
    drain(TOP)

    @pl.when(r < last)
    def _():
        diag_copy.wait_send()

    for d in range(2):
        @pl.when((r < last) if d == 0 else (r > 0))
        def _():
            l_copy(d).wait_send()
            for k in range(chunks):
                f_copy(k, d).wait_send()


def fused(block, panels, pivots):
    n_row, n_col = lax.axis_size("row"), lax.axis_size("col")
    rows, cols = block.shape
    kc = panels.shape[2]
    tops = 2 * PW
    vmem = pl.BlockSpec(memory_space=pltpu.VMEM)
    n_peer = n_col // 2
    dma = pltpu.SemaphoreType.DMA
    return pl.pallas_call(
        functools.partial(kernel, n_row, n_col),
        out_shape=jax.ShapeDtypeStruct((rows, cols), F32),
        in_specs=[vmem] * 3,
        out_specs=vmem,
        scratch_shapes=[
            pltpu.VMEM((2, kc, PW), F32),
            pltpu.VMEM((n_col, kc, PW), F32),
            pltpu.VMEM((2, n_col, kc, rows), F32),
            pltpu.VMEM((n_col, kc, PW), F32),
            pltpu.VMEM((cols, tops), F32),
            pltpu.VMEM((2, cols, tops), F32),
            pltpu.VMEM((2, cols, tops), F32),
            pltpu.VMEM((2, kc, PW), F32),
            pltpu.VMEM((2, kc, PW), F32),
            pltpu.VMEM((2, PW, PW), F32),
            pltpu.VMEM((cols, rows), F32),
            pltpu.VMEM((tops, rows), BF16),
            pltpu.VMEM((8, rows), F32),
            pltpu.VMEM((tops, rows), BF16),
            pltpu.VMEM((tops, rows), BF16),
            dma((2,)),
            dma((2,)),
            dma((2, 2)),
            dma((2, 2, cols // PART)),
        ]
        + [dma((4, n_peer))] * 4,
        compiler_params=pltpu.CompilerParams(
            collective_id=0, has_side_effects=True, vmem_limit_bytes=48 * 1024 * 1024
        ),
    )(pivots, block, jnp.swapaxes(panels, 1, 2))


def body(block, panels, pivots):
    kc = panels.shape[2]
    fits = (
        block.shape[0] == 2 * PW
        and block.shape[1] % 128 == 0
        and kc % 8 == 0
        and lax.axis_size("col") % 2 == 0
        and lax.axis_size("row") > 1
    )
    return fused(block, panels, pivots) if fits else plain(block, panels, pivots)


def solution(mesh):
    return jax.shard_map(
        body,
        mesh=mesh,
        in_specs=(P("row", "col"), P(None, "row", "col"), P()),
        out_specs=P("row", "col"),
        check_vma=False,
    )
```

```python
import functools

import jax
import jax.numpy as jnp
from jax import lax
from jax.experimental import pallas as pl
from jax.experimental.pallas import tpu as pltpu
from jax.sharding import PartitionSpec as P

PW = 256


def swap_order(piv_row, offset, count):
    own = offset + jnp.arange(piv_row.shape[0], dtype=jnp.int32)
    base = jnp.arange(count, dtype=jnp.int32)
    return base.at[own].set(piv_row).at[piv_row].set(own)


def pick_rows(data, perm, targets, start):
    local_src = perm[targets] - start
    owned = (local_src >= 0) & (local_src < data.shape[0])
    taken = jnp.take(data, jnp.clip(local_src, 0, data.shape[0] - 1), axis=0)
    return jnp.where(owned[:, None], taken, 0.0)


def place_rows(data, targets, values, start):
    local_dst = targets - start
    inside = (local_dst >= 0) & (local_dst < data.shape[0])
    where_to = jnp.where(inside, local_dst, data.shape[0])
    return data.at[where_to].set(values, mode="drop")


def solve_top(diag_rows, rows):
    strict = jnp.tril(diag_rows, -1)
    inverse = jnp.eye(PW, dtype=jnp.float32) - strict
    power = strict
    for level in range(1, PW.bit_length() - 1):
        power = jnp.dot(
            power, power, precision=lax.Precision.HIGHEST, preferred_element_type=jnp.float32
        )
        inverse = inverse + jnp.dot(
            inverse, power, precision=lax.Precision.HIGHEST, preferred_element_type=jnp.float32
        )
    return jnp.dot(
        inverse, rows, precision=lax.Precision.HIGHEST, preferred_element_type=jnp.float32
    )


def finish(work, lower, offset, start, upper):
    product = jnp.dot(
        lower, upper, precision=lax.Precision.HIGHEST, preferred_element_type=jnp.float32
    )
    global_rows = start + jnp.arange(work.shape[0], dtype=jnp.int32)
    work = jnp.where((global_rows >= offset + PW)[:, None], work - product, work)
    placed = work.at[offset : offset + PW].set(upper)
    in_top = (global_rows >= offset) & (global_rows < offset + PW)
    return jnp.where(in_top[:, None], placed, work)


def plain(block, panels, pivots):
    rows_here = block.shape[0]
    rows_all = rows_here * lax.axis_size("row")
    start = lax.axis_index("row") * rows_here
    identity_perm = jnp.arange(rows_all, dtype=jnp.int32)
    perms = [swap_order(pivots[panel], panel * PW, rows_all) for panel in range(2)]
    targets = [
        jnp.concatenate([jnp.arange(panel * PW, panel * PW + PW, dtype=jnp.int32), pivots[panel]])
        for panel in range(2)
    ]
    tops_index = [jnp.arange(panel * PW, panel * PW + PW, dtype=jnp.int32) for panel in range(2)]
    work = block
    lowers = lax.all_gather(panels, "col", axis=2, tiled=True)
    for panel in range(2):
        offset = panel * PW
        diag_rows = pick_rows(lowers[panel], identity_perm, tops_index[panel], start)
        picked = pick_rows(work, perms[panel], targets[panel], start)
        moved, diag_all = lax.psum((picked, diag_rows), "row")
        work = place_rows(work, targets[panel], moved, start)
        upper = solve_top(diag_all, moved[:PW])
        work = finish(work, lowers[panel], offset, start, upper)
    return work

MESH = pl.DeviceIdType.MESH
F32, BF16 = jnp.float32, jnp.bfloat16
SMALL = 32
PART = 32
LAG = 2
ONE, ZERO, TOP, DIAG = range(4)


def dot(a, b):
    return jnp.dot(a, b, preferred_element_type=F32)


def split(a):
    high = a.astype(BF16)
    return high, (a - high.astype(F32)).astype(BF16)


def dot_split(a, b):
    m = a[0].shape[0]
    both = dot(jnp.concatenate(a, 0), b[0])
    return both[:m] + (both[m:] + dot(a[0], b[1]))


def dot_pick(a, one_hot):
    m = a.shape[0]
    out = dot(jnp.concatenate(split(a), 0), one_hot)
    return out[:m] + out[m:]


def iota(shape, dim):
    return lax.broadcasted_iota(jnp.int32, shape, dim)


def one_hot(condition):
    return jnp.where(condition, 1.0, 0.0)


def kernel(
    n_row, n_col, piv_ref, block_ref, panels_ref, out_ref, d_from, g_diag,
    g, g_top, own_ref, f_in, f_out, l_in, l_out, inverse_ref,
    block_t, put_ref, moved_ref, low_high, low_low,
    d_sem, i_sem, l_sem, f_sem, peer_send, peer_recv, sib_send, sib_recv,
):
    r, c = lax.axis_index("row"), lax.axis_index("col")
    rows, cols = block_ref.shape
    tops = 2 * PW
    kc = panels_ref.shape[1]
    n_peer = n_col // 2
    chunks = cols // PART
    last = n_row - 1
    p = c % 2
    sibling = c + 1 - 2 * p
    is_first, is_last = r == 0, r == last
    is_middle = (r > 0) & (r < last)
    is_upper = 2 * r >= n_row
    start = r * rows

    barrier = pltpu.get_barrier_semaphore()

    @pl.when(r > 0)
    def _():
        pl.semaphore_signal(barrier, 1, device_id={"row": r - 1}, device_id_type=MESH)

    @pl.when(r < last)
    def _():
        pl.semaphore_signal(barrier, 1, device_id={"row": r + 1}, device_id_type=MESH)

    for m in range(1, n_col):
        pl.semaphore_signal(barrier, 1, device_id={"col": (c + m) % n_col}, device_id_type=MESH)

    first = piv_ref[0:1, :].astype(F32)
    second = piv_ref[1:2, :].astype(F32)
    sub, lane = iota((PW, PW), 0).astype(F32), iota((PW, PW), 1).astype(F32)

    def upright(v):
        return jnp.sum(jnp.where(sub == lane, v, 0.0), axis=1, keepdims=True)

    first_c, second_c = upright(first), upright(second)
    lane_row = lane[0:1, :]
    sub_col = sub[:, 0:1]

    def lookup(match, found, otherwise, axis):
        hit = jnp.sum(one_hot(match), axis=axis, keepdims=True)
        return jnp.sum(jnp.where(match, found, 0.0), axis=axis, keepdims=True) + jnp.where(hit > 0.5, 0.0, otherwise)

    q_second = lookup(first_c == second, sub, second, 0)
    q_second_c = lookup(second_c == first, lane, second_c, 1)
    home = lookup(first_c == lane + PW, sub, lane_row + PW, 0)
    home_c = lookup(first == sub + PW, lane, sub_col + PW, 1)
    out_first = jnp.where(first < tops, first, lookup(second_c == first, home_c, lane_row, 0))
    out_second = jnp.where(q_second < tops, q_second, home)
    q = jnp.concatenate([first, q_second], 1)
    q_c = jnp.concatenate([first_c, q_second_c], 0)
    outward = jnp.concatenate([out_first, out_second], 1)

    start_f = start.astype(F32)
    local = jnp.where(is_first, outward, q - start_f)
    local_one = jnp.where(is_first, lane_row + PW, second - start_f)

    def from_here(v):
        return (v >= start_f) & (v < start_f + rows)

    @pl.when(is_first)
    def _():
        d_from[0] = panels_ref[0, :, :PW]
        d_from[1] = panels_ref[1, :, PW:tops]

    @pl.when(r > 0)
    def _():
        g[ONE, c] = panels_ref[1]

    @pl.when(is_middle)
    def _():
        pl.semaphore_wait(barrier, n_col + 1)

    @pl.when(is_first | is_last)
    def _():
        pl.semaphore_wait(barrier, n_col)

    def l_copy(d):
        return pltpu.make_async_remote_copy(
            src_ref=l_out.at[d], dst_ref=l_in.at[d], send_sem=l_sem.at[0, d], recv_sem=l_sem.at[1, d],
            device_id={"row": r + 1 - 2 * d}, device_id_type=MESH,
        )

    def f_copy(k, d):
        at = pl.ds(k * PART, PART)
        return pltpu.make_async_remote_copy(
            src_ref=f_out.at[d, at], dst_ref=f_in.at[d, at],
            send_sem=f_sem.at[0, d, k], recv_sem=f_sem.at[1, d, k],
            device_id={"row": r + 1 - 2 * d}, device_id_type=MESH,
        )

    diag_copy = pltpu.make_async_remote_copy(
        src_ref=d_from, dst_ref=d_from, send_sem=d_sem.at[0], recv_sem=d_sem.at[1],
        device_id={"row": r + 1}, device_id_type=MESH,
    )

    def arrives(d):
        return jnp.where(d == 0, r > 0, r < last)

    def l_step(d):
        @pl.when(arrives(d))
        def _():
            l_copy(d).wait_recv()

        @pl.when(is_middle)
        def _():
            l_out[d] = jnp.where(from_here(second), l_out[d], l_in[d])
            l_copy(d).start()

    def f_step(k, d):
        at = pl.ds(k * PART, PART)
        f_copy(k, d).wait_recv()
        f_out[d, at, :] = jnp.where(from_here(q), f_out[d, at, :], f_in[d, at, :])
        f_copy(k, d).start()

    def stage(k):
        upper = jnp.where(is_upper, 1, 0)
        near, far = k < chunks, 0 <= k - LAG < chunks
        if near or far:
            @pl.when(is_middle)
            def _():
                if near:
                    f_step(k, upper)
                if far:
                    f_step(k - LAG, 1 - upper)

    def slot_ref(kind, slot):
        return g_top.at[slot] if kind == TOP else g.at[kind, slot]

    def peer_copy(kind, m, slot):
        return pltpu.make_async_remote_copy(
            src_ref=slot_ref(kind, slot), dst_ref=slot_ref(kind, slot),
            send_sem=peer_send.at[kind, m], recv_sem=peer_recv.at[kind, m],
            device_id={"col": (c + 2 * m) % n_col}, device_id_type=MESH,
        )

    def sib_copy(kind, m, slot):
        return pltpu.make_async_remote_copy(
            src_ref=slot_ref(kind, slot), dst_ref=slot_ref(kind, slot),
            send_sem=sib_send.at[kind, m], recv_sem=sib_recv.at[kind, m],
            device_id={"col": sibling}, device_id_type=MESH,
        )

    def spread(kind):
        for m in range(1, n_peer):
            peer_copy(kind, m, c).start()
        sib_copy(kind, 0, c).start()

    def diag_peer(m):
        return pltpu.make_async_remote_copy(
            src_ref=d_from.at[p], dst_ref=g_diag.at[c],
            send_sem=peer_send.at[DIAG, m], recv_sem=peer_recv.at[DIAG, m],
            device_id={"col": (c + 2 * m) % n_col}, device_id_type=MESH,
        )

    def diag_cross(m):
        return pltpu.make_async_remote_copy(
            src_ref=d_from.at[1 - p], dst_ref=g_diag.at[c],
            send_sem=sib_send.at[DIAG, m], recv_sem=sib_recv.at[DIAG, m],
            device_id={"col": (sibling + 2 * m) % n_col}, device_id_type=MESH,
        )

    def spread_diag():
        for m in range(n_peer - 1, 0, -1):
            diag_peer(m).start()
            diag_cross(m).start()
        diag_cross(0).start()
        g_diag[c] = d_from[p]

    inverse_copy = pltpu.make_async_remote_copy(
        src_ref=inverse_ref.at[p], dst_ref=inverse_ref.at[p], send_sem=i_sem.at[0], recv_sem=i_sem.at[1],
        device_id={"col": sibling}, device_id_type=MESH,
    )

    def share(kind):
        for m in range(1, n_peer):
            slot = (c + n_col - 2 * m) % n_col
            peer_copy(kind, m, slot).wait_recv()
            sib_copy(kind, m, slot).start()

    def settle(kind):
        for m in range(n_peer):
            sib_copy(kind, m, (sibling + n_col - 2 * m) % n_col).wait_recv()

    def drain(kind):
        for m in range(1, n_peer):
            peer_copy(kind, m, c).wait_send()
        for m in range(n_peer):
            sib_copy(kind, m, c).wait_send()

    @pl.when(is_first)
    def _():
        diag_copy.start()
        spread_diag()

    @pl.when(r > 0)
    def _():
        spread(ONE)

    own_top = dot_pick(panels_ref[0], one_hot(iota((rows, PW), 0).astype(F32) == local_one).astype(BF16))
    l_out[0] = own_top
    l_out[1] = own_top
    block_t[...] = block_ref[...].T
    own = dot_pick(block_t[...], one_hot(iota((rows, tops), 0).astype(F32) == local).astype(BF16))
    own_ref[...] = own
    f_out[0] = own
    f_out[1] = own

    @pl.when(is_first)
    def _():
        l_copy(0).start()
        for k in range(chunks):
            f_copy(k, 0).start()

    @pl.when(is_last)
    def _():
        l_copy(1).start()
        for k in range(chunks):
            f_copy(k, 1).start()

    @pl.when(is_upper)
    def _():
        l_step(1)

    @pl.when(r > 0)
    def _():
        diag_copy.wait_recv()

        @pl.when(r < last)
        def _():
            diag_copy.start()

        spread_diag()

    l_step(0)

    @pl.when(jnp.logical_not(is_upper))
    def _():
        l_step(1)

    top_rows = jnp.where(second < start_f, l_in[0], jnp.where(from_here(second), own_top, l_in[1]))
    g_top[c] = top_rows
    spread(TOP)
    stage(0)

    @pl.when(r > 0)
    def _():
        put = one_hot(iota((PW, rows), 1).astype(F32) == second_c - start_f)
        moved = jnp.sum(put, axis=0, keepdims=True) > 0.5
        g[ZERO, c] = jnp.where(moved, dot_pick(l_in[0], put.astype(BF16)), panels_ref[0])
        spread(ZERO)

    stage(1)
    stage(2)

    for m in range(n_peer):
        diag_cross(m).wait_recv()
        if m:
            diag_peer(m).wait_recv()
    whole = jnp.where(iota((PW, PW), 0) < iota((PW, PW), 1), g_diag[...].reshape(PW, PW), 0.0)
    lanes = iota((SMALL, PW), 1)
    small = jnp.zeros((SMALL, PW), F32)
    for b in range(PW // SMALL):
        small += jnp.where(lanes // SMALL == b, whole[b * SMALL : (b + 1) * SMALL], 0.0)

    def spaced(small):
        same = iota((PW, PW), 0) // SMALL == iota((PW, PW), 1) // SMALL
        return split(jnp.where(same, jnp.concatenate([small] * (PW // SMALL), 0), 0.0))

    power = dot_split(split(small), spaced(small))
    stage(3)
    small = one_hot(lanes % SMALL == iota((SMALL, PW), 0)) - small
    span = 2
    while span < SMALL:
        last_one = 2 * span >= SMALL
        new = dot_split(split(small if last_one else jnp.concatenate([small, power], 0)), spaced(power))
        small = small + new[:SMALL]
        power = new[SMALL:]
        span *= 2
        stage(span.bit_length() + 1)
    share(TOP)

    same = iota((PW, PW), 0) // SMALL == iota((PW, PW), 1) // SMALL
    inverse = jnp.where(same, jnp.concatenate([small] * (PW // SMALL), 0), 0.0)
    size = SMALL
    while size < PW:
        pairs = PW // (2 * size)
        pair_lanes = iota((size, PW), 1) // (2 * size)

        def fold(a):
            return sum(a[2 * size * i : 2 * size * i + size] for i in range(pairs))

        def unfold(a):
            empty = jnp.zeros((size, PW), F32)
            return jnp.concatenate([x for i in range(pairs) for x in (jnp.where(pair_lanes == i, a, 0.0), empty)], 0)

        other = (iota((size, PW), 1) // size) % 2 == 1
        beside = sum(
            jnp.where(other & (pair_lanes == i), whole[2 * size * i : 2 * size * i + size], 0.0) for i in range(pairs)
        )
        right = dot_split(split(beside), split(inverse))
        inverse = inverse - unfold(dot_split(split(fold(inverse)), split(unfold(right))))
        size *= 2
    for k in range(8, chunks + LAG):
        stage(k)
    inverse_ref[p] = inverse
    inverse_copy.start()

    @pl.when(r > 0)
    def _():
        share(ZERO)
        share(ONE)

    @pl.when(r > 0)
    def _():
        put = one_hot(iota((tops, rows), 1).astype(F32) == q_c - start_f)
        moved_ref[0:1, :] = jnp.sum(put, axis=0, keepdims=True)
        put_ref[...] = put.astype(BF16)
        for kind, at in ((ZERO, 0), (ONE, PW)):
            settle(kind)
            high, low = split(g[kind].reshape(PW, rows))
            low_high[at : at + PW] = high
            low_low[at : at + PW] = low

    settle(TOP)
    above = split(g_top[...].reshape(PW, PW))
    inverse_copy.wait_recv()
    inverses = [split(inverse_ref[0]), split(inverse_ref[1])]

    for half in range(2):
        mine = range(half * chunks // 2, (half + 1) * chunks // 2)
        at = slice(mine[0] * PART, (mine[-1] + 1) * PART)

        @pl.when(is_first)
        def _():
            for k in mine:
                f_copy(k, 1).wait_recv()

        @pl.when(is_last)
        def _():
            for k in mine:
                f_copy(k, 0).wait_recv()

        top = jnp.where(q < start_f, f_in[0, at], jnp.where(from_here(q), own_ref[at], f_in[1, at]))
        upper0 = dot_split(split(top[:, :PW]), inverses[0])
        upper1 = dot_split(split(top[:, PW:] - dot_split(split(upper0), above)), inverses[1])
        upper = jnp.concatenate([upper0, upper1], 1)

        @pl.when(is_first)
        def _():
            out_ref[:, at] = upper.T

        @pl.when(r > 0)
        def _():
            work = jnp.where(moved_ref[0:1, :] > 0.5, dot_pick(f_in[0, at], put_ref[...]), block_t[at])
            out_ref[:, at] = (work - dot_split(split(upper), (low_high[...], low_low[...]))).T

    @pl.when(r > 0)
    def _():
        drain(ZERO)
        drain(ONE)

    for m in range(n_peer):
        diag_cross(m).wait_send()
        if m:
            diag_peer(m).wait_send()
    inverse_copy.wait_send()
    drain(TOP)

    @pl.when(r < last)
    def _():
        diag_copy.wait_send()

    for d in range(2):
        @pl.when((r < last) if d == 0 else (r > 0))
        def _():
            l_copy(d).wait_send()
            for k in range(chunks):
                f_copy(k, d).wait_send()


def fused(block, panels, pivots):
    n_row, n_col = lax.axis_size("row"), lax.axis_size("col")
    rows, cols = block.shape
    kc = panels.shape[2]
    tops = 2 * PW
    vmem = pl.BlockSpec(memory_space=pltpu.VMEM)
    n_peer = n_col // 2
    dma = pltpu.SemaphoreType.DMA
    return pl.pallas_call(
        functools.partial(kernel, n_row, n_col),
        out_shape=jax.ShapeDtypeStruct((rows, cols), F32),
        in_specs=[vmem] * 3,
        out_specs=vmem,
        scratch_shapes=[
            pltpu.VMEM((2, kc, PW), F32),
            pltpu.VMEM((n_col, kc, PW), F32),
            pltpu.VMEM((2, n_col, kc, rows), F32),
            pltpu.VMEM((n_col, kc, PW), F32),
            pltpu.VMEM((cols, tops), F32),
            pltpu.VMEM((2, cols, tops), F32),
            pltpu.VMEM((2, cols, tops), F32),
            pltpu.VMEM((2, kc, PW), F32),
            pltpu.VMEM((2, kc, PW), F32),
            pltpu.VMEM((2, PW, PW), F32),
            pltpu.VMEM((cols, rows), F32),
            pltpu.VMEM((tops, rows), BF16),
            pltpu.VMEM((8, rows), F32),
            pltpu.VMEM((tops, rows), BF16),
            pltpu.VMEM((tops, rows), BF16),
            dma((2,)),
            dma((2,)),
            dma((2, 2)),
            dma((2, 2, cols // PART)),
        ]
        + [dma((4, n_peer))] * 4,
        compiler_params=pltpu.CompilerParams(
            collective_id=0, has_side_effects=True, vmem_limit_bytes=48 * 1024 * 1024
        ),
    )(pivots, block, jnp.swapaxes(panels, 1, 2))


def body(block, panels, pivots):
    kc = panels.shape[2]
    fits = (
        block.shape[0] == 2 * PW
        and block.shape[1] % 128 == 0
        and kc % 8 == 0
        and lax.axis_size("col") % 2 == 0
        and lax.axis_size("row") > 1
    )
    return fused(block, panels, pivots) if fits else plain(block, panels, pivots)


def solution(mesh):
    return jax.shard_map(
        body,
        mesh=mesh,
        in_specs=(P("row", "col"), P(None, "row", "col"), P()),
        out_specs=P("row", "col"),
        check_vma=False,
    )
```

```python
import functools

import jax
import jax.numpy as jnp
from jax import lax
from jax.experimental import pallas as pl
from jax.experimental.pallas import tpu as pltpu
from jax.sharding import PartitionSpec as P

PW = 256


def swap_order(piv_row, offset, count):
    own = offset + jnp.arange(piv_row.shape[0], dtype=jnp.int32)
    base = jnp.arange(count, dtype=jnp.int32)
    return base.at[own].set(piv_row).at[piv_row].set(own)


def pick_rows(data, perm, targets, start):
    local_src = perm[targets] - start
    owned = (local_src >= 0) & (local_src < data.shape[0])
    taken = jnp.take(data, jnp.clip(local_src, 0, data.shape[0] - 1), axis=0)
    return jnp.where(owned[:, None], taken, 0.0)


def place_rows(data, targets, values, start):
    local_dst = targets - start
    inside = (local_dst >= 0) & (local_dst < data.shape[0])
    where_to = jnp.where(inside, local_dst, data.shape[0])
    return data.at[where_to].set(values, mode="drop")


def solve_top(diag_rows, rows):
    strict = jnp.tril(diag_rows, -1)
    inverse = jnp.eye(PW, dtype=jnp.float32) - strict
    power = strict
    for level in range(1, PW.bit_length() - 1):
        power = jnp.dot(
            power, power, precision=lax.Precision.HIGHEST, preferred_element_type=jnp.float32
        )
        inverse = inverse + jnp.dot(
            inverse, power, precision=lax.Precision.HIGHEST, preferred_element_type=jnp.float32
        )
    return jnp.dot(
        inverse, rows, precision=lax.Precision.HIGHEST, preferred_element_type=jnp.float32
    )


def finish(work, lower, offset, start, upper):
    product = jnp.dot(
        lower, upper, precision=lax.Precision.HIGHEST, preferred_element_type=jnp.float32
    )
    global_rows = start + jnp.arange(work.shape[0], dtype=jnp.int32)
    work = jnp.where((global_rows >= offset + PW)[:, None], work - product, work)
    placed = work.at[offset : offset + PW].set(upper)
    in_top = (global_rows >= offset) & (global_rows < offset + PW)
    return jnp.where(in_top[:, None], placed, work)


def plain(block, panels, pivots):
    rows_here = block.shape[0]
    rows_all = rows_here * lax.axis_size("row")
    start = lax.axis_index("row") * rows_here
    identity_perm = jnp.arange(rows_all, dtype=jnp.int32)
    perms = [swap_order(pivots[panel], panel * PW, rows_all) for panel in range(2)]
    targets = [
        jnp.concatenate([jnp.arange(panel * PW, panel * PW + PW, dtype=jnp.int32), pivots[panel]])
        for panel in range(2)
    ]
    tops_index = [jnp.arange(panel * PW, panel * PW + PW, dtype=jnp.int32) for panel in range(2)]
    work = block
    lowers = lax.all_gather(panels, "col", axis=2, tiled=True)
    for panel in range(2):
        offset = panel * PW
        diag_rows = pick_rows(lowers[panel], identity_perm, tops_index[panel], start)
        picked = pick_rows(work, perms[panel], targets[panel], start)
        moved, diag_all = lax.psum((picked, diag_rows), "row")
        work = place_rows(work, targets[panel], moved, start)
        upper = solve_top(diag_all, moved[:PW])
        work = finish(work, lowers[panel], offset, start, upper)
    return work

MESH = pl.DeviceIdType.MESH
F32, BF16 = jnp.float32, jnp.bfloat16
SMALL = 32
PART = 32
LAG = 2
ONE, ZERO, TOP, DIAG = range(4)


def dot(a, b):
    return jnp.dot(a, b, preferred_element_type=F32)


def split(a):
    high = a.astype(BF16)
    return high, (a - high.astype(F32)).astype(BF16)


def dot_split(a, b):
    m = a[0].shape[0]
    both = dot(jnp.concatenate(a, 0), b[0])
    return both[:m] + (both[m:] + dot(a[0], b[1]))


def dot_pick(a, one_hot):
    m = a.shape[0]
    out = dot(jnp.concatenate(split(a), 0), one_hot)
    return out[:m] + out[m:]


def iota(shape, dim):
    return lax.broadcasted_iota(jnp.int32, shape, dim)


def one_hot(condition):
    return jnp.where(condition, 1.0, 0.0)


def kernel(
    n_row, n_col, block_ref, panels_ref, out_ref, d_from, g_diag,
    g, g_top, own_ref, f_in, f_out, l_in, l_out, inverse_ref,
    block_t, local_ref, put_ref, put_one_ref, moved_ref, low_high, low_low,
    d_sem, i_sem, l_sem, f_sem, peer_send, peer_recv, sib_send, sib_recv,
):
    r, c = lax.axis_index("row"), lax.axis_index("col")
    rows, cols = block_ref.shape
    tops = 2 * PW
    kc = g_top.shape[1]
    n_peer = n_col // 2
    chunks = cols // PART
    last = n_row - 1
    p = c % 2
    sibling = c + 1 - 2 * p
    is_first, is_last = r == 0, r == last
    is_middle = (r > 0) & (r < last)
    is_upper = 2 * r >= n_row
    start = r * rows

    barrier = pltpu.get_barrier_semaphore()

    @pl.when(r > 0)
    def _():
        pl.semaphore_signal(barrier, 1, device_id={"row": r - 1}, device_id_type=MESH)

    @pl.when(r < last)
    def _():
        pl.semaphore_signal(barrier, 1, device_id={"row": r + 1}, device_id_type=MESH)

    for m in range(1, n_col):
        pl.semaphore_signal(barrier, 1, device_id={"col": (c + m) % n_col}, device_id_type=MESH)

    first = panels_ref[2 * kc : 2 * kc + 1, :PW]
    second = panels_ref[2 * kc + 1 : 2 * kc + 2, :PW]
    sub, lane = iota((PW, PW), 0).astype(F32), iota((PW, PW), 1).astype(F32)

    def upright(v):
        return jnp.sum(jnp.where(sub == lane, v, 0.0), axis=1, keepdims=True)

    first_c = upright(first)
    lane_row = lane[0:1, :]
    sub_col = sub[:, 0:1]

    def lookup(match, found, otherwise, axis):
        hit = jnp.sum(one_hot(match), axis=axis, keepdims=True)
        return jnp.sum(jnp.where(match, found, 0.0), axis=axis, keepdims=True) + jnp.where(hit > 0.5, 0.0, otherwise)

    q_second = lookup(first_c == second, sub, second, 0)
    q = jnp.concatenate([first, q_second], 1)
    start_f = start.astype(F32)
    local_ref[0:1, :] = q - start_f
    local_ref[1:2, :PW] = second - start_f

    @pl.when(is_first)
    def _():
        second_c = upright(second)
        home = lookup(first_c == lane + PW, sub, lane_row + PW, 0)
        home_c = lookup(first == sub + PW, lane, sub_col + PW, 1)
        out_first = jnp.where(first < tops, first, lookup(second_c == first, home_c, lane_row, 0))
        out_second = jnp.where(q_second < tops, q_second, home)
        local_ref[0:1, :] = jnp.concatenate([out_first, out_second], 1)
        local_ref[1:2, :PW] = lane_row + PW

    def from_here(v):
        return (v >= start_f) & (v < start_f + rows)

    @pl.when(is_first)
    def _():
        d_from[0] = panels_ref[:kc, :PW]
        d_from[1] = panels_ref[kc : 2 * kc, PW:tops]

    @pl.when(r > 0)
    def _():
        g[ONE, c] = panels_ref[kc : 2 * kc]

    @pl.when(is_middle)
    def _():
        pl.semaphore_wait(barrier, n_col + 1)

    @pl.when(is_first | is_last)
    def _():
        pl.semaphore_wait(barrier, n_col)

    def l_copy(d):
        return pltpu.make_async_remote_copy(
            src_ref=l_out.at[d], dst_ref=l_in.at[d], send_sem=l_sem.at[0, d], recv_sem=l_sem.at[1, d],
            device_id={"row": r + 1 - 2 * d}, device_id_type=MESH,
        )

    def f_copy(k, d):
        at = pl.ds(k * PART, PART)
        return pltpu.make_async_remote_copy(
            src_ref=f_out.at[d, at], dst_ref=f_in.at[d, at],
            send_sem=f_sem.at[0, d, k], recv_sem=f_sem.at[1, d, k],
            device_id={"row": r + 1 - 2 * d}, device_id_type=MESH,
        )

    diag_copy = pltpu.make_async_remote_copy(
        src_ref=d_from, dst_ref=d_from, send_sem=d_sem.at[0], recv_sem=d_sem.at[1],
        device_id={"row": r + 1}, device_id_type=MESH,
    )

    def arrives(d):
        return jnp.where(d == 0, r > 0, r < last)

    def l_step(d):
        @pl.when(arrives(d))
        def _():
            l_copy(d).wait_recv()

        @pl.when(is_middle)
        def _():
            l_out[d] = jnp.where(from_here(second), l_out[d], l_in[d])
            l_copy(d).start()

    def f_step(k, d):
        at = pl.ds(k * PART, PART)
        f_copy(k, d).wait_recv()
        f_out[d, at, :] = jnp.where(from_here(q), f_out[d, at, :], f_in[d, at, :])
        f_copy(k, d).start()

    def stage(k):
        upper = jnp.where(is_upper, 1, 0)
        near, far = k < chunks, 0 <= k - LAG < chunks
        if near or far:
            @pl.when(is_middle)
            def _():
                if near:
                    f_step(k, upper)
                if far:
                    f_step(k - LAG, 1 - upper)

    def slot_ref(kind, slot):
        return g_top.at[slot] if kind == TOP else g.at[kind, slot]

    def peer_copy(kind, m, slot):
        return pltpu.make_async_remote_copy(
            src_ref=slot_ref(kind, slot), dst_ref=slot_ref(kind, slot),
            send_sem=peer_send.at[kind, m], recv_sem=peer_recv.at[kind, m],
            device_id={"col": (c + 2 * m) % n_col}, device_id_type=MESH,
        )

    def sib_copy(kind, m, slot):
        return pltpu.make_async_remote_copy(
            src_ref=slot_ref(kind, slot), dst_ref=slot_ref(kind, slot),
            send_sem=sib_send.at[kind, m], recv_sem=sib_recv.at[kind, m],
            device_id={"col": sibling}, device_id_type=MESH,
        )

    def spread(kind):
        for m in range(1, n_peer):
            peer_copy(kind, m, c).start()
        sib_copy(kind, 0, c).start()

    def diag_peer(m):
        return pltpu.make_async_remote_copy(
            src_ref=d_from.at[p], dst_ref=g_diag.at[c],
            send_sem=peer_send.at[DIAG, m], recv_sem=peer_recv.at[DIAG, m],
            device_id={"col": (c + 2 * m) % n_col}, device_id_type=MESH,
        )

    def diag_cross(m):
        return pltpu.make_async_remote_copy(
            src_ref=d_from.at[1 - p], dst_ref=g_diag.at[c],
            send_sem=sib_send.at[DIAG, m], recv_sem=sib_recv.at[DIAG, m],
            device_id={"col": (sibling + 2 * m) % n_col}, device_id_type=MESH,
        )

    def spread_diag():
        for m in range(n_peer - 1, 0, -1):
            diag_peer(m).start()
            diag_cross(m).start()
        diag_cross(0).start()
        g_diag[c] = d_from[p]

    inverse_copy = pltpu.make_async_remote_copy(
        src_ref=inverse_ref.at[p], dst_ref=inverse_ref.at[p], send_sem=i_sem.at[0], recv_sem=i_sem.at[1],
        device_id={"col": sibling}, device_id_type=MESH,
    )

    def share(kind):
        for m in range(1, n_peer):
            slot = (c + n_col - 2 * m) % n_col
            peer_copy(kind, m, slot).wait_recv()
            sib_copy(kind, m, slot).start()

    def settle(kind):
        for m in range(n_peer):
            sib_copy(kind, m, (sibling + n_col - 2 * m) % n_col).wait_recv()

    def drain(kind):
        for m in range(1, n_peer):
            peer_copy(kind, m, c).wait_send()
        for m in range(n_peer):
            sib_copy(kind, m, c).wait_send()

    @pl.when(is_first)
    def _():
        diag_copy.start()
        spread_diag()

    @pl.when(r > 0)
    def _():
        spread(ONE)

    own_top = dot_pick(panels_ref[:kc], one_hot(iota((rows, PW), 0).astype(F32) == local_ref[1:2, :PW]).astype(BF16))
    l_out[0] = own_top
    l_out[1] = own_top

    @pl.when(is_first)
    def _():
        l_copy(0).start()

    @pl.when(is_last)
    def _():
        l_copy(1).start()

    block_t[...] = block_ref[...].T
    own = dot_pick(block_t[...], one_hot(iota((rows, tops), 0).astype(F32) == local_ref[0:1, :]).astype(BF16))
    own_ref[...] = own
    f_out[0] = own
    f_out[1] = own

    @pl.when(is_first)
    def _():
        for k in range(chunks):
            f_copy(k, 0).start()

    @pl.when(is_last)
    def _():
        for k in range(chunks):
            f_copy(k, 1).start()

    @pl.when(r > 0)
    def _():
        second_c = upright(second)
        q_c = jnp.concatenate([first_c, lookup(second_c == first, lane, second_c, 1)], 0)
        put = one_hot(iota((PW, rows), 1).astype(F32) == second_c - start_f)
        put_one_ref[...] = put.astype(BF16)
        moved_ref[1:2, :] = jnp.sum(put, axis=0, keepdims=True)
        put = one_hot(iota((tops, rows), 1).astype(F32) == q_c - start_f)
        put_ref[...] = put.astype(BF16)
        moved_ref[0:1, :] = jnp.sum(put, axis=0, keepdims=True)

    @pl.when(is_upper)
    def _():
        l_step(1)

    @pl.when(r > 0)
    def _():
        diag_copy.wait_recv()

        @pl.when(r < last)
        def _():
            diag_copy.start()

        spread_diag()

    l_step(0)

    @pl.when(jnp.logical_not(is_upper))
    def _():
        l_step(1)

    top_rows = jnp.where(second < start_f, l_in[0], jnp.where(from_here(second), own_top, l_in[1]))
    g_top[c] = top_rows
    spread(TOP)
    stage(0)

    @pl.when(r > 0)
    def _():
        g[ZERO, c] = jnp.where(moved_ref[1:2, :] > 0.5, dot_pick(l_in[0], put_one_ref[...]), panels_ref[:kc])
        spread(ZERO)

    stage(1)
    stage(2)

    for m in range(n_peer):
        diag_cross(m).wait_recv()
        if m:
            diag_peer(m).wait_recv()
    whole = jnp.where(iota((PW, PW), 0) < iota((PW, PW), 1), g_diag[...].reshape(PW, PW), 0.0)
    lanes = iota((SMALL, PW), 1)
    small = jnp.zeros((SMALL, PW), F32)
    for b in range(PW // SMALL):
        small += jnp.where(lanes // SMALL == b, whole[b * SMALL : (b + 1) * SMALL], 0.0)

    def spaced(small):
        same = iota((PW, PW), 0) // SMALL == iota((PW, PW), 1) // SMALL
        return split(jnp.where(same, jnp.concatenate([small] * (PW // SMALL), 0), 0.0))

    power = dot_split(split(small), spaced(small))
    stage(3)
    small = one_hot(lanes % SMALL == iota((SMALL, PW), 0)) - small
    span = 2
    while span < SMALL:
        last_one = 2 * span >= SMALL
        new = dot_split(split(small if last_one else jnp.concatenate([small, power], 0)), spaced(power))
        small = small + new[:SMALL]
        power = new[SMALL:]
        span *= 2
        stage(span.bit_length() + 1)
    share(TOP)

    same = iota((PW, PW), 0) // SMALL == iota((PW, PW), 1) // SMALL
    inverse = jnp.where(same, jnp.concatenate([small] * (PW // SMALL), 0), 0.0)
    size = SMALL
    while size < PW:
        pairs = PW // (2 * size)
        pair_lanes = iota((size, PW), 1) // (2 * size)

        def fold(a):
            return sum(a[2 * size * i : 2 * size * i + size] for i in range(pairs))

        def unfold(a):
            empty = jnp.zeros((size, PW), F32)
            return jnp.concatenate([x for i in range(pairs) for x in (jnp.where(pair_lanes == i, a, 0.0), empty)], 0)

        other = (iota((size, PW), 1) // size) % 2 == 1
        beside = sum(
            jnp.where(other & (pair_lanes == i), whole[2 * size * i : 2 * size * i + size], 0.0) for i in range(pairs)
        )
        right = dot_split(split(beside), split(inverse))
        inverse = inverse - unfold(dot_split(split(fold(inverse)), split(unfold(right))))
        size *= 2
    for k in range(8, chunks + LAG):
        stage(k)
    inverse_ref[p] = inverse
    inverse_copy.start()

    def settle_rows(at):
        block_t[at] = jnp.where(moved_ref[0:1, :] > 0.5, dot_pick(f_in[0, at], put_ref[...]), block_t[at])

    @pl.when(r > 0)
    def _():
        share(ZERO)
        share(ONE)

    @pl.when(is_middle)
    def _():
        settle_rows(slice(0, cols))

    @pl.when(r > 0)
    def _():
        for kind, at in ((ZERO, 0), (ONE, PW)):
            settle(kind)
            high, low = split(g[kind].reshape(PW, rows))
            low_high[at : at + PW] = high
            low_low[at : at + PW] = low

    settle(TOP)
    above = split(g_top[...].reshape(PW, PW))
    inverse_copy.wait_recv()
    inverses = [split(inverse_ref[0]), split(inverse_ref[1])]

    for half in range(2):
        mine = range(half * chunks // 2, (half + 1) * chunks // 2)
        at = slice(mine[0] * PART, (mine[-1] + 1) * PART)

        @pl.when(is_first)
        def _():
            for k in mine:
                f_copy(k, 1).wait_recv()

        @pl.when(is_last)
        def _():
            for k in mine:
                f_copy(k, 0).wait_recv()
            settle_rows(at)

        top = jnp.where(q < start_f, f_in[0, at], jnp.where(from_here(q), own_ref[at], f_in[1, at]))
        upper0 = dot_split(split(top[:, :PW]), inverses[0])
        upper1 = dot_split(split(top[:, PW:] - dot_split(split(upper0), above)), inverses[1])
        upper = jnp.concatenate([upper0, upper1], 1)

        @pl.when(is_first)
        def _():
            out_ref[:, at] = upper.T

        @pl.when(r > 0)
        def _():
            out_ref[:, at] = (block_t[at] - dot_split(split(upper), (low_high[...], low_low[...]))).T

    @pl.when(r > 0)
    def _():
        drain(ZERO)
        drain(ONE)

    for m in range(n_peer):
        diag_cross(m).wait_send()
        if m:
            diag_peer(m).wait_send()
    inverse_copy.wait_send()
    drain(TOP)

    @pl.when(r < last)
    def _():
        diag_copy.wait_send()

    for d in range(2):
        @pl.when((r < last) if d == 0 else (r > 0))
        def _():
            l_copy(d).wait_send()
            for k in range(chunks):
                f_copy(k, d).wait_send()


def fused(block, panels, pivots):
    n_row, n_col = lax.axis_size("row"), lax.axis_size("col")
    rows, cols = block.shape
    kc = panels.shape[2]
    tops = 2 * PW
    vmem = pl.BlockSpec(memory_space=pltpu.VMEM)
    n_peer = n_col // 2
    dma = pltpu.SemaphoreType.DMA
    lists = jnp.pad(pivots.astype(F32), ((0, 6), (0, rows - PW)))
    packed = jnp.concatenate([jnp.swapaxes(panels, 1, 2).reshape(2 * kc, rows), lists], 0)
    return pl.pallas_call(
        functools.partial(kernel, n_row, n_col),
        out_shape=jax.ShapeDtypeStruct((rows, cols), F32),
        in_specs=[vmem] * 2,
        out_specs=vmem,
        scratch_shapes=[
            pltpu.VMEM((2, kc, PW), F32),
            pltpu.VMEM((n_col, kc, PW), F32),
            pltpu.VMEM((2, n_col, kc, rows), F32),
            pltpu.VMEM((n_col, kc, PW), F32),
            pltpu.VMEM((cols, tops), F32),
            pltpu.VMEM((2, cols, tops), F32),
            pltpu.VMEM((2, cols, tops), F32),
            pltpu.VMEM((2, kc, PW), F32),
            pltpu.VMEM((2, kc, PW), F32),
            pltpu.VMEM((2, PW, PW), F32),
            pltpu.VMEM((cols, rows), F32),
            pltpu.VMEM((8, rows), F32),
            pltpu.VMEM((tops, rows), BF16),
            pltpu.VMEM((PW, rows), BF16),
            pltpu.VMEM((8, rows), F32),
            pltpu.VMEM((tops, rows), BF16),
            pltpu.VMEM((tops, rows), BF16),
            dma((2,)),
            dma((2,)),
            dma((2, 2)),
            dma((2, 2, cols // PART)),
        ]
        + [dma((4, n_peer))] * 4,
        compiler_params=pltpu.CompilerParams(
            collective_id=0, has_side_effects=True, vmem_limit_bytes=48 * 1024 * 1024
        ),
    )(block, packed)


def body(block, panels, pivots):
    kc = panels.shape[2]
    fits = (
        block.shape[0] == 2 * PW
        and block.shape[1] % 128 == 0
        and kc % 8 == 0
        and lax.axis_size("col") % 2 == 0
        and lax.axis_size("row") > 1
    )
    return fused(block, panels, pivots) if fits else plain(block, panels, pivots)


def solution(mesh):
    return jax.shard_map(
        body,
        mesh=mesh,
        in_specs=(P("row", "col"), P(None, "row", "col"), P()),
        out_specs=P("row", "col"),
        check_vma=False,
    )
```

```python
import functools

import jax
import jax.numpy as jnp
from jax import lax
from jax.experimental import pallas as pl
from jax.experimental.pallas import tpu as pltpu
from jax.sharding import PartitionSpec as P

PW = 256


def swap_order(piv_row, offset, count):
    own = offset + jnp.arange(piv_row.shape[0], dtype=jnp.int32)
    base = jnp.arange(count, dtype=jnp.int32)
    return base.at[own].set(piv_row).at[piv_row].set(own)


def pick_rows(data, perm, targets, start):
    local_src = perm[targets] - start
    owned = (local_src >= 0) & (local_src < data.shape[0])
    taken = jnp.take(data, jnp.clip(local_src, 0, data.shape[0] - 1), axis=0)
    return jnp.where(owned[:, None], taken, 0.0)


def place_rows(data, targets, values, start):
    local_dst = targets - start
    inside = (local_dst >= 0) & (local_dst < data.shape[0])
    where_to = jnp.where(inside, local_dst, data.shape[0])
    return data.at[where_to].set(values, mode="drop")


def solve_top(diag_rows, rows):
    strict = jnp.tril(diag_rows, -1)
    inverse = jnp.eye(PW, dtype=jnp.float32) - strict
    power = strict
    for level in range(1, PW.bit_length() - 1):
        power = jnp.dot(
            power, power, precision=lax.Precision.HIGHEST, preferred_element_type=jnp.float32
        )
        inverse = inverse + jnp.dot(
            inverse, power, precision=lax.Precision.HIGHEST, preferred_element_type=jnp.float32
        )
    return jnp.dot(
        inverse, rows, precision=lax.Precision.HIGHEST, preferred_element_type=jnp.float32
    )


def finish(work, lower, offset, start, upper):
    product = jnp.dot(
        lower, upper, precision=lax.Precision.HIGHEST, preferred_element_type=jnp.float32
    )
    global_rows = start + jnp.arange(work.shape[0], dtype=jnp.int32)
    work = jnp.where((global_rows >= offset + PW)[:, None], work - product, work)
    placed = work.at[offset : offset + PW].set(upper)
    in_top = (global_rows >= offset) & (global_rows < offset + PW)
    return jnp.where(in_top[:, None], placed, work)


def plain(block, panels, pivots):
    rows_here = block.shape[0]
    rows_all = rows_here * lax.axis_size("row")
    start = lax.axis_index("row") * rows_here
    identity_perm = jnp.arange(rows_all, dtype=jnp.int32)
    perms = [swap_order(pivots[panel], panel * PW, rows_all) for panel in range(2)]
    targets = [
        jnp.concatenate([jnp.arange(panel * PW, panel * PW + PW, dtype=jnp.int32), pivots[panel]])
        for panel in range(2)
    ]
    tops_index = [jnp.arange(panel * PW, panel * PW + PW, dtype=jnp.int32) for panel in range(2)]
    work = block
    lowers = lax.all_gather(panels, "col", axis=2, tiled=True)
    for panel in range(2):
        offset = panel * PW
        diag_rows = pick_rows(lowers[panel], identity_perm, tops_index[panel], start)
        picked = pick_rows(work, perms[panel], targets[panel], start)
        moved, diag_all = lax.psum((picked, diag_rows), "row")
        work = place_rows(work, targets[panel], moved, start)
        upper = solve_top(diag_all, moved[:PW])
        work = finish(work, lowers[panel], offset, start, upper)
    return work

MESH = pl.DeviceIdType.MESH
F32, BF16 = jnp.float32, jnp.bfloat16
SMALL = 32
PART = 32
LAG = 2
ONE, ZERO, TOP, DIAG = range(4)


def dot(a, b):
    return jnp.dot(a, b, preferred_element_type=F32)


def split(a):
    high = a.astype(BF16)
    return high, (a - high.astype(F32)).astype(BF16)


def dot_split(a, b):
    m = a[0].shape[0]
    both = dot(jnp.concatenate(a, 0), b[0])
    return both[:m] + (both[m:] + dot(a[0], b[1]))


def dot_pick(a, one_hot):
    m = a.shape[0]
    out = dot(jnp.concatenate(split(a), 0), one_hot)
    return out[:m] + out[m:]


def iota(shape, dim):
    return lax.broadcasted_iota(jnp.int32, shape, dim)


def one_hot(condition):
    return jnp.where(condition, 1.0, 0.0)


def kernel(
    n_row, n_col, block_ref, panels_ref, out_ref, d_from, g_diag,
    g, g_top, own_ref, f_in, f_out, l_in, l_out, inverse_ref,
    block_t, local_ref, put_ref, put_one_ref, moved_ref, low_high, low_low,
    d_sem, i_sem, l_sem, f_sem, peer_send, peer_recv, sib_send, sib_recv,
):
    r, c = lax.axis_index("row"), lax.axis_index("col")
    rows, cols = block_ref.shape
    tops = 2 * PW
    kc = g_top.shape[1]
    n_peer = n_col // 2
    chunks = cols // PART
    last = n_row - 1
    p = c % 2
    sibling = c + 1 - 2 * p
    is_first, is_last = r == 0, r == last
    is_middle = (r > 0) & (r < last)
    is_upper = 2 * r >= n_row
    start = r * rows

    barrier = pltpu.get_barrier_semaphore()

    def greet(row):
        pl.semaphore_signal(barrier, 1, device_id={"row": row}, device_id_type=MESH)

    @pl.when(is_first)
    def _():
        for row in range(1, n_row):
            greet(row)

    @pl.when(r > 0)
    def _():
        greet(0)

    @pl.when(r > 1)
    def _():
        greet(r - 1)

    @pl.when((r > 0) & (r < last))
    def _():
        greet(r + 1)

    for m in range(1, n_col):
        pl.semaphore_signal(barrier, 1, device_id={"col": (c + m) % n_col}, device_id_type=MESH)

    first = panels_ref[2 * kc : 2 * kc + 1, :PW]
    second = panels_ref[2 * kc + 1 : 2 * kc + 2, :PW]
    sub, lane = iota((PW, PW), 0).astype(F32), iota((PW, PW), 1).astype(F32)

    def upright(v):
        return jnp.sum(jnp.where(sub == lane, v, 0.0), axis=1, keepdims=True)

    first_c = upright(first)
    lane_row = lane[0:1, :]
    sub_col = sub[:, 0:1]

    def lookup(match, found, otherwise, axis):
        hit = jnp.sum(one_hot(match), axis=axis, keepdims=True)
        return jnp.sum(jnp.where(match, found, 0.0), axis=axis, keepdims=True) + jnp.where(hit > 0.5, 0.0, otherwise)

    q_second = lookup(first_c == second, sub, second, 0)
    q = jnp.concatenate([first, q_second], 1)
    start_f = start.astype(F32)
    local_ref[0:1, :] = q - start_f
    local_ref[1:2, :PW] = second - start_f

    @pl.when(is_first)
    def _():
        second_c = upright(second)
        home = lookup(first_c == lane + PW, sub, lane_row + PW, 0)
        home_c = lookup(first == sub + PW, lane, sub_col + PW, 1)
        out_first = jnp.where(first < tops, first, lookup(second_c == first, home_c, lane_row, 0))
        out_second = jnp.where(q_second < tops, q_second, home)
        local_ref[0:1, :] = jnp.concatenate([out_first, out_second], 1)
        local_ref[1:2, :PW] = lane_row + PW

    def from_here(v):
        return (v >= start_f) & (v < start_f + rows)

    @pl.when(is_first)
    def _():
        d_from[0] = panels_ref[:kc, :PW]
        d_from[1] = panels_ref[kc : 2 * kc, PW:tops]

    @pl.when(r > 0)
    def _():
        g[ONE, c] = panels_ref[kc : 2 * kc]

    greeted = n_col + jnp.where(r > 1, 1, 0) + jnp.where(r < last, 1, 0)
    pl.semaphore_wait(barrier, jnp.where(is_first, n_col + n_row - 2, greeted))

    def l_copy(d):
        return pltpu.make_async_remote_copy(
            src_ref=l_out.at[d], dst_ref=l_in.at[d], send_sem=l_sem.at[0, d], recv_sem=l_sem.at[1, d],
            device_id={"row": r + 1 - 2 * d}, device_id_type=MESH,
        )

    def f_copy(k, d):
        at = pl.ds(k * PART, PART)
        return pltpu.make_async_remote_copy(
            src_ref=f_out.at[d, at], dst_ref=f_in.at[d, at],
            send_sem=f_sem.at[0, d, k], recv_sem=f_sem.at[1, d, k],
            device_id={"row": r + 1 - 2 * d}, device_id_type=MESH,
        )

    def diag_copy(row):
        return pltpu.make_async_remote_copy(
            src_ref=d_from, dst_ref=d_from, send_sem=d_sem.at[0, row], recv_sem=d_sem.at[1, 0],
            device_id={"row": row}, device_id_type=MESH,
        )

    def arrives(d):
        return jnp.where(d == 0, r > 0, r < last)

    def l_step(d):
        @pl.when(arrives(d))
        def _():
            l_copy(d).wait_recv()

        @pl.when(is_middle)
        def _():
            l_out[d] = jnp.where(from_here(second), l_out[d], l_in[d])
            l_copy(d).start()

    def f_step(k, d):
        at = pl.ds(k * PART, PART)
        f_copy(k, d).wait_recv()
        f_out[d, at, :] = jnp.where(from_here(q), f_out[d, at, :], f_in[d, at, :])
        f_copy(k, d).start()

    def stage(k):
        upper = jnp.where(is_upper, 1, 0)
        near, far = k < chunks, 0 <= k - LAG < chunks
        if near or far:
            @pl.when(is_middle)
            def _():
                if near:
                    f_step(k, upper)
                if far:
                    f_step(k - LAG, 1 - upper)

    def slot_ref(kind, slot):
        return g_top.at[slot] if kind == TOP else g.at[kind, slot]

    def peer_copy(kind, m, slot):
        return pltpu.make_async_remote_copy(
            src_ref=slot_ref(kind, slot), dst_ref=slot_ref(kind, slot),
            send_sem=peer_send.at[kind, m], recv_sem=peer_recv.at[kind, m],
            device_id={"col": (c + 2 * m) % n_col}, device_id_type=MESH,
        )

    def sib_copy(kind, m, slot):
        return pltpu.make_async_remote_copy(
            src_ref=slot_ref(kind, slot), dst_ref=slot_ref(kind, slot),
            send_sem=sib_send.at[kind, m], recv_sem=sib_recv.at[kind, m],
            device_id={"col": sibling}, device_id_type=MESH,
        )

    def spread(kind):
        for m in range(1, n_peer):
            peer_copy(kind, m, c).start()
        sib_copy(kind, 0, c).start()

    def diag_peer(m):
        return pltpu.make_async_remote_copy(
            src_ref=d_from.at[p], dst_ref=g_diag.at[c],
            send_sem=peer_send.at[DIAG, m], recv_sem=peer_recv.at[DIAG, m],
            device_id={"col": (c + 2 * m) % n_col}, device_id_type=MESH,
        )

    def diag_cross(m):
        return pltpu.make_async_remote_copy(
            src_ref=d_from.at[1 - p], dst_ref=g_diag.at[c],
            send_sem=sib_send.at[DIAG, m], recv_sem=sib_recv.at[DIAG, m],
            device_id={"col": (sibling + 2 * m) % n_col}, device_id_type=MESH,
        )

    def spread_diag():
        for m in range(n_peer - 1, 0, -1):
            diag_peer(m).start()
            diag_cross(m).start()
        diag_cross(0).start()
        g_diag[c] = d_from[p]

    inverse_copy = pltpu.make_async_remote_copy(
        src_ref=inverse_ref.at[p], dst_ref=inverse_ref.at[p], send_sem=i_sem.at[0], recv_sem=i_sem.at[1],
        device_id={"col": sibling}, device_id_type=MESH,
    )

    def share(kind):
        for m in range(1, n_peer):
            slot = (c + n_col - 2 * m) % n_col
            peer_copy(kind, m, slot).wait_recv()
            sib_copy(kind, m, slot).start()

    def settle(kind):
        for m in range(n_peer):
            sib_copy(kind, m, (sibling + n_col - 2 * m) % n_col).wait_recv()

    def drain(kind):
        for m in range(1, n_peer):
            peer_copy(kind, m, c).wait_send()
        for m in range(n_peer):
            sib_copy(kind, m, c).wait_send()

    @pl.when(is_first)
    def _():
        for row in range(last, 0, -1):
            diag_copy(row).start()
        spread_diag()

    @pl.when(r > 0)
    def _():
        spread(ONE)

    own_top = dot_pick(panels_ref[:kc], one_hot(iota((rows, PW), 0).astype(F32) == local_ref[1:2, :PW]).astype(BF16))
    l_out[0] = own_top
    l_out[1] = own_top

    @pl.when(is_first)
    def _():
        l_copy(0).start()

    @pl.when(is_last)
    def _():
        l_copy(1).start()

    block_t[...] = block_ref[...].T
    own = dot_pick(block_t[...], one_hot(iota((rows, tops), 0).astype(F32) == local_ref[0:1, :]).astype(BF16))
    own_ref[...] = own
    f_out[0] = own
    f_out[1] = own

    @pl.when(is_first)
    def _():
        for k in range(chunks):
            f_copy(k, 0).start()

    @pl.when(is_last)
    def _():
        for k in range(chunks):
            f_copy(k, 1).start()

    @pl.when(r > 0)
    def _():
        diag_copy(1).wait_recv()
        spread_diag()

        second_c = upright(second)
        q_c = jnp.concatenate([first_c, lookup(second_c == first, lane, second_c, 1)], 0)
        put = one_hot(iota((PW, rows), 1).astype(F32) == second_c - start_f)
        put_one_ref[...] = put.astype(BF16)
        moved_ref[1:2, :] = jnp.sum(put, axis=0, keepdims=True)
        put = one_hot(iota((tops, rows), 1).astype(F32) == q_c - start_f)
        put_ref[...] = put.astype(BF16)
        moved_ref[0:1, :] = jnp.sum(put, axis=0, keepdims=True)

    @pl.when(is_upper)
    def _():
        l_step(1)

    l_step(0)

    @pl.when(jnp.logical_not(is_upper))
    def _():
        l_step(1)

    top_rows = jnp.where(second < start_f, l_in[0], jnp.where(from_here(second), own_top, l_in[1]))
    g_top[c] = top_rows
    spread(TOP)
    stage(0)

    @pl.when(r > 0)
    def _():
        g[ZERO, c] = jnp.where(moved_ref[1:2, :] > 0.5, dot_pick(l_in[0], put_one_ref[...]), panels_ref[:kc])
        spread(ZERO)

    stage(1)
    stage(2)

    for m in range(n_peer):
        diag_cross(m).wait_recv()
        if m:
            diag_peer(m).wait_recv()
    whole = jnp.where(iota((PW, PW), 0) < iota((PW, PW), 1), g_diag[...].reshape(PW, PW), 0.0)
    lanes = iota((SMALL, PW), 1)
    small = jnp.zeros((SMALL, PW), F32)
    for b in range(PW // SMALL):
        small += jnp.where(lanes // SMALL == b, whole[b * SMALL : (b + 1) * SMALL], 0.0)

    def spaced(small):
        same = iota((PW, PW), 0) // SMALL == iota((PW, PW), 1) // SMALL
        return split(jnp.where(same, jnp.concatenate([small] * (PW // SMALL), 0), 0.0))

    power = dot_split(split(small), spaced(small))
    stage(3)
    small = one_hot(lanes % SMALL == iota((SMALL, PW), 0)) - small
    span = 2
    while span < SMALL:
        last_one = 2 * span >= SMALL
        new = dot_split(split(small if last_one else jnp.concatenate([small, power], 0)), spaced(power))
        small = small + new[:SMALL]
        power = new[SMALL:]
        span *= 2
        stage(span.bit_length() + 1)
    share(TOP)

    same = iota((PW, PW), 0) // SMALL == iota((PW, PW), 1) // SMALL
    inverse = jnp.where(same, jnp.concatenate([small] * (PW // SMALL), 0), 0.0)
    size = SMALL
    while size < PW:
        pairs = PW // (2 * size)
        pair_lanes = iota((size, PW), 1) // (2 * size)

        def fold(a):
            return sum(a[2 * size * i : 2 * size * i + size] for i in range(pairs))

        def unfold(a):
            empty = jnp.zeros((size, PW), F32)
            return jnp.concatenate([x for i in range(pairs) for x in (jnp.where(pair_lanes == i, a, 0.0), empty)], 0)

        other = (iota((size, PW), 1) // size) % 2 == 1
        beside = sum(
            jnp.where(other & (pair_lanes == i), whole[2 * size * i : 2 * size * i + size], 0.0) for i in range(pairs)
        )
        right = dot_split(split(beside), split(inverse))
        inverse = inverse - unfold(dot_split(split(fold(inverse)), split(unfold(right))))
        size *= 2
    for k in range(8, chunks + LAG):
        stage(k)
    inverse_ref[p] = inverse
    inverse_copy.start()

    def settle_rows(at):
        block_t[at] = jnp.where(moved_ref[0:1, :] > 0.5, dot_pick(f_in[0, at], put_ref[...]), block_t[at])

    @pl.when(r > 0)
    def _():
        share(ZERO)
        share(ONE)

    @pl.when(is_middle)
    def _():
        settle_rows(slice(0, cols))

    @pl.when(r > 0)
    def _():
        for kind, at in ((ZERO, 0), (ONE, PW)):
            settle(kind)
            high, low = split(g[kind].reshape(PW, rows))
            low_high[at : at + PW] = high
            low_low[at : at + PW] = low

    settle(TOP)
    above = split(g_top[...].reshape(PW, PW))
    inverse_copy.wait_recv()
    inverses = [split(inverse_ref[0]), split(inverse_ref[1])]

    for half in range(2):
        mine = range(half * chunks // 2, (half + 1) * chunks // 2)
        at = slice(mine[0] * PART, (mine[-1] + 1) * PART)

        @pl.when(is_first)
        def _():
            for k in mine:
                f_copy(k, 1).wait_recv()

        @pl.when(is_last)
        def _():
            for k in mine:
                f_copy(k, 0).wait_recv()
            settle_rows(at)

        top = jnp.where(q < start_f, f_in[0, at], jnp.where(from_here(q), own_ref[at], f_in[1, at]))
        upper0 = dot_split(split(top[:, :PW]), inverses[0])
        upper1 = dot_split(split(top[:, PW:] - dot_split(split(upper0), above)), inverses[1])
        upper = jnp.concatenate([upper0, upper1], 1)

        @pl.when(is_first)
        def _():
            out_ref[:, at] = upper.T

        @pl.when(r > 0)
        def _():
            out_ref[:, at] = (block_t[at] - dot_split(split(upper), (low_high[...], low_low[...]))).T

    @pl.when(r > 0)
    def _():
        drain(ZERO)
        drain(ONE)

    for m in range(n_peer):
        diag_cross(m).wait_send()
        if m:
            diag_peer(m).wait_send()
    inverse_copy.wait_send()
    drain(TOP)

    @pl.when(is_first)
    def _():
        for row in range(1, n_row):
            diag_copy(row).wait_send()

    for d in range(2):
        @pl.when((r < last) if d == 0 else (r > 0))
        def _():
            l_copy(d).wait_send()
            for k in range(chunks):
                f_copy(k, d).wait_send()


def fused(block, panels, pivots):
    n_row, n_col = lax.axis_size("row"), lax.axis_size("col")
    rows, cols = block.shape
    kc = panels.shape[2]
    tops = 2 * PW
    vmem = pl.BlockSpec(memory_space=pltpu.VMEM)
    n_peer = n_col // 2
    dma = pltpu.SemaphoreType.DMA
    lists = jnp.pad(pivots, ((0, 6), (0, rows - PW))).astype(F32)
    packed = jnp.concatenate([jnp.swapaxes(panels, 1, 2).reshape(2 * kc, rows), lists], 0)
    return pl.pallas_call(
        functools.partial(kernel, n_row, n_col),
        out_shape=jax.ShapeDtypeStruct((rows, cols), F32),
        in_specs=[vmem] * 2,
        out_specs=vmem,
        scratch_shapes=[
            pltpu.VMEM((2, kc, PW), F32),
            pltpu.VMEM((n_col, kc, PW), F32),
            pltpu.VMEM((2, n_col, kc, rows), F32),
            pltpu.VMEM((n_col, kc, PW), F32),
            pltpu.VMEM((cols, tops), F32),
            pltpu.VMEM((2, cols, tops), F32),
            pltpu.VMEM((2, cols, tops), F32),
            pltpu.VMEM((2, kc, PW), F32),
            pltpu.VMEM((2, kc, PW), F32),
            pltpu.VMEM((2, PW, PW), F32),
            pltpu.VMEM((cols, rows), F32),
            pltpu.VMEM((8, rows), F32),
            pltpu.VMEM((tops, rows), BF16),
            pltpu.VMEM((PW, rows), BF16),
            pltpu.VMEM((8, rows), F32),
            pltpu.VMEM((tops, rows), BF16),
            pltpu.VMEM((tops, rows), BF16),
            dma((2, n_row)),
            dma((2,)),
            dma((2, 2)),
            dma((2, 2, cols // PART)),
        ]
        + [dma((4, n_peer))] * 4,
        compiler_params=pltpu.CompilerParams(
            collective_id=0, has_side_effects=True, vmem_limit_bytes=48 * 1024 * 1024
        ),
    )(block, packed)


def body(block, panels, pivots):
    kc = panels.shape[2]
    fits = (
        block.shape[0] == 2 * PW
        and block.shape[1] % 128 == 0
        and kc % 8 == 0
        and lax.axis_size("col") % 2 == 0
        and lax.axis_size("row") > 1
    )
    return fused(block, panels, pivots) if fits else plain(block, panels, pivots)


def solution(mesh):
    return jax.shard_map(
        body,
        mesh=mesh,
        in_specs=(P("row", "col"), P(None, "row", "col"), P()),
        out_specs=P("row", "col"),
        check_vma=False,
    )
```

```python
import functools

import jax
import jax.numpy as jnp
from jax import lax
from jax.experimental import pallas as pl
from jax.experimental.pallas import tpu as pltpu
from jax.sharding import PartitionSpec as P

PW = 256


def swap_order(piv_row, offset, count):
    own = offset + jnp.arange(piv_row.shape[0], dtype=jnp.int32)
    base = jnp.arange(count, dtype=jnp.int32)
    return base.at[own].set(piv_row).at[piv_row].set(own)


def pick_rows(data, perm, targets, start):
    local_src = perm[targets] - start
    owned = (local_src >= 0) & (local_src < data.shape[0])
    taken = jnp.take(data, jnp.clip(local_src, 0, data.shape[0] - 1), axis=0)
    return jnp.where(owned[:, None], taken, 0.0)


def place_rows(data, targets, values, start):
    local_dst = targets - start
    inside = (local_dst >= 0) & (local_dst < data.shape[0])
    where_to = jnp.where(inside, local_dst, data.shape[0])
    return data.at[where_to].set(values, mode="drop")


def solve_top(diag_rows, rows):
    strict = jnp.tril(diag_rows, -1)
    inverse = jnp.eye(PW, dtype=jnp.float32) - strict
    power = strict
    for level in range(1, PW.bit_length() - 1):
        power = jnp.dot(
            power, power, precision=lax.Precision.HIGHEST, preferred_element_type=jnp.float32
        )
        inverse = inverse + jnp.dot(
            inverse, power, precision=lax.Precision.HIGHEST, preferred_element_type=jnp.float32
        )
    return jnp.dot(
        inverse, rows, precision=lax.Precision.HIGHEST, preferred_element_type=jnp.float32
    )


def finish(work, lower, offset, start, upper):
    product = jnp.dot(
        lower, upper, precision=lax.Precision.HIGHEST, preferred_element_type=jnp.float32
    )
    global_rows = start + jnp.arange(work.shape[0], dtype=jnp.int32)
    work = jnp.where((global_rows >= offset + PW)[:, None], work - product, work)
    placed = work.at[offset : offset + PW].set(upper)
    in_top = (global_rows >= offset) & (global_rows < offset + PW)
    return jnp.where(in_top[:, None], placed, work)


def plain(block, panels, pivots):
    rows_here = block.shape[0]
    rows_all = rows_here * lax.axis_size("row")
    start = lax.axis_index("row") * rows_here
    identity_perm = jnp.arange(rows_all, dtype=jnp.int32)
    perms = [swap_order(pivots[panel], panel * PW, rows_all) for panel in range(2)]
    targets = [
        jnp.concatenate([jnp.arange(panel * PW, panel * PW + PW, dtype=jnp.int32), pivots[panel]])
        for panel in range(2)
    ]
    tops_index = [jnp.arange(panel * PW, panel * PW + PW, dtype=jnp.int32) for panel in range(2)]
    work = block
    lowers = lax.all_gather(panels, "col", axis=2, tiled=True)
    for panel in range(2):
        offset = panel * PW
        diag_rows = pick_rows(lowers[panel], identity_perm, tops_index[panel], start)
        picked = pick_rows(work, perms[panel], targets[panel], start)
        moved, diag_all = lax.psum((picked, diag_rows), "row")
        work = place_rows(work, targets[panel], moved, start)
        upper = solve_top(diag_all, moved[:PW])
        work = finish(work, lowers[panel], offset, start, upper)
    return work

MESH = pl.DeviceIdType.MESH
F32, BF16 = jnp.float32, jnp.bfloat16
SMALL = 32
PART = 32
LAG = 2
ONE, ZERO, TOP, DIAG = range(4)


def dot(a, b):
    return jnp.dot(a, b, preferred_element_type=F32)


def split(a):
    high = a.astype(BF16)
    return high, (a - high.astype(F32)).astype(BF16)


def dot_split(a, b):
    m = a[0].shape[0]
    both = dot(jnp.concatenate(a, 0), b[0])
    return both[:m] + (both[m:] + dot(a[0], b[1]))


def dot_pick(a, one_hot):
    m = a.shape[0]
    out = dot(jnp.concatenate(split(a), 0), one_hot)
    return out[:m] + out[m:]


def iota(shape, dim):
    return lax.broadcasted_iota(jnp.int32, shape, dim)


def one_hot(condition):
    return jnp.where(condition, 1.0, 0.0)


def kernel(
    n_row, n_col, block_ref, panels_ref, out_ref, d_from, g_diag,
    g, g_top, own_ref, f_in, f_out, l_in, l_out, inverse_ref,
    block_t, local_ref, put_ref, put_one_ref, moved_ref, low_high, low_low,
    d_sem, i_sem, l_sem, f_sem, peer_send, peer_recv, sib_send, sib_recv,
):
    r, c = lax.axis_index("row"), lax.axis_index("col")
    rows, cols = block_ref.shape
    tops = 2 * PW
    kc = g_top.shape[1]
    n_peer = n_col // 2
    chunks = cols // PART
    last = n_row - 1
    p = c % 2
    sibling = c + 1 - 2 * p
    is_first, is_last = r == 0, r == last
    is_middle = (r > 0) & (r < last)
    is_upper = 2 * r >= n_row
    start = r * rows

    barrier = pltpu.get_barrier_semaphore()

    @pl.when(r > 0)
    def _():
        pl.semaphore_signal(barrier, 1, device_id={"row": r - 1}, device_id_type=MESH)

    @pl.when(r < last)
    def _():
        pl.semaphore_signal(barrier, 1, device_id={"row": r + 1}, device_id_type=MESH)

    for m in range(1, n_col):
        pl.semaphore_signal(barrier, 1, device_id={"col": (c + m) % n_col}, device_id_type=MESH)

    first = panels_ref[2 * kc : 2 * kc + 1, :PW]
    second = panels_ref[2 * kc + 1 : 2 * kc + 2, :PW]
    sub, lane = iota((PW, PW), 0).astype(F32), iota((PW, PW), 1).astype(F32)

    def upright(v):
        return jnp.sum(jnp.where(sub == lane, v, 0.0), axis=1, keepdims=True)

    first_c = upright(first)
    lane_row = lane[0:1, :]
    sub_col = sub[:, 0:1]

    def lookup(match, found, otherwise, axis):
        hit = jnp.sum(one_hot(match), axis=axis, keepdims=True)
        return jnp.sum(jnp.where(match, found, 0.0), axis=axis, keepdims=True) + jnp.where(hit > 0.5, 0.0, otherwise)

    q_second = lookup(first_c == second, sub, second, 0)
    q = jnp.concatenate([first, q_second], 1)
    start_f = start.astype(F32)
    local_ref[0:1, :] = q - start_f
    local_ref[1:2, :PW] = second - start_f

    @pl.when(is_first)
    def _():
        second_c = upright(second)
        home = lookup(first_c == lane + PW, sub, lane_row + PW, 0)
        home_c = lookup(first == sub + PW, lane, sub_col + PW, 1)
        out_first = jnp.where(first < tops, first, lookup(second_c == first, home_c, lane_row, 0))
        out_second = jnp.where(q_second < tops, q_second, home)
        local_ref[0:1, :] = jnp.concatenate([out_first, out_second], 1)
        local_ref[1:2, :PW] = lane_row + PW

    def from_here(v):
        return (v >= start_f) & (v < start_f + rows)

    @pl.when(is_first)
    def _():
        d_from[0] = panels_ref[:kc, :PW]
        d_from[1] = panels_ref[kc : 2 * kc, PW:tops]

    @pl.when(r > 0)
    def _():
        g[ONE, c] = panels_ref[kc : 2 * kc]

    @pl.when(is_middle)
    def _():
        pl.semaphore_wait(barrier, n_col + 1)

    @pl.when(is_first | is_last)
    def _():
        pl.semaphore_wait(barrier, n_col)

    def l_copy(d):
        return pltpu.make_async_remote_copy(
            src_ref=l_out.at[d], dst_ref=l_in.at[d], send_sem=l_sem.at[0, d], recv_sem=l_sem.at[1, d],
            device_id={"row": r + 1 - 2 * d}, device_id_type=MESH,
        )

    def f_copy(k, d):
        at = pl.ds(k * PART, PART)
        return pltpu.make_async_remote_copy(
            src_ref=f_out.at[d, at], dst_ref=f_in.at[d, at],
            send_sem=f_sem.at[0, d, k], recv_sem=f_sem.at[1, d, k],
            device_id={"row": r + 1 - 2 * d}, device_id_type=MESH,
        )

    diag_copy = pltpu.make_async_remote_copy(
        src_ref=d_from, dst_ref=d_from, send_sem=d_sem.at[0], recv_sem=d_sem.at[1],
        device_id={"row": r + 1}, device_id_type=MESH,
    )

    def arrives(d):
        return jnp.where(d == 0, r > 0, r < last)

    def l_step(d):
        @pl.when(arrives(d))
        def _():
            l_copy(d).wait_recv()

        @pl.when(is_middle)
        def _():
            l_out[d] = jnp.where(from_here(second), l_out[d], l_in[d])
            l_copy(d).start()

    def f_step(k, d):
        at = pl.ds(k * PART, PART)
        f_copy(k, d).wait_recv()
        f_out[d, at, :] = jnp.where(from_here(q), f_out[d, at, :], f_in[d, at, :])
        f_copy(k, d).start()

    def stage(k):
        upper = jnp.where(is_upper, 1, 0)
        near, far = k < chunks, 0 <= k - LAG < chunks
        if near or far:
            @pl.when(is_middle)
            def _():
                if near:
                    f_step(k, upper)
                if far:
                    f_step(k - LAG, 1 - upper)

    def slot_ref(kind, slot):
        return g_top.at[slot] if kind == TOP else g.at[kind, slot]

    def peer_copy(kind, m, slot):
        return pltpu.make_async_remote_copy(
            src_ref=slot_ref(kind, slot), dst_ref=slot_ref(kind, slot),
            send_sem=peer_send.at[kind, m], recv_sem=peer_recv.at[kind, m],
            device_id={"col": (c + 2 * m) % n_col}, device_id_type=MESH,
        )

    def sib_copy(kind, m, slot):
        return pltpu.make_async_remote_copy(
            src_ref=slot_ref(kind, slot), dst_ref=slot_ref(kind, slot),
            send_sem=sib_send.at[kind, m], recv_sem=sib_recv.at[kind, m],
            device_id={"col": sibling}, device_id_type=MESH,
        )

    def spread(kind):
        for m in range(1, n_peer):
            peer_copy(kind, m, c).start()
        sib_copy(kind, 0, c).start()

    def diag_peer(m):
        return pltpu.make_async_remote_copy(
            src_ref=d_from.at[p], dst_ref=g_diag.at[c],
            send_sem=peer_send.at[DIAG, m], recv_sem=peer_recv.at[DIAG, m],
            device_id={"col": (c + 2 * m) % n_col}, device_id_type=MESH,
        )

    def diag_cross(m):
        return pltpu.make_async_remote_copy(
            src_ref=d_from.at[1 - p], dst_ref=g_diag.at[c],
            send_sem=sib_send.at[DIAG, m], recv_sem=sib_recv.at[DIAG, m],
            device_id={"col": (sibling + 2 * m) % n_col}, device_id_type=MESH,
        )

    def spread_diag():
        for m in range(n_peer - 1, 0, -1):
            diag_peer(m).start()
            diag_cross(m).start()
        diag_cross(0).start()
        g_diag[c] = d_from[p]

    inverse_copy = pltpu.make_async_remote_copy(
        src_ref=inverse_ref.at[p], dst_ref=inverse_ref.at[p], send_sem=i_sem.at[0], recv_sem=i_sem.at[1],
        device_id={"col": sibling}, device_id_type=MESH,
    )

    def share(kind):
        for m in range(1, n_peer):
            slot = (c + n_col - 2 * m) % n_col
            peer_copy(kind, m, slot).wait_recv()
            sib_copy(kind, m, slot).start()

    def settle(kind):
        for m in range(n_peer):
            sib_copy(kind, m, (sibling + n_col - 2 * m) % n_col).wait_recv()

    def drain(kind):
        for m in range(1, n_peer):
            peer_copy(kind, m, c).wait_send()
        for m in range(n_peer):
            sib_copy(kind, m, c).wait_send()

    @pl.when(is_first)
    def _():
        diag_copy.start()
        spread_diag()

    @pl.when(r > 0)
    def _():
        spread(ONE)

    own_top = dot_pick(panels_ref[:kc], one_hot(iota((rows, PW), 0).astype(F32) == local_ref[1:2, :PW]).astype(BF16))
    l_out[0] = own_top
    l_out[1] = own_top

    @pl.when(is_first)
    def _():
        l_copy(0).start()

    @pl.when(is_last)
    def _():
        l_copy(1).start()

    block_t[...] = block_ref[...].T
    own = dot_pick(block_t[...], one_hot(iota((rows, tops), 0).astype(F32) == local_ref[0:1, :]).astype(BF16))
    own_ref[...] = own
    f_out[0] = own
    f_out[1] = own

    @pl.when(is_first)
    def _():
        for k in range(chunks):
            f_copy(k, 0).start()

    @pl.when(is_last)
    def _():
        for k in range(chunks):
            f_copy(k, 1).start()

    def pass_diag():
        diag_copy.wait_recv()

        @pl.when(r < last)
        def _():
            diag_copy.start()

        spread_diag()

    @pl.when((r > 0) & jnp.logical_not(is_upper))
    def _():
        pass_diag()

    @pl.when(r > 0)
    def _():
        second_c = upright(second)
        q_c = jnp.concatenate([first_c, lookup(second_c == first, lane, second_c, 1)], 0)
        put = one_hot(iota((PW, rows), 1).astype(F32) == second_c - start_f)
        put_one_ref[...] = put.astype(BF16)
        moved_ref[1:2, :] = jnp.sum(put, axis=0, keepdims=True)
        put = one_hot(iota((tops, rows), 1).astype(F32) == q_c - start_f)
        put_ref[...] = put.astype(BF16)
        moved_ref[0:1, :] = jnp.sum(put, axis=0, keepdims=True)

    @pl.when(is_upper)
    def _():
        l_step(1)

    @pl.when(is_upper)
    def _():
        pass_diag()

    l_step(0)

    @pl.when(jnp.logical_not(is_upper))
    def _():
        l_step(1)

    top_rows = jnp.where(second < start_f, l_in[0], jnp.where(from_here(second), own_top, l_in[1]))
    g_top[c] = top_rows
    spread(TOP)
    stage(0)

    @pl.when(r > 0)
    def _():
        g[ZERO, c] = jnp.where(moved_ref[1:2, :] > 0.5, dot_pick(l_in[0], put_one_ref[...]), panels_ref[:kc])
        spread(ZERO)

    stage(1)
    stage(2)

    for m in range(n_peer):
        diag_cross(m).wait_recv()
        if m:
            diag_peer(m).wait_recv()
    whole = jnp.where(iota((PW, PW), 0) < iota((PW, PW), 1), g_diag[...].reshape(PW, PW), 0.0)
    lanes = iota((SMALL, PW), 1)
    small = jnp.zeros((SMALL, PW), F32)
    for b in range(PW // SMALL):
        small += jnp.where(lanes // SMALL == b, whole[b * SMALL : (b + 1) * SMALL], 0.0)

    def spaced(small):
        same = iota((PW, PW), 0) // SMALL == iota((PW, PW), 1) // SMALL
        return split(jnp.where(same, jnp.concatenate([small] * (PW // SMALL), 0), 0.0))

    power = dot_split(split(small), spaced(small))
    stage(3)
    small = one_hot(lanes % SMALL == iota((SMALL, PW), 0)) - small
    span = 2
    while span < SMALL:
        last_one = 2 * span >= SMALL
        new = dot_split(split(small if last_one else jnp.concatenate([small, power], 0)), spaced(power))
        small = small + new[:SMALL]
        power = new[SMALL:]
        span *= 2
        stage(span.bit_length() + 1)
    share(TOP)

    same = iota((PW, PW), 0) // SMALL == iota((PW, PW), 1) // SMALL
    inverse = jnp.where(same, jnp.concatenate([small] * (PW // SMALL), 0), 0.0)
    size = SMALL
    while size < PW:
        pairs = PW // (2 * size)
        pair_lanes = iota((size, PW), 1) // (2 * size)

        def fold(a):
            return sum(a[2 * size * i : 2 * size * i + size] for i in range(pairs))

        def unfold(a):
            empty = jnp.zeros((size, PW), F32)
            return jnp.concatenate([x for i in range(pairs) for x in (jnp.where(pair_lanes == i, a, 0.0), empty)], 0)

        other = (iota((size, PW), 1) // size) % 2 == 1
        beside = sum(
            jnp.where(other & (pair_lanes == i), whole[2 * size * i : 2 * size * i + size], 0.0) for i in range(pairs)
        )
        right = dot_split(split(beside), split(inverse))
        inverse = inverse - unfold(dot_split(split(fold(inverse)), split(unfold(right))))
        size *= 2
    for k in range(8, chunks + LAG):
        stage(k)
    inverse_ref[p] = inverse
    inverse_copy.start()

    def settle_rows(at):
        block_t[at] = jnp.where(moved_ref[0:1, :] > 0.5, dot_pick(f_in[0, at], put_ref[...]), block_t[at])

    @pl.when(r > 0)
    def _():
        share(ZERO)
        share(ONE)

    @pl.when(is_middle)
    def _():
        settle_rows(slice(0, cols))

    @pl.when(r > 0)
    def _():
        for kind, at in ((ZERO, 0), (ONE, PW)):
            settle(kind)
            high, low = split(g[kind].reshape(PW, rows))
            low_high[at : at + PW] = high
            low_low[at : at + PW] = low

    settle(TOP)
    above = split(g_top[...].reshape(PW, PW))
    inverse_copy.wait_recv()
    inverses = [split(inverse_ref[0]), split(inverse_ref[1])]

    def solve(at, mine):
        @pl.when(is_first)
        def _():
            for k in mine:
                f_copy(k, 1).wait_recv()

        @pl.when(is_last)
        def _():
            for k in mine:
                f_copy(k, 0).wait_recv()
            settle_rows(at)

        top = jnp.where(q < start_f, f_in[0, at], jnp.where(from_here(q), own_ref[at], f_in[1, at]))
        upper0 = dot_split(split(top[:, :PW]), inverses[0])
        upper1 = dot_split(split(top[:, PW:] - dot_split(split(upper0), above)), inverses[1])
        upper = jnp.concatenate([upper0, upper1], 1)

        @pl.when(is_first)
        def _():
            out_ref[:, at] = upper.T

        @pl.when(r > 0)
        def _():
            out_ref[:, at] = (block_t[at] - dot_split(split(upper), (low_high[...], low_low[...]))).T

    @pl.when(is_middle)
    def _():
        solve(slice(0, cols), range(0))

    @pl.when(is_first | is_last)
    def _():
        for half in range(2):
            mine = range(half * chunks // 2, (half + 1) * chunks // 2)
            solve(slice(mine[0] * PART, (mine[-1] + 1) * PART), mine)

    @pl.when(r > 0)
    def _():
        drain(ZERO)
        drain(ONE)

    for m in range(n_peer):
        diag_cross(m).wait_send()
        if m:
            diag_peer(m).wait_send()
    inverse_copy.wait_send()
    drain(TOP)

    @pl.when(r < last)
    def _():
        diag_copy.wait_send()

    for d in range(2):
        @pl.when((r < last) if d == 0 else (r > 0))
        def _():
            l_copy(d).wait_send()
            for k in range(chunks):
                f_copy(k, d).wait_send()


def fused(block, panels, pivots):
    n_row, n_col = lax.axis_size("row"), lax.axis_size("col")
    rows, cols = block.shape
    kc = panels.shape[2]
    tops = 2 * PW
    vmem = pl.BlockSpec(memory_space=pltpu.VMEM)
    n_peer = n_col // 2
    dma = pltpu.SemaphoreType.DMA
    lists = jnp.pad(pivots.astype(F32), ((0, 6), (0, rows - PW)))
    packed = jnp.concatenate([jnp.swapaxes(panels, 1, 2).reshape(2 * kc, rows), lists], 0)
    return pl.pallas_call(
        functools.partial(kernel, n_row, n_col),
        out_shape=jax.ShapeDtypeStruct((rows, cols), F32),
        in_specs=[vmem] * 2,
        out_specs=vmem,
        scratch_shapes=[
            pltpu.VMEM((2, kc, PW), F32),
            pltpu.VMEM((n_col, kc, PW), F32),
            pltpu.VMEM((2, n_col, kc, rows), F32),
            pltpu.VMEM((n_col, kc, PW), F32),
            pltpu.VMEM((cols, tops), F32),
            pltpu.VMEM((2, cols, tops), F32),
            pltpu.VMEM((2, cols, tops), F32),
            pltpu.VMEM((2, kc, PW), F32),
            pltpu.VMEM((2, kc, PW), F32),
            pltpu.VMEM((2, PW, PW), F32),
            pltpu.VMEM((cols, rows), F32),
            pltpu.VMEM((8, rows), F32),
            pltpu.VMEM((tops, rows), BF16),
            pltpu.VMEM((PW, rows), BF16),
            pltpu.VMEM((8, rows), F32),
            pltpu.VMEM((tops, rows), BF16),
            pltpu.VMEM((tops, rows), BF16),
            dma((2,)),
            dma((2,)),
            dma((2, 2)),
            dma((2, 2, cols // PART)),
        ]
        + [dma((4, n_peer))] * 4,
        compiler_params=pltpu.CompilerParams(
            collective_id=0, has_side_effects=True, vmem_limit_bytes=48 * 1024 * 1024
        ),
    )(block, packed)


def body(block, panels, pivots):
    kc = panels.shape[2]
    fits = (
        block.shape[0] == 2 * PW
        and block.shape[1] % 128 == 0
        and kc % 8 == 0
        and lax.axis_size("col") % 2 == 0
        and lax.axis_size("row") > 1
    )
    return fused(block, panels, pivots) if fits else plain(block, panels, pivots)


def solution(mesh):
    return jax.shard_map(
        body,
        mesh=mesh,
        in_specs=(P("row", "col"), P(None, "row", "col"), P()),
        out_specs=P("row", "col"),
        check_vma=False,
    )
```

```python
import functools

import jax
import jax.numpy as jnp
from jax import lax
from jax.experimental import pallas as pl
from jax.experimental.pallas import tpu as pltpu
from jax.sharding import PartitionSpec as P

PW = 256


def swap_order(piv_row, offset, count):
    own = offset + jnp.arange(piv_row.shape[0], dtype=jnp.int32)
    base = jnp.arange(count, dtype=jnp.int32)
    return base.at[own].set(piv_row).at[piv_row].set(own)


def pick_rows(data, perm, targets, start):
    local_src = perm[targets] - start
    owned = (local_src >= 0) & (local_src < data.shape[0])
    taken = jnp.take(data, jnp.clip(local_src, 0, data.shape[0] - 1), axis=0)
    return jnp.where(owned[:, None], taken, 0.0)


def place_rows(data, targets, values, start):
    local_dst = targets - start
    inside = (local_dst >= 0) & (local_dst < data.shape[0])
    where_to = jnp.where(inside, local_dst, data.shape[0])
    return data.at[where_to].set(values, mode="drop")


def solve_top(diag_rows, rows):
    strict = jnp.tril(diag_rows, -1)
    inverse = jnp.eye(PW, dtype=jnp.float32) - strict
    power = strict
    for level in range(1, PW.bit_length() - 1):
        power = jnp.dot(
            power, power, precision=lax.Precision.HIGHEST, preferred_element_type=jnp.float32
        )
        inverse = inverse + jnp.dot(
            inverse, power, precision=lax.Precision.HIGHEST, preferred_element_type=jnp.float32
        )
    return jnp.dot(
        inverse, rows, precision=lax.Precision.HIGHEST, preferred_element_type=jnp.float32
    )


def finish(work, lower, offset, start, upper):
    product = jnp.dot(
        lower, upper, precision=lax.Precision.HIGHEST, preferred_element_type=jnp.float32
    )
    global_rows = start + jnp.arange(work.shape[0], dtype=jnp.int32)
    work = jnp.where((global_rows >= offset + PW)[:, None], work - product, work)
    placed = work.at[offset : offset + PW].set(upper)
    in_top = (global_rows >= offset) & (global_rows < offset + PW)
    return jnp.where(in_top[:, None], placed, work)


def plain(block, panels, pivots):
    rows_here = block.shape[0]
    rows_all = rows_here * lax.axis_size("row")
    start = lax.axis_index("row") * rows_here
    identity_perm = jnp.arange(rows_all, dtype=jnp.int32)
    perms = [swap_order(pivots[panel], panel * PW, rows_all) for panel in range(2)]
    targets = [
        jnp.concatenate([jnp.arange(panel * PW, panel * PW + PW, dtype=jnp.int32), pivots[panel]])
        for panel in range(2)
    ]
    tops_index = [jnp.arange(panel * PW, panel * PW + PW, dtype=jnp.int32) for panel in range(2)]
    work = block
    lowers = lax.all_gather(panels, "col", axis=2, tiled=True)
    for panel in range(2):
        offset = panel * PW
        diag_rows = pick_rows(lowers[panel], identity_perm, tops_index[panel], start)
        picked = pick_rows(work, perms[panel], targets[panel], start)
        moved, diag_all = lax.psum((picked, diag_rows), "row")
        work = place_rows(work, targets[panel], moved, start)
        upper = solve_top(diag_all, moved[:PW])
        work = finish(work, lowers[panel], offset, start, upper)
    return work

MESH = pl.DeviceIdType.MESH
F32, BF16 = jnp.float32, jnp.bfloat16
SMALL = 32
PART = 32
LAG = 2
ONE, ZERO, TOP, DIAG = range(4)


def dot(a, b):
    return jnp.dot(a, b, preferred_element_type=F32)


def split(a):
    high = a.astype(BF16)
    return high, (a - high.astype(F32)).astype(BF16)


def dot_split(a, b):
    m = a[0].shape[0]
    both = dot(jnp.concatenate(a, 0), b[0])
    return both[:m] + (both[m:] + dot(a[0], b[1]))


def dot_pick(a, one_hot):
    m = a.shape[0]
    out = dot(jnp.concatenate(split(a), 0), one_hot)
    return out[:m] + out[m:]


def iota(shape, dim):
    return lax.broadcasted_iota(jnp.int32, shape, dim)


def one_hot(condition):
    return jnp.where(condition, 1.0, 0.0)


def kernel(
    n_row, n_col, block_ref, panels_ref, out_ref, d_from, g_diag,
    g, g_top, own_ref, f_in, f_out, l_in, l_out, inverse_ref,
    block_t, local_ref, put_ref, put_one_ref, moved_ref, low_high, low_low,
    d_sem, i_sem, l_sem, f_sem, peer_send, peer_recv, sib_send, sib_recv,
):
    r, c = lax.axis_index("row"), lax.axis_index("col")
    rows, cols = block_ref.shape
    tops = 2 * PW
    kc = g_top.shape[1]
    n_peer = n_col // 2
    chunks = cols // PART
    last = n_row - 1
    p = c % 2
    sibling = c + 1 - 2 * p
    is_first, is_last = r == 0, r == last
    is_middle = (r > 0) & (r < last)
    is_upper = 2 * r >= n_row
    start = r * rows

    barrier = pltpu.get_barrier_semaphore()

    @pl.when(r > 0)
    def _():
        pl.semaphore_signal(barrier, 1, device_id={"row": r - 1}, device_id_type=MESH)

    @pl.when(r < last)
    def _():
        pl.semaphore_signal(barrier, 1, device_id={"row": r + 1}, device_id_type=MESH)

    for m in range(1, n_col):
        pl.semaphore_signal(barrier, 1, device_id={"col": (c + m) % n_col}, device_id_type=MESH)

    first = panels_ref[2 * kc : 2 * kc + 1, :PW]
    second = panels_ref[2 * kc + 1 : 2 * kc + 2, :PW]
    sub, lane = iota((PW, PW), 0).astype(F32), iota((PW, PW), 1).astype(F32)

    def upright(v):
        return jnp.sum(jnp.where(sub == lane, v, 0.0), axis=1, keepdims=True)

    first_c = upright(first)
    lane_row = lane[0:1, :]
    sub_col = sub[:, 0:1]

    def lookup(match, found, otherwise, axis):
        hit = jnp.sum(one_hot(match), axis=axis, keepdims=True)
        return jnp.sum(jnp.where(match, found, 0.0), axis=axis, keepdims=True) + jnp.where(hit > 0.5, 0.0, otherwise)

    q_second = lookup(first_c == second, sub, second, 0)
    q = jnp.concatenate([first, q_second], 1)
    start_f = start.astype(F32)
    local_ref[0:1, :] = q - start_f
    local_ref[1:2, :PW] = second - start_f

    @pl.when(is_first)
    def _():
        second_c = upright(second)
        home = lookup(first_c == lane + PW, sub, lane_row + PW, 0)
        home_c = lookup(first == sub + PW, lane, sub_col + PW, 1)
        out_first = jnp.where(first < tops, first, lookup(second_c == first, home_c, lane_row, 0))
        out_second = jnp.where(q_second < tops, q_second, home)
        local_ref[0:1, :] = jnp.concatenate([out_first, out_second], 1)
        local_ref[1:2, :PW] = lane_row + PW

    def from_here(v):
        return (v >= start_f) & (v < start_f + rows)

    @pl.when(is_first)
    def _():
        d_from[0] = panels_ref[:kc, :PW]
        d_from[1] = panels_ref[kc : 2 * kc, PW:tops]

    @pl.when(r > 0)
    def _():
        g[ONE, c] = panels_ref[kc : 2 * kc]

    @pl.when(is_middle)
    def _():
        pl.semaphore_wait(barrier, n_col + 1)

    @pl.when(is_first | is_last)
    def _():
        pl.semaphore_wait(barrier, n_col)

    def l_copy(d):
        return pltpu.make_async_remote_copy(
            src_ref=l_out.at[d], dst_ref=l_in.at[d], send_sem=l_sem.at[0, d], recv_sem=l_sem.at[1, d],
            device_id={"row": r + 1 - 2 * d}, device_id_type=MESH,
        )

    def f_copy(k, d):
        at = pl.ds(k * PART, PART)
        return pltpu.make_async_remote_copy(
            src_ref=f_out.at[d, at], dst_ref=f_in.at[d, at],
            send_sem=f_sem.at[0, d, k], recv_sem=f_sem.at[1, d, k],
            device_id={"row": r + 1 - 2 * d}, device_id_type=MESH,
        )

    diag_copy = pltpu.make_async_remote_copy(
        src_ref=d_from, dst_ref=d_from, send_sem=d_sem.at[0], recv_sem=d_sem.at[1],
        device_id={"row": r + 1}, device_id_type=MESH,
    )

    def arrives(d):
        return jnp.where(d == 0, r > 0, r < last)

    def l_step(d):
        @pl.when(arrives(d))
        def _():
            l_copy(d).wait_recv()

        @pl.when(is_middle)
        def _():
            l_out[d] = jnp.where(from_here(second), l_out[d], l_in[d])
            l_copy(d).start()

    def f_step(k, d):
        at = pl.ds(k * PART, PART)
        f_copy(k, d).wait_recv()
        f_out[d, at, :] = jnp.where(from_here(q), f_out[d, at, :], f_in[d, at, :])
        f_copy(k, d).start()

    def stage(k):
        upper = jnp.where(is_upper, 1, 0)
        near, far = k < chunks, 0 <= k - LAG < chunks
        if near or far:
            @pl.when(is_middle)
            def _():
                if near:
                    f_step(k, upper)
                if far:
                    f_step(k - LAG, 1 - upper)

    def slot_ref(kind, slot):
        return g_top.at[slot] if kind == TOP else g.at[kind, slot]

    def peer_copy(kind, m, slot):
        return pltpu.make_async_remote_copy(
            src_ref=slot_ref(kind, slot), dst_ref=slot_ref(kind, slot),
            send_sem=peer_send.at[kind, m], recv_sem=peer_recv.at[kind, m],
            device_id={"col": (c + 2 * m) % n_col}, device_id_type=MESH,
        )

    def sib_copy(kind, m, slot):
        return pltpu.make_async_remote_copy(
            src_ref=slot_ref(kind, slot), dst_ref=slot_ref(kind, slot),
            send_sem=sib_send.at[kind, m], recv_sem=sib_recv.at[kind, m],
            device_id={"col": sibling}, device_id_type=MESH,
        )

    def spread(kind):
        for m in range(1, n_peer):
            peer_copy(kind, m, c).start()
        sib_copy(kind, 0, c).start()

    def diag_peer(m):
        return pltpu.make_async_remote_copy(
            src_ref=d_from.at[p], dst_ref=g_diag.at[c],
            send_sem=peer_send.at[DIAG, m], recv_sem=peer_recv.at[DIAG, m],
            device_id={"col": (c + 2 * m) % n_col}, device_id_type=MESH,
        )

    def diag_cross(m):
        return pltpu.make_async_remote_copy(
            src_ref=d_from.at[1 - p], dst_ref=g_diag.at[c],
            send_sem=sib_send.at[DIAG, m], recv_sem=sib_recv.at[DIAG, m],
            device_id={"col": (sibling + 2 * m) % n_col}, device_id_type=MESH,
        )

    def spread_diag():
        for m in range(n_peer - 1, 0, -1):
            diag_peer(m).start()
            diag_cross(m).start()
        diag_cross(0).start()
        g_diag[c] = d_from[p]

    inverse_copy = pltpu.make_async_remote_copy(
        src_ref=inverse_ref.at[p], dst_ref=inverse_ref.at[p], send_sem=i_sem.at[0], recv_sem=i_sem.at[1],
        device_id={"col": sibling}, device_id_type=MESH,
    )

    def share(kind):
        for m in range(1, n_peer):
            slot = (c + n_col - 2 * m) % n_col
            peer_copy(kind, m, slot).wait_recv()
            sib_copy(kind, m, slot).start()

    def settle(kind):
        for m in range(n_peer):
            sib_copy(kind, m, (sibling + n_col - 2 * m) % n_col).wait_recv()

    def drain(kind):
        for m in range(1, n_peer):
            peer_copy(kind, m, c).wait_send()
        for m in range(n_peer):
            sib_copy(kind, m, c).wait_send()

    @pl.when(is_first)
    def _():
        diag_copy.start()
        spread_diag()

    @pl.when(r > 0)
    def _():
        spread(ONE)

    own_top = dot_pick(panels_ref[:kc], one_hot(iota((rows, PW), 0).astype(F32) == local_ref[1:2, :PW]).astype(BF16))
    l_out[0] = own_top
    l_out[1] = own_top

    @pl.when(is_first)
    def _():
        l_copy(0).start()

    @pl.when(is_last)
    def _():
        l_copy(1).start()

    block_t[...] = block_ref[...].T
    own = dot_pick(block_t[...], one_hot(iota((rows, tops), 0).astype(F32) == local_ref[0:1, :]).astype(BF16))
    own_ref[...] = own
    f_out[0] = own
    f_out[1] = own

    @pl.when(is_first)
    def _():
        for k in range(chunks):
            f_copy(k, 0).start()

    @pl.when(is_last)
    def _():
        for k in range(chunks):
            f_copy(k, 1).start()

    def pass_diag():
        diag_copy.wait_recv()

        @pl.when(r < last)
        def _():
            diag_copy.start()

        spread_diag()

    @pl.when((r > 0) & jnp.logical_not(is_upper))
    def _():
        pass_diag()

    @pl.when(r > 0)
    def _():
        second_c = upright(second)
        q_c = jnp.concatenate([first_c, lookup(second_c == first, lane, second_c, 1)], 0)
        put = one_hot(iota((PW, rows), 1).astype(F32) == second_c - start_f)
        put_one_ref[...] = put.astype(BF16)
        moved_ref[1:2, :] = jnp.sum(put, axis=0, keepdims=True)
        put = one_hot(iota((tops, rows), 1).astype(F32) == q_c - start_f)
        put_ref[...] = put.astype(BF16)
        moved_ref[0:1, :] = jnp.sum(put, axis=0, keepdims=True)

    @pl.when(is_upper)
    def _():
        l_step(1)

    @pl.when(is_upper)
    def _():
        pass_diag()

    l_step(0)

    @pl.when(jnp.logical_not(is_upper))
    def _():
        l_step(1)

    top_rows = jnp.where(second < start_f, l_in[0], jnp.where(from_here(second), own_top, l_in[1]))
    g_top[c] = top_rows
    spread(TOP)
    stage(0)

    @pl.when(r > 0)
    def _():
        g[ZERO, c] = jnp.where(moved_ref[1:2, :] > 0.5, dot_pick(l_in[0], put_one_ref[...]), panels_ref[:kc])
        spread(ZERO)

    stage(1)
    stage(2)
    stage(3)

    for m in range(n_peer):
        diag_cross(m).wait_recv()
        if m:
            diag_peer(m).wait_recv()
    whole = jnp.where(iota((PW, PW), 0) < iota((PW, PW), 1), g_diag[...].reshape(PW, PW), 0.0)
    lanes = iota((SMALL, PW), 1)
    small = jnp.zeros((SMALL, PW), F32)
    for b in range(PW // SMALL):
        small += jnp.where(lanes // SMALL == b, whole[b * SMALL : (b + 1) * SMALL], 0.0)

    def spaced(small):
        same = iota((PW, PW), 0) // SMALL == iota((PW, PW), 1) // SMALL
        return split(jnp.where(same, jnp.concatenate([small] * (PW // SMALL), 0), 0.0))

    power = dot_split(split(small), spaced(small))
    stage(4)
    small = one_hot(lanes % SMALL == iota((SMALL, PW), 0)) - small
    span = 2
    while span < SMALL:
        last_one = 2 * span >= SMALL
        new = dot_split(split(small if last_one else jnp.concatenate([small, power], 0)), spaced(power))
        small = small + new[:SMALL]
        power = new[SMALL:]
        span *= 2
        stage(span.bit_length() + 2)
    share(TOP)

    same = iota((PW, PW), 0) // SMALL == iota((PW, PW), 1) // SMALL
    inverse = jnp.where(same, jnp.concatenate([small] * (PW // SMALL), 0), 0.0)
    size = SMALL
    while size < PW:
        pairs = PW // (2 * size)
        pair_lanes = iota((size, PW), 1) // (2 * size)

        def fold(a):
            return sum(a[2 * size * i : 2 * size * i + size] for i in range(pairs))

        def unfold(a):
            empty = jnp.zeros((size, PW), F32)
            return jnp.concatenate([x for i in range(pairs) for x in (jnp.where(pair_lanes == i, a, 0.0), empty)], 0)

        other = (iota((size, PW), 1) // size) % 2 == 1
        beside = sum(
            jnp.where(other & (pair_lanes == i), whole[2 * size * i : 2 * size * i + size], 0.0) for i in range(pairs)
        )
        right = dot_split(split(beside), split(inverse))
        inverse = inverse - unfold(dot_split(split(fold(inverse)), split(unfold(right))))
        size *= 2
    for k in range(9, chunks + LAG):
        stage(k)
    inverse_ref[p] = inverse
    inverse_copy.start()

    def settle_rows(at):
        block_t[at] = jnp.where(moved_ref[0:1, :] > 0.5, dot_pick(f_in[0, at], put_ref[...]), block_t[at])

    @pl.when(r > 0)
    def _():
        share(ZERO)
        share(ONE)

    @pl.when(is_middle)
    def _():
        settle_rows(slice(0, cols))

    @pl.when(r > 0)
    def _():
        for kind, at in ((ZERO, 0), (ONE, PW)):
            settle(kind)
            high, low = split(g[kind].reshape(PW, rows))
            low_high[at : at + PW] = high
            low_low[at : at + PW] = low

    settle(TOP)
    above = split(g_top[...].reshape(PW, PW))
    inverse_copy.wait_recv()
    inverses = [split(inverse_ref[0]), split(inverse_ref[1])]

    def solve(at, mine):
        @pl.when(is_first)
        def _():
            for k in mine:
                f_copy(k, 1).wait_recv()

        @pl.when(is_last)
        def _():
            for k in mine:
                f_copy(k, 0).wait_recv()
            settle_rows(at)

        top = jnp.where(q < start_f, f_in[0, at], jnp.where(from_here(q), own_ref[at], f_in[1, at]))
        upper0 = dot_split(split(top[:, :PW]), inverses[0])
        upper1 = dot_split(split(top[:, PW:] - dot_split(split(upper0), above)), inverses[1])
        upper = jnp.concatenate([upper0, upper1], 1)

        @pl.when(is_first)
        def _():
            out_ref[:, at] = upper.T

        @pl.when(r > 0)
        def _():
            out_ref[:, at] = (block_t[at] - dot_split(split(upper), (low_high[...], low_low[...]))).T

    @pl.when(is_middle)
    def _():
        solve(slice(0, cols), range(0))

    @pl.when(is_first | is_last)
    def _():
        for half in range(2):
            mine = range(half * chunks // 2, (half + 1) * chunks // 2)
            solve(slice(mine[0] * PART, (mine[-1] + 1) * PART), mine)

    @pl.when(r > 0)
    def _():
        drain(ZERO)
        drain(ONE)

    for m in range(n_peer):
        diag_cross(m).wait_send()
        if m:
            diag_peer(m).wait_send()
    inverse_copy.wait_send()
    drain(TOP)

    @pl.when(r < last)
    def _():
        diag_copy.wait_send()

    for d in range(2):
        @pl.when((r < last) if d == 0 else (r > 0))
        def _():
            l_copy(d).wait_send()
            for k in range(chunks):
                f_copy(k, d).wait_send()


def fused(block, panels, pivots):
    n_row, n_col = lax.axis_size("row"), lax.axis_size("col")
    rows, cols = block.shape
    kc = panels.shape[2]
    tops = 2 * PW
    vmem = pl.BlockSpec(memory_space=pltpu.VMEM)
    n_peer = n_col // 2
    dma = pltpu.SemaphoreType.DMA
    lists = jnp.pad(pivots.astype(F32), ((0, 6), (0, rows - PW)))
    packed = jnp.concatenate([jnp.swapaxes(panels, 1, 2).reshape(2 * kc, rows), lists], 0)
    return pl.pallas_call(
        functools.partial(kernel, n_row, n_col),
        out_shape=jax.ShapeDtypeStruct((rows, cols), F32),
        in_specs=[vmem] * 2,
        out_specs=vmem,
        scratch_shapes=[
            pltpu.VMEM((2, kc, PW), F32),
            pltpu.VMEM((n_col, kc, PW), F32),
            pltpu.VMEM((2, n_col, kc, rows), F32),
            pltpu.VMEM((n_col, kc, PW), F32),
            pltpu.VMEM((cols, tops), F32),
            pltpu.VMEM((2, cols, tops), F32),
            pltpu.VMEM((2, cols, tops), F32),
            pltpu.VMEM((2, kc, PW), F32),
            pltpu.VMEM((2, kc, PW), F32),
            pltpu.VMEM((2, PW, PW), F32),
            pltpu.VMEM((cols, rows), F32),
            pltpu.VMEM((8, rows), F32),
            pltpu.VMEM((tops, rows), BF16),
            pltpu.VMEM((PW, rows), BF16),
            pltpu.VMEM((8, rows), F32),
            pltpu.VMEM((tops, rows), BF16),
            pltpu.VMEM((tops, rows), BF16),
            dma((2,)),
            dma((2,)),
            dma((2, 2)),
            dma((2, 2, cols // PART)),
        ]
        + [dma((4, n_peer))] * 4,
        compiler_params=pltpu.CompilerParams(
            collective_id=0, has_side_effects=True, vmem_limit_bytes=48 * 1024 * 1024
        ),
    )(block, packed)


def body(block, panels, pivots):
    kc = panels.shape[2]
    fits = (
        block.shape[0] == 2 * PW
        and block.shape[1] % 128 == 0
        and kc % 8 == 0
        and lax.axis_size("col") % 2 == 0
        and lax.axis_size("row") > 1
    )
    return fused(block, panels, pivots) if fits else plain(block, panels, pivots)


def solution(mesh):
    return jax.shard_map(
        body,
        mesh=mesh,
        in_specs=(P("row", "col"), P(None, "row", "col"), P()),
        out_specs=P("row", "col"),
        check_vma=False,
    )
```
